128 devices in a mesh: dp: 16 (over y, x), ctx: 4 (over z), tensor: 2 (over core).
Axes of the slice: x: 4, y: 4, z: 4, core: 2. Of those that a mesh axis runs over, the one named last changes fastest.
Arguments:
- tokens: bfloat16 [16, 2048, 640], P('dp', 'ctx'), may hold values from -6 to 6
- segments: int32 [16, 2048], P('dp', 'ctx'), may hold values from 0 to 8, as said below
- cotangent: bfloat16 [16, 2048, 640], P('dp', 'ctx'), may hold values from -6 to 6
- w_query: bfloat16 [640, 1024], P('dp', 'tensor'), may hold values from -0.25 to 0.25
- w_keyval: bfloat16 [640, 512], P('dp'), may hold values from -0.25 to 0.25
- w_out: bfloat16 [1024, 640], P('tensor', 'dp'), may hold values from -0.1875 to 0.1875
- w_gateup: bfloat16 [2, 640, 2048], P(None, 'dp', 'tensor'), may hold values from -0.25 to 0.25
- w_down: bfloat16 [2048, 640], P('tensor', 'dp'), may hold values from -0.125 to 0.125
- norm_gains: bfloat16 [4, 640], P(None, 'dp'), may hold values from 0.099609375 to 1.8984375
- head_gains: bfloat16 [2, 256], P(None, 'dp'), may hold values from 0.099609375 to 1.8984375
Outputs:
- output: bfloat16 [16, 2048, 640], P('dp', 'ctx')
- input_grad: float32 [16, 2048, 640], P('dp', 'ctx')
- grad_query: float32 [640, 1024], P('dp', 'tensor')
- grad_keyval: float32 [640, 512], P('dp')
- grad_out: float32 [1024, 640], P('tensor', 'dp')
- grad_gateup: float32 [2, 640, 2048], P(None, 'dp', 'tensor')
- grad_down: float32 [2048, 640], P('tensor', 'dp')
- grad_norm_gains: float32 [4, 640], P(None, 'dp')
- grad_head_gains: float32 [2, 256], P(None, 'dp')
The draws below stay inside these ranges and needn't reach their ends.
Inputs may be any that keep to these rules, and one draw needn't show every extreme that they name: `segments`: segment numbers never fall along a sequence. In every sequence exactly 4 boundaries fall among its first 512 positions and 4 among its last 512, so one document runs from the first of those ranges to the last.
All inputs are finite; a program needn't handle non-finite values.
Results may differ from the reference program's by a relative error of at most 0.025.
Values may be sent and summed in bfloat16 or wider, within the bound.
A program may use at most 128 MiB of HBM per device.

```python
import math
import jax
import jax.numpy as jnp
from jax import lax

D = 640
HEADS = 4
HD = 256
FF = 2048
WINDOW = 512
TOK_DEV = 512
CUTS = 4
NSEQ = 16
LENGTH = 2048


def draw_segments(key, part):
    key = jax.random.fold_in(key, 11)

    def one_sequence(seq_key):
        head_key, tail_key = jax.random.split(seq_key)
        head_cuts = jax.random.permutation(head_key, TOK_DEV - 1)[:CUTS] + 1
        tail_cuts = jax.random.permutation(tail_key, TOK_DEV - 1)[:CUTS] + (LENGTH - TOK_DEV + 1)
        boundaries = jnp.concatenate([head_cuts, tail_cuts]).astype(jnp.int32)
        places = jnp.arange(LENGTH, dtype=jnp.int32)
        return jnp.sum((places[:, None] >= boundaries[None, :]).astype(jnp.int32), axis=1).astype(jnp.int32)
    return jax.vmap(one_sequence)(jax.random.split(key, NSEQ))


def raised(drawn, key, source, target, parts, factor):
    def block_of(axis_at):
        return (jnp.arange(drawn.shape[axis_at]) // (drawn.shape[axis_at] // parts)).reshape((-1,) + (1,) * (drawn.ndim - 1 - axis_at))

    near = jax.random.permutation(key, parts)[block_of(target)]
    second = (block_of(target) + parts // 2) % parts
    return jnp.where((block_of(source) == near) | (block_of(source) == second), factor * drawn, drawn)


def block_levels(key, shape, shards, low, top_value):
    loudness = 1.0
    for dim, blocks in shards:
        draws = jax.random.uniform(jax.random.fold_in(jax.random.fold_in(key, 6), dim), (blocks,), jnp.float32, low / len(shards), top_value / len(shards))
        loudness = loudness * jnp.repeat(jnp.exp(draws), shape[dim] // blocks).reshape((-1,) + (1,) * (len(shape) - 1 - dim))
    return loudness


def scatter_about(own_key, dims, deviation, most, shards=(), kind=jnp.bfloat16):
    gain = block_levels(own_key, dims, shards, -0.22, 0.18) if shards else 1.0
    drawn = jax.random.normal(own_key, dims, jnp.float32) * deviation * gain
    return jnp.minimum(jnp.maximum(drawn, -most), most).astype(kind)


def heavy_noise(rng, dims, spread, most, cuts, heavy, kind=jnp.bfloat16):
    values = spread * jax.random.normal(rng, dims, jnp.float32)
    if cuts:
        values = values * block_levels(rng, dims, cuts, -0.22, 0.18)
    return jnp.clip(raised(values, jax.random.fold_in(rng, 3), *heavy), -most, most).astype(kind)


def setup_inputs(seed: int = 0) -> dict:
    seeds = jax.random.split(jax.random.key(seed), 11)
    tokens = heavy_noise(seeds[0], (NSEQ, LENGTH, D), 1.0, 6.0, ((0, 16), (1, 4)), (0, 2, 16, 2.0))
    segments = draw_segments(jax.random.fold_in(seeds[10], 71), 0)
    cotangent = heavy_noise(seeds[2], (NSEQ, LENGTH, D), 1.0, 6.0, ((0, 16), (1, 4)), (1, 2, 4, 2.0))
    w_query = scatter_about(seeds[3], (D, HEADS * HD), D ** -0.5, 0.25, ((0, 16), (1, 2)))
    w_keyval = scatter_about(seeds[4], (D, 2 * HD), D ** -0.5, 0.25, ((0, 16),))
    w_out = scatter_about(seeds[5], (HEADS * HD, D), (HEADS * HD) ** -0.5, 0.1875, ((0, 2), (1, 16)))
    w_gateup = scatter_about(seeds[6], (2, D, FF), D ** -0.5, 0.25, ((1, 16), (2, 2)))
    w_down = scatter_about(seeds[7], (FF, D), FF ** -0.5, 0.125, ((0, 2), (1, 16)))
    norm_gains = jnp.clip(1.0 + 0.18 * jax.random.normal(seeds[8], (4, D), jnp.float32), 0.099609375, 1.8984375).astype(jnp.bfloat16)
    head_gains = jnp.clip(1.0 + 0.18 * jax.random.normal(seeds[9], (2, HD), jnp.float32), 0.099609375, 1.8984375).astype(jnp.bfloat16)
    return dict(tokens=tokens, segments=segments, cotangent=cotangent, w_query=w_query, w_keyval=w_keyval, w_out=w_out, w_gateup=w_gateup, w_down=w_down, norm_gains=norm_gains, head_gains=head_gains)


EPSILON = 1e-06

@jax.custom_vjp
def low(v):
    return lax.optimization_barrier(v.astype(jnp.bfloat16)).astype(jnp.float32)

@jax.custom_vjp
def low_back(v):
    return v

def low_keep(v):
    return (low(v), None)

def low_pass(kept, grad):
    return (grad,)

def back_keep(v):
    return (v, None)

def back_low(kept, grad):
    return (low(grad),)
low.defvjp(low_keep, low_pass)
low_back.defvjp(back_keep, back_low)

def norm_rows(field, gain_row):
    return field * lax.rsqrt(lax.optimization_barrier(jnp.mean(field * field, axis=-1, keepdims=True)) + EPSILON) * gain_row

def angle_tables(positions, head_width):
    rates = jnp.exp(jnp.arange(head_width // 2, dtype=jnp.float32) * (-2.0 * math.log(10000.0) / head_width))
    angle_grid = positions[:, None] * rates[None, :]
    return (jnp.cos(angle_grid), jnp.sin(angle_grid))

def rotate(field, cos_table, sin_table):
    half_width = field.shape[-1] // 2
    front_half = field[..., :half_width]
    rear_half = field[..., half_width:]
    return jnp.concatenate([front_half * cos_table - rear_half * sin_table, rear_half * cos_table + front_half * sin_table], axis=-1)

def attend(queries, keys_all, values_all, seg_ids):
    length, head_count, head_width = queries.shape
    count = length // TOK_DEV
    scale = 1.0 / math.sqrt(head_width)
    padded_keys = jnp.concatenate([jnp.zeros((WINDOW, head_width), keys_all.dtype), keys_all], axis=0)
    padded_values = jnp.concatenate([jnp.zeros((WINDOW, head_width), values_all.dtype), values_all], axis=0)
    padded_ids = jnp.concatenate([jnp.full((WINDOW,), -1, jnp.int32), seg_ids.astype(jnp.int32)], axis=0)

    def one_block(number):
        begin = (number * TOK_DEV).astype(jnp.int32)
        block_queries = lax.dynamic_slice_in_dim(queries, begin, TOK_DEV, 0)
        block_keys = lax.dynamic_slice_in_dim(padded_keys, begin, TOK_DEV + WINDOW, 0)
        block_values = lax.dynamic_slice_in_dim(padded_values, begin, TOK_DEV + WINDOW, 0)
        query_ids = lax.dynamic_slice_in_dim(seg_ids.astype(jnp.int32), begin, TOK_DEV, 0)
        key_ids = lax.dynamic_slice_in_dim(padded_ids, begin, TOK_DEV + WINDOW, 0)
        query_pos = begin + jnp.arange(TOK_DEV, dtype=jnp.int32)
        key_pos = begin - WINDOW + jnp.arange(TOK_DEV + WINDOW, dtype=jnp.int32)
        distance = query_pos[:, None] - key_pos[None, :]
        allowed = (distance >= 0) & (distance < WINDOW) & (query_ids[:, None] == key_ids[None, :])
        scores = low_back(jnp.einsum('qhd,kd->hqk', block_queries, block_keys, precision=lax.Precision.HIGHEST) * scale)
        scores = jnp.where(allowed[None], scores, -1e+30)
        highest = lax.optimization_barrier(jnp.max(scores, axis=-1, keepdims=True))
        expo = jnp.exp(scores - highest)
        probs = low(expo / lax.optimization_barrier(jnp.sum(expo, axis=-1, keepdims=True)))
        return jnp.einsum('hqk,kd->qhd', probs, block_values, precision=lax.Precision.HIGHEST)
    blocks = lax.map(jax.checkpoint(one_block), jnp.arange(count, dtype=jnp.int32))
    return blocks.reshape(length, head_count * head_width)

def apply_layer(inputs, seg_ids, weight_query, weight_keyval, weight_out, weight_gateup, weight_down, weight_norms, weight_heads):
    length = inputs.shape[0]
    head_width = weight_heads.shape[1]
    head_count = weight_query.shape[1] // head_width
    cos_table, sin_table = angle_tables(jnp.arange(length, dtype=jnp.int32).astype(jnp.float32), head_width)
    normed = low(norm_rows(inputs, weight_norms[0]))
    query_raw = low_back(jnp.dot(normed, weight_query, precision=lax.Precision.HIGHEST)).reshape(length, head_count, head_width)
    keyval = jnp.dot(normed, weight_keyval, precision=lax.Precision.HIGHEST)
    key_raw = low_back(keyval[:, :head_width])
    values_all = low(low_back(keyval[:, head_width:]))
    queries = low(rotate(norm_rows(query_raw, weight_heads[0]), cos_table[:, None, :], sin_table[:, None, :]))
    keys_all = low(rotate(norm_rows(key_raw, weight_heads[1]), cos_table, sin_table))
    mixed = low_back(low(attend(queries, keys_all, values_all, seg_ids)))
    branch = low_back(jnp.dot(mixed, weight_out, precision=lax.Precision.HIGHEST))
    hidden_state = inputs + norm_rows(branch, weight_norms[1])
    normed_second = low(norm_rows(hidden_state, weight_norms[2]))
    gate_part = low_back(jnp.dot(normed_second, weight_gateup[0], precision=lax.Precision.HIGHEST))
    up_part = low_back(jnp.dot(normed_second, weight_gateup[1], precision=lax.Precision.HIGHEST))
    inner = low(jax.nn.gelu(gate_part, approximate=True) * up_part)
    feed = low_back(jnp.dot(inner, weight_down, precision=lax.Precision.HIGHEST))
    return hidden_state + norm_rows(feed, weight_norms[3])

def reference(tokens, segments, cotangent, w_query, w_keyval, w_out, w_gateup, w_down, norm_gains, head_gains):
    params = (w_query.astype(jnp.float32), w_keyval.astype(jnp.float32), w_out.astype(jnp.float32), w_gateup.astype(jnp.float32), w_down.astype(jnp.float32), norm_gains.astype(jnp.float32), head_gains.astype(jnp.float32))

    def per_sequence(totals, bundle):
        seq_tokens, seq_ids, seq_cot = bundle

        def forward(inputs, weight_query, weight_keyval, weight_out, weight_gateup, weight_down, weight_norms, weight_heads):
            return apply_layer(inputs, seq_ids, weight_query, weight_keyval, weight_out, weight_gateup, weight_down, weight_norms, weight_heads)
        result, pullback = jax.vjp(forward, seq_tokens.astype(jnp.float32), params[0], params[1], params[2], params[3], params[4], params[5], params[6])
        gradients = pullback(seq_cot.astype(jnp.float32))
        new_totals = tuple((running + fresh for running, fresh in zip(totals, gradients[1:])))
        return (new_totals, (result.astype(jnp.bfloat16), gradients[0]))
    initial = tuple((jnp.zeros(parameter.shape, jnp.float32) for parameter in params))
    totals, (outputs, input_grads) = lax.scan(per_sequence, initial, (tokens, segments, cotangent))
    return (outputs, input_grads, totals[0], totals[1], totals[2], totals[3], totals[4], totals[5], totals[6])
```

```python
import functools
import math

import jax
import jax.numpy as jnp
from jax import lax
from jax.experimental import pallas as pl
from jax.experimental.pallas import tpu as pltpu
from jax.sharding import PartitionSpec as P

WINDOW = 512
EPSILON = 1e-06
MESH = pl.DeviceIdType.MESH
VMEM_BYTES = 58 * 1024 * 1024

KV, QUERY, EXTRA, OUT, GATEUP, DOWN = 0, 256, 512, 640, 896, 1920
WIRE = 2432
PIECES = (
    ((0, 384), (384, 256)),
    ((640, 128), (768, 128)),
    ((896, 512), (1408, 512)),
    ((1920, 256), (2176, 256)),
)
SET_COLS = (1280, 1152)
CUT = 48


def place(u):
    return lax.rem(u + 8, 4)


class Wires:
    def __init__(self, send, recv):
        self.send, self.recv, self.used = send, recv, 0
        self.started = []

    def copy(self, src, dst, target):
        index = self.used
        self.used += 1
        made = pltpu.make_async_remote_copy(
            src_ref=src,
            dst_ref=dst,
            send_sem=self.send.at[index],
            recv_sem=self.recv.at[index],
            device_id=target,
            device_id_type=MESH,
        )
        made.start()
        self.started.append(made)
        return made

    def drain(self):
        for made in self.started:
            made.wait_send()
        self.started = []


class Ring:
    def __init__(self, first, x, y):
        self.first = first
        self.f, self.s = (x, y) if first == "x" else (y, x)

    def slot(self, ref, f, s, *rest):
        return ref.at[(s, f) + rest] if self.first == "x" else ref.at[(f, s) + rest]

    def index(self, f, s):
        return (s, f) if self.first == "x" else (f, s)

    def to_f(self, step):
        f = place(self.f + step)
        return {"dp": self.s * 4 + f} if self.first == "x" else {"dp": f * 4 + self.s}

    def to_s(self, step):
        s = place(self.s + step)
        return {"dp": s * 4 + self.f} if self.first == "x" else {"dp": self.f * 4 + s}


class Gather:
    def __init__(self, ring, wires, shard, whole, start, width):
        self.ring, self.wires, self.shard, self.whole = ring, wires, shard, whole
        self.cols = pl.ds(start, width)

    def one(self):
        r, c = self.ring, self.cols
        src = self.shard.at[:, c]
        dst = r.slot(self.whole, r.f, r.s, slice(None), c)
        self.a = self.wires.copy(src, dst, r.to_f(1))
        self.b = self.wires.copy(src, dst, r.to_f(-1))

    def two(self):
        r, c = self.ring, self.cols
        self.a.wait_recv()
        part = r.slot(self.whole, place(r.f - 1), r.s, pl.ds(0, CUT), c)
        a = self.wires.copy(part, part, r.to_f(1))
        self.b.wait_recv()
        part = r.slot(self.whole, place(r.f + 1), r.s, pl.ds(CUT, 80 - CUT), c)
        b = self.wires.copy(part, part, r.to_f(-1))
        self.a, self.b = a, b

    def three(self):
        r, c = self.ring, self.cols
        self.a.wait_recv()
        self.b.wait_recv()
        part = r.slot(self.whole, slice(None), r.s, slice(None), c)
        self.a = self.wires.copy(part, part, r.to_s(1))
        self.b = self.wires.copy(part, part, r.to_s(-1))

    def four(self):
        r, c = self.ring, self.cols
        self.a.wait_recv()
        part = r.slot(self.whole, pl.ds(0, 2), place(r.s - 1), slice(None), c)
        a = self.wires.copy(part, part, r.to_s(1))
        self.b.wait_recv()
        part = r.slot(self.whole, pl.ds(2, 2), place(r.s + 1), slice(None), c)
        b = self.wires.copy(part, part, r.to_s(-1))
        self.a, self.b = a, b

    def finish(self):
        self.a.wait_recv()
        self.b.wait_recv()


def added(*terms):
    total = terms[0].astype(jnp.float32)
    for term in terms[1:]:
        total = total + term.astype(jnp.float32)
    return total


class Scatter:
    def __init__(self, ring, wires, grads, bufs, final, z, start, width, offset):
        self.ring, self.wires, self.grads, self.final, self.z = ring, wires, grads, final, z
        self.r1, self.r2, self.sums, self.r3, self.r4 = bufs
        self.cols = pl.ds(start, width)
        self.near = pl.ds(offset, width)

    def one(self):
        r, c, n = self.ring, self.cols, self.near
        far = place(r.s + 2)
        self.a = self.wires.copy(
            r.slot(self.grads, pl.ds(0, 2), far, slice(None), c), self.r1.at[0, :, :, n], r.to_s(1)
        )
        self.b = self.wires.copy(
            r.slot(self.grads, pl.ds(2, 2), far, slice(None), c), self.r1.at[1, :, :, n], r.to_s(-1)
        )

    def two(self):
        r, c, n = self.ring, self.cols, self.near
        after, before = place(r.s + 1), place(r.s - 1)
        self.a.wait_recv()
        for i in range(2):
            at = r.index(i, after) + (slice(None), c)
            self.grads[at] = added(self.grads[at], self.r1[0, i, :, n]).astype(jnp.bfloat16)
        a = self.wires.copy(
            r.slot(self.grads, slice(None), after, slice(None), c), self.r2.at[0, :, :, n], r.to_s(1)
        )
        self.b.wait_recv()
        for i in range(2):
            at = r.index(2 + i, before) + (slice(None), c)
            self.grads[at] = added(self.grads[at], self.r1[1, i, :, n]).astype(jnp.bfloat16)
        b = self.wires.copy(
            r.slot(self.grads, slice(None), before, slice(None), c),
            self.r2.at[1, :, :, n],
            r.to_s(-1),
        )
        self.a, self.b = a, b

    def three(self):
        r, c, n = self.ring, self.cols, self.near
        self.a.wait_recv()
        self.b.wait_recv()
        for i in range(4):
            at = r.index(i, r.s) + (slice(None), c)
            self.sums[i, :, n] = added(
                self.grads[at], self.r2[0, i, :, n], self.r2[1, i, :, n]
            ).astype(jnp.bfloat16)
        far = place(r.f + 2)
        self.a = self.wires.copy(
            self.sums.at[far, pl.ds(0, CUT), n], self.r3.at[pl.ds(0, CUT), n], r.to_f(1)
        )
        self.b = self.wires.copy(
            self.sums.at[far, pl.ds(CUT, 80 - CUT), n],
            self.r3.at[pl.ds(CUT, 80 - CUT), n],
            r.to_f(-1),
        )

    def four(self):
        r, n = self.ring, self.near
        after, before = place(r.f + 1), place(r.f - 1)
        top, low = pl.ds(0, CUT), pl.ds(CUT, 80 - CUT)
        self.a.wait_recv()
        self.sums[after, top, n] = added(self.sums[after, top, n], self.r3[top, n]).astype(
            jnp.bfloat16
        )
        a = self.wires.copy(self.sums.at[after, :, n], self.r4.at[0, :, n], r.to_f(1))
        self.b.wait_recv()
        self.sums[before, low, n] = added(self.sums[before, low, n], self.r3[low, n]).astype(
            jnp.bfloat16
        )
        b = self.wires.copy(self.sums.at[before, :, n], self.r4.at[1, :, n], r.to_f(-1))
        self.a, self.b = a, b

    def five(self):
        r, c, n = self.ring, self.cols, self.near
        self.a.wait_recv()
        self.b.wait_recv()
        self.final[self.z, :, c] = added(
            self.sums[r.f, :, n], self.r4[0, :, n], self.r4[1, :, n]
        ).astype(jnp.bfloat16)
        part = self.final.at[self.z, :, c]
        self.zs = [self.wires.copy(part, part, {"ctx": place(self.z + k)}) for k in (1, 3, 2)]

    def finish(self):
        for made in self.zs:
            made.wait_recv()


def greet(targets):
    barrier = pltpu.get_barrier_semaphore()
    for target in targets:
        pl.semaphore_signal(barrier, inc=1, device_id=target, device_id_type=MESH)
    pl.semaphore_wait(barrier, len(targets))


def spot():
    d = lax.axis_index("dp")
    return lax.rem(d, 4), lax.div(d, 4), lax.axis_index("ctx")


def gather_kernel(shard, out, whole, send, recv):
    x, y, _ = spot()
    rings = (Ring("x", x, y), Ring("y", x, y))
    wires = Wires(send, recv)
    greet([r.to_f(k) for r in rings for k in (1, -1)])
    parts = [
        Gather(ring, wires, shard, whole, *piece[i])
        for piece in PIECES
        for i, ring in enumerate(rings)
    ]
    for part in parts:
        part.one()
    whole[y, x] = shard[...]
    for part in parts:
        part.two()
    for part in parts:
        part.three()
    for part in parts:
        part.four()
    for part in parts:
        part.finish()
    wires.drain()
    for i in range(4):
        out[i] = whole[i]


def scatter_kernel(grads_in, out, grads, final, *rest):
    bufs_a, bufs_b, send, recv = rest[:5], rest[5:10], rest[10], rest[11]
    x, y, z = spot()
    rings = (Ring("x", x, y), Ring("y", x, y))
    wires = Wires(send, recv)
    for i in range(4):
        grads[i] = grads_in[i]
    greet(
        [r.to_f(k) for r in rings for k in (1, -1)] + [{"ctx": place(z + k)} for k in (1, 2, 3)]
    )
    parts, offsets = [], [0, 0]
    for piece in PIECES:
        for i, ring in enumerate(rings):
            start, width = piece[i]
            parts.append(
                Scatter(
                    ring, wires, grads, (bufs_a, bufs_b)[i], final, z, start, width, offsets[i]
                )
            )
            offsets[i] += width
    for step in ("one", "two", "three", "four", "five", "finish"):
        for part in parts:
            getattr(part, step)()
    wires.drain()
    out[...] = added(final[0], final[1], final[2], final[3])


def pair_kernel(value, out, other, send, recv):
    mate = {"tensor": 1 - lax.axis_index("tensor")}
    greet([mate])
    made = pltpu.make_async_remote_copy(
        src_ref=value, dst_ref=other, send_sem=send, recv_sem=recv, device_id=mate, device_id_type=MESH
    )
    made.start()
    made.wait()
    out[...] = added(value[...], other[...])


def vmem():
    return pl.BlockSpec(memory_space=pltpu.VMEM)


def pair_sum(value, number):
    return pl.pallas_call(
        pair_kernel,
        out_shape=jax.ShapeDtypeStruct(value.shape, jnp.float32),
        in_specs=[vmem()],
        out_specs=vmem(),
        scratch_shapes=[
            pltpu.VMEM(value.shape, jnp.bfloat16),
            pltpu.SemaphoreType.DMA,
            pltpu.SemaphoreType.DMA,
        ],
        compiler_params=pltpu.CompilerParams(
            collective_id=number, has_side_effects=True, vmem_limit_bytes=VMEM_BYTES
        ),
    )(value)


def gather_all(wire):
    return pl.pallas_call(
        gather_kernel,
        out_shape=jax.ShapeDtypeStruct((4, 4, 80, WIRE), jnp.bfloat16),
        in_specs=[vmem()],
        out_specs=vmem(),
        scratch_shapes=[
            pltpu.VMEM((4, 4, 80, WIRE), jnp.bfloat16),
            pltpu.SemaphoreType.DMA((64,)),
            pltpu.SemaphoreType.DMA((64,)),
        ],
        compiler_params=pltpu.CompilerParams(
            collective_id=0, has_side_effects=True, vmem_limit_bytes=VMEM_BYTES
        ),
    )(wire)


def ring_buffers(cols):
    return [
        pltpu.VMEM((2, 2, 80, cols), jnp.bfloat16),
        pltpu.VMEM((2, 4, 80, cols), jnp.bfloat16),
        pltpu.VMEM((4, 80, cols), jnp.bfloat16),
        pltpu.VMEM((80, cols), jnp.bfloat16),
        pltpu.VMEM((2, 80, cols), jnp.bfloat16),
    ]


def scatter_all(grads):
    return pl.pallas_call(
        scatter_kernel,
        out_shape=jax.ShapeDtypeStruct((80, WIRE), jnp.float32),
        in_specs=[vmem()],
        out_specs=vmem(),
        scratch_shapes=[
            pltpu.VMEM((4, 4, 80, WIRE), jnp.bfloat16),
            pltpu.VMEM((4, 80, WIRE), jnp.bfloat16),
            *ring_buffers(SET_COLS[0]),
            *ring_buffers(SET_COLS[1]),
            pltpu.SemaphoreType.DMA((96,)),
            pltpu.SemaphoreType.DMA((96,)),
        ],
        compiler_params=pltpu.CompilerParams(
            collective_id=1, has_side_effects=True, vmem_limit_bytes=VMEM_BYTES
        ),
    )(grads)


def fold(block):
    half = block.shape[-1] // 2
    return jnp.concatenate([block[..., :half], block[..., half:]], axis=-2)


def unfold(block):
    rows = block.shape[-2] // 2
    return jnp.concatenate([block[..., :rows, :], block[..., rows:, :]], axis=-1)


def from_behind(block, axis, distance):
    devices = range(lax.axis_size(axis))
    route = [(i - distance, i) for i in devices if i - distance in devices]
    return lax.ppermute(block, axis, route)


def norm_rows(field, gain_row):
    return field * lax.rsqrt(jnp.mean(field * field, axis=-1, keepdims=True) + EPSILON) * gain_row


def angle_tables(positions, head_width):
    rates = jnp.exp(
        jnp.arange(head_width // 2, dtype=jnp.float32) * (-2.0 * math.log(10000.0) / head_width)
    )
    angle_grid = positions[:, None] * rates[None, :]
    return (jnp.cos(angle_grid), jnp.sin(angle_grid))


def rotate(field, cos_table, sin_table):
    half_width = field.shape[-1] // 2
    front_half = field[..., :half_width]
    rear_half = field[..., half_width:]
    return jnp.concatenate(
        [
            front_half * cos_table - rear_half * sin_table,
            rear_half * cos_table + front_half * sin_table,
        ],
        axis=-1,
    )


def gated_inner(gate_part, up_part):
    return jax.nn.gelu(gate_part, approximate=True) * up_part


def dot(a, b, dims=((1,), (0,))):
    return lax.dot_general(a, b, (dims, ((), ())), preferred_element_type=jnp.float32)


NT = ((1,), (1,))
TN = ((0,), (0,))


def pack_shards(w_query, w_keyval, w_out, w_gateup, w_down, norm_gains, head_gains):
    def extra(block):
        rows, cols = block.shape
        return jnp.pad(block, ((0, 40 - rows), (0, 128 - cols)))

    return jnp.concatenate(
        [
            fold(w_keyval),
            fold(w_query),
            jnp.concatenate([extra(norm_gains.T), extra(head_gains.T)], axis=0),
            fold(w_out.T),
            w_gateup.reshape(80, -1),
            fold(w_down.T),
        ],
        axis=1,
    )


def shards(
    tokens, segments, cotangent, w_query, w_keyval, w_out, w_gateup, w_down, norm_gains, head_gains
):
    whole = gather_all(
        pack_shards(w_query, w_keyval, w_out, w_gateup, w_down, norm_gains, head_gains)
    ).reshape(16, 80, WIRE)

    def weight(start, stop):
        return unfold(whole[:, :, start:stop]).reshape(640, -1)

    full_keyval, full_query = weight(KV, QUERY), weight(QUERY, EXTRA)
    full_out, full_gateup, full_down = weight(OUT, GATEUP), weight(GATEUP, DOWN), weight(DOWN, WIRE)
    gains = whole[:, :40, EXTRA : EXTRA + 4].reshape(640, 4).T.astype(jnp.float32)
    head_gain = whole[:, 40:56, EXTRA : EXTRA + 2].reshape(256, 2).T.astype(jnp.float32)
    rows, model_width = tokens.shape[1:]
    tokens, cotangent, segments = tokens[0], cotangent[0], segments[0]
    head_width = head_gain.shape[1]
    local_heads = full_query.shape[1] // head_width
    scale = 1.0 / math.sqrt(head_width)
    piece_index = lax.axis_index("ctx")
    query_pos = piece_index * rows + jnp.arange(rows, dtype=jnp.int32)
    key_pos = piece_index * rows - WINDOW + jnp.arange(rows + WINDOW, dtype=jnp.int32)
    cos_table, sin_table = angle_tables(query_pos.astype(jnp.float32), head_width)

    def query_map(query_raw, gain_row):
        return rotate(norm_rows(query_raw, gain_row), cos_table[:, None, :], sin_table[:, None, :])

    def key_map(key_raw, gain_row):
        return rotate(norm_rows(key_raw, gain_row), cos_table, sin_table)

    inputs = tokens.astype(jnp.float32)
    normed, norm_pull = jax.vjp(norm_rows, inputs, gains[0])
    normed_low = normed.astype(jnp.bfloat16)
    query_raw = dot(normed_low, full_query).reshape(rows, local_heads, head_width)
    keyval = dot(normed_low, full_keyval)
    queries, query_pull = jax.vjp(query_map, query_raw, head_gain[0])
    keys_own, key_pull = jax.vjp(key_map, keyval[..., :head_width], head_gain[1])
    query_low = queries.astype(jnp.bfloat16)
    own_keyval = jnp.concatenate(
        [keys_own.astype(jnp.bfloat16), keyval[..., head_width:].astype(jnp.bfloat16)], axis=-1
    )
    prior_keyval, prior_ids = from_behind((own_keyval, segments), "ctx", 1)
    seq_keyval = jnp.concatenate([prior_keyval, own_keyval], axis=0)
    all_ids = jnp.concatenate([prior_ids, segments], axis=0)
    distance = query_pos[:, None] - key_pos[None, :]
    nearby = (distance >= 0) & (distance < WINDOW) & (key_pos[None, :] >= 0)
    allowed = (nearby & (segments[:, None] == all_ids[None, :]))[None]
    keys_seq, values_seq = seq_keyval[:, :head_width], seq_keyval[:, head_width:]

    def ein(spec, a, b):
        return jnp.einsum(spec, a, b, preferred_element_type=jnp.float32)

    scores = ein("qhd,kd->hqk", query_low, keys_seq) * scale
    scores = jnp.where(allowed, scores, -1e30)
    highest = jnp.max(scores, axis=-1, keepdims=True)
    expo = jnp.exp(scores - highest)
    summed = jnp.sum(expo, axis=-1, keepdims=True)
    probs_low = (expo / summed).astype(jnp.bfloat16)
    mixed = ein("hqk,kd->qhd", probs_low, values_seq).astype(jnp.bfloat16)
    mixed = mixed.reshape(rows, local_heads * head_width)
    log_totals = (highest + jnp.log(summed))[..., 0]

    branch = pair_sum(dot(mixed, full_out, NT).astype(jnp.bfloat16), 2)
    post_attn, post_attn_pull = jax.vjp(norm_rows, branch, gains[1])
    hidden_state = inputs + post_attn
    normed_second, second_pull = jax.vjp(norm_rows, hidden_state, gains[2])
    second_low = normed_second.astype(jnp.bfloat16)
    gate_up = dot(second_low, full_gateup)
    wide = gate_up.shape[1] // 2
    inner, inner_pull = jax.vjp(gated_inner, gate_up[:, :wide], gate_up[:, wide:])
    inner_low = inner.astype(jnp.bfloat16)
    feed = pair_sum(dot(inner_low, full_down, NT).astype(jnp.bfloat16), 2)
    post_feed, post_feed_pull = jax.vjp(norm_rows, feed, gains[3])
    output = (hidden_state + post_feed).astype(jnp.bfloat16)
    grad_output = cotangent.astype(jnp.float32)
    grad_feed, grad_gain_last = post_feed_pull(grad_output)
    grad_feed_low = grad_feed.astype(jnp.bfloat16)
    grad_down = dot(grad_feed_low, inner_low, TN)
    grad_inner = dot(grad_feed_low, full_down)
    grad_gate, grad_up = inner_pull(grad_inner)
    grad_gate_up = jnp.concatenate([grad_gate, grad_up], axis=1).astype(jnp.bfloat16)
    grad_gateup = dot(second_low, grad_gate_up, TN)
    grad_second = pair_sum(dot(grad_gate_up, full_gateup, NT).astype(jnp.bfloat16), 2)
    grad_hidden_norm, grad_gain_pre = second_pull(grad_second)
    grad_hidden = grad_output + grad_hidden_norm
    grad_branch, grad_gain_post = post_attn_pull(grad_hidden)
    grad_branch_low = grad_branch.astype(jnp.bfloat16)
    grad_wout = dot(grad_branch_low, mixed, TN)
    grad_mixed = dot(grad_branch_low, full_out).astype(jnp.bfloat16)
    grad_mixed = grad_mixed.reshape(rows, local_heads, head_width)

    scores = ein("qhd,kd->hqk", query_low, keys_seq) * scale
    probs = jnp.where(allowed, jnp.exp(scores - log_totals[..., None]), 0.0)
    probs_low = probs.astype(jnp.bfloat16)
    grad_probs = ein("qhd,kd->hqk", grad_mixed, values_seq)
    spread = jnp.sum(probs * grad_probs, axis=-1, keepdims=True)
    grad_scores = (probs * (grad_probs - spread)).astype(jnp.bfloat16)
    grad_queries = ein("hqk,kd->qhd", grad_scores, keys_seq) * scale
    grad_keys = ein("hqk,qhd->kd", grad_scores, query_low) * scale
    grad_values = ein("hqk,qhd->kd", probs_low, grad_mixed)
    grad_keyvals = jnp.concatenate([grad_keys, grad_values], axis=-1)
    returned = from_behind(grad_keyvals[:WINDOW].astype(jnp.bfloat16), "ctx", -1)
    own_grad = grad_keyvals[WINDOW:] + returned.astype(jnp.float32)
    grad_query_raw, grad_qgain = query_pull(grad_queries)
    grad_query_low = grad_query_raw.reshape(rows, local_heads * head_width).astype(jnp.bfloat16)
    grad_wquery = dot(normed_low, grad_query_low, TN)
    query_side = dot(grad_query_low, full_query, NT)
    gain_rows = jnp.pad(grad_qgain[None, :], ((0, 15), (0, 512 + model_width - head_width)))
    bundle = jnp.concatenate([own_grad, query_side], axis=1)
    summed = pair_sum(jnp.concatenate([bundle, gain_rows], axis=0).astype(jnp.bfloat16), 3)
    summed_keyval, summed_query_side = summed[:rows, :512], summed[:rows, 512:]
    summed_qgain = summed[rows, :head_width]
    grad_key_raw, grad_kgain = key_pull(summed_keyval[..., :head_width])
    grad_keyval_low = jnp.concatenate(
        [grad_key_raw, summed_keyval[..., head_width:]], axis=-1
    ).astype(jnp.bfloat16)
    grad_wkeyval = dot(normed_low, grad_keyval_low, TN)
    grad_normed = summed_query_side + dot(grad_keyval_low, full_keyval, NT)
    grad_input_norm, grad_gain_first = norm_pull(grad_normed)
    input_grad = grad_hidden + grad_input_norm
    grad_norms = jnp.stack([grad_gain_first, grad_gain_post, grad_gain_pre, grad_gain_last])
    grad_heads = jnp.stack([summed_qgain, grad_kgain])

    def chunks(block):
        return fold(block.astype(jnp.bfloat16).reshape(16, 40, -1))

    extra = jnp.concatenate(
        [
            jnp.pad(grad_norms.T.reshape(16, 40, 4), ((0, 0), (0, 0), (0, 124))),
            jnp.pad(grad_heads.T.reshape(16, 16, 2), ((0, 0), (0, 24), (0, 126))),
        ],
        axis=1,
    ).astype(jnp.bfloat16)
    grads = jnp.concatenate(
        [
            chunks(grad_wkeyval),
            chunks(grad_wquery),
            extra,
            chunks(grad_wout),
            chunks(grad_gateup),
            chunks(grad_down),
        ],
        axis=2,
    )
    done = scatter_all(grads.reshape(4, 4, 80, WIRE))
    return (
        output[None],
        input_grad[None],
        unfold(done[:, QUERY:EXTRA]),
        unfold(done[:, KV:QUERY]),
        unfold(done[:, OUT:GATEUP]).T,
        done[:, GATEUP:DOWN].reshape(2, 40, -1),
        unfold(done[:, DOWN:WIRE]).T,
        done[:40, EXTRA : EXTRA + 4].T,
        done[40:56, EXTRA : EXTRA + 2].T,
    )


def solution(mesh):
    placed = (
        P("dp", "ctx", None),
        P("dp", "ctx"),
        P("dp", "ctx", None),
        P("dp", "tensor"),
        P("dp", None),
        P("tensor", "dp"),
        P(None, "dp", "tensor"),
        P("tensor", "dp"),
        P(None, "dp"),
        P(None, "dp"),
    )
    return jax.shard_map(
        shards,
        mesh=mesh,
        in_specs=placed,
        out_specs=(
            P("dp", "ctx", None),
            P("dp", "ctx", None),
            P("dp", "tensor"),
            P("dp", None),
            P("tensor", "dp"),
            P(None, "dp", "tensor"),
            P("tensor", "dp"),
            P(None, "dp"),
            P(None, "dp"),
        ),
        check_vma=False,
    )
```

```python
import math
import types

import jax
import jax.numpy as jnp
from jax import lax
from jax.experimental import pallas as pl
from jax.experimental.pallas import tpu as pltpu
from jax.sharding import PartitionSpec as P

WINDOW = 512
EPSILON = 1e-06
MESH = pl.DeviceIdType.MESH
VMEM_BYTES = 60 * 1024 * 1024

KV, QUERY, EXTRA, OUT, GATEUP, DOWN, WIRE = 0, 128, 384, 512, 768, 1792, 2304
GATHERS = (
    ((0, 256), (256, 256)),
    ((512, 128), (640, 128)),
    ((768, 512), (1280, 512)),
    ((1792, 256), (2048, 256)),
)
SCATTERS = (
    ((0, 256), (256, 128)),
    ((512, 128), (640, 128)),
    ((768, 512), (1280, 512)),
    ((1792, 256), (2048, 256)),
    (None, (384, 128)),
)
SET_COLS = 1152
CUT = 48
ROWS, D, HD, FFH = 512, 640, 256, 1024
SCALE = 1.0 / math.sqrt(HD)
LOW = jnp.bfloat16
F32 = jnp.float32
NN, NT, TN = ((1,), (0,)), ((1,), (1,)), ((0,), (0,))


def place(u):
    return lax.rem(u + 8, 4)


class Wires:
    def __init__(self, send, recv):
        self.send, self.recv, self.used = send, recv, 0
        self.started = []

    def copy(self, src, dst, target):
        index = self.used
        self.used += 1
        made = pltpu.make_async_remote_copy(
            src_ref=src,
            dst_ref=dst,
            send_sem=self.send.at[index],
            recv_sem=self.recv.at[index],
            device_id=target,
            device_id_type=MESH,
        )
        made.start()
        self.started.append(made)
        return made

    def drain(self):
        for made in self.started:
            made.wait_send()
        self.started = []


class Ring:
    def __init__(self, first, x, y):
        self.first = first
        self.f, self.s = (x, y) if first == "x" else (y, x)

    def slot(self, ref, f, s, *rest):
        return ref.at[(s, f) + rest] if self.first == "x" else ref.at[(f, s) + rest]

    def index(self, f, s):
        return (s, f) if self.first == "x" else (f, s)

    def to_f(self, step):
        f = place(self.f + step)
        return {"dp": self.s * 4 + f} if self.first == "x" else {"dp": f * 4 + self.s}

    def to_s(self, step):
        s = place(self.s + step)
        return {"dp": s * 4 + self.f} if self.first == "x" else {"dp": self.f * 4 + s}


class Gather:
    def __init__(self, ring, wires, shard, whole, start, width):
        self.ring, self.wires, self.shard, self.whole = ring, wires, shard, whole
        self.cols = pl.ds(start, width)

    def one(self):
        r, c = self.ring, self.cols
        src = self.shard.at[:, c]
        dst = r.slot(self.whole, r.f, r.s, slice(None), c)
        self.a = self.wires.copy(src, dst, r.to_f(1))
        self.b = self.wires.copy(src, dst, r.to_f(-1))

    def two(self):
        r, c = self.ring, self.cols
        self.a.wait_recv()
        part = r.slot(self.whole, place(r.f - 1), r.s, pl.ds(0, CUT), c)
        a = self.wires.copy(part, part, r.to_f(1))
        self.b.wait_recv()
        part = r.slot(self.whole, place(r.f + 1), r.s, pl.ds(CUT, 80 - CUT), c)
        b = self.wires.copy(part, part, r.to_f(-1))
        self.a, self.b = a, b

    def three(self):
        r, c = self.ring, self.cols
        self.a.wait_recv()
        self.b.wait_recv()
        part = r.slot(self.whole, slice(None), r.s, slice(None), c)
        self.a = self.wires.copy(part, part, r.to_s(1))
        self.b = self.wires.copy(part, part, r.to_s(-1))

    def four(self):
        r, c = self.ring, self.cols
        self.a.wait_recv()
        part = r.slot(self.whole, pl.ds(0, 2), place(r.s - 1), slice(None), c)
        a = self.wires.copy(part, part, r.to_s(1))
        self.b.wait_recv()
        part = r.slot(self.whole, pl.ds(2, 2), place(r.s + 1), slice(None), c)
        b = self.wires.copy(part, part, r.to_s(-1))
        self.a, self.b = a, b

    def finish(self):
        self.a.wait_recv()
        self.b.wait_recv()


def added(*terms):
    total = terms[0].astype(jnp.float32)
    for term in terms[1:]:
        total = total + term.astype(jnp.float32)
    return total


class Scatter:
    def __init__(self, ring, wires, grads, bufs, final, z, start, width, offset):
        self.ring, self.wires, self.grads, self.final, self.z = ring, wires, grads, final, z
        self.r1, self.r2, self.sums, self.r3, self.r4 = bufs
        self.cols = pl.ds(start, width)
        self.near = pl.ds(offset, width)

    def one(self):
        r, c, n = self.ring, self.cols, self.near
        far = place(r.s + 2)
        self.a = self.wires.copy(
            r.slot(self.grads, pl.ds(0, 2), far, slice(None), c), self.r1.at[0, :, :, n], r.to_s(1)
        )
        self.b = self.wires.copy(
            r.slot(self.grads, pl.ds(2, 2), far, slice(None), c), self.r1.at[1, :, :, n], r.to_s(-1)
        )

    def two(self):
        r, c, n = self.ring, self.cols, self.near
        after, before = place(r.s + 1), place(r.s - 1)
        self.a.wait_recv()
        for i in range(2):
            at = r.index(i, after) + (slice(None), c)
            self.grads[at] = added(self.grads[at], self.r1[0, i, :, n]).astype(jnp.bfloat16)
        a = self.wires.copy(
            r.slot(self.grads, slice(None), after, slice(None), c), self.r2.at[0, :, :, n], r.to_s(1)
        )
        self.b.wait_recv()
        for i in range(2):
            at = r.index(2 + i, before) + (slice(None), c)
            self.grads[at] = added(self.grads[at], self.r1[1, i, :, n]).astype(jnp.bfloat16)
        b = self.wires.copy(
            r.slot(self.grads, slice(None), before, slice(None), c),
            self.r2.at[1, :, :, n],
            r.to_s(-1),
        )
        self.a, self.b = a, b

    def three(self):
        r, c, n = self.ring, self.cols, self.near
        self.a.wait_recv()
        self.b.wait_recv()
        for i in range(4):
            at = r.index(i, r.s) + (slice(None), c)
            self.sums[i, :, n] = added(
                self.grads[at], self.r2[0, i, :, n], self.r2[1, i, :, n]
            ).astype(jnp.bfloat16)
        far = place(r.f + 2)
        self.a = self.wires.copy(
            self.sums.at[far, pl.ds(0, CUT), n], self.r3.at[pl.ds(0, CUT), n], r.to_f(1)
        )
        self.b = self.wires.copy(
            self.sums.at[far, pl.ds(CUT, 80 - CUT), n],
            self.r3.at[pl.ds(CUT, 80 - CUT), n],
            r.to_f(-1),
        )

    def four(self):
        r, n = self.ring, self.near
        after, before = place(r.f + 1), place(r.f - 1)
        top, low = pl.ds(0, CUT), pl.ds(CUT, 80 - CUT)
        self.a.wait_recv()
        self.sums[after, top, n] = added(self.sums[after, top, n], self.r3[top, n]).astype(
            jnp.bfloat16
        )
        a = self.wires.copy(self.sums.at[after, :, n], self.r4.at[0, :, n], r.to_f(1))
        self.b.wait_recv()
        self.sums[before, low, n] = added(self.sums[before, low, n], self.r3[low, n]).astype(
            jnp.bfloat16
        )
        b = self.wires.copy(self.sums.at[before, :, n], self.r4.at[1, :, n], r.to_f(-1))
        self.a, self.b = a, b

    def five(self):
        r, c, n = self.ring, self.cols, self.near
        self.a.wait_recv()
        self.b.wait_recv()
        self.final[self.z, :, c] = added(
            self.sums[r.f, :, n], self.r4[0, :, n], self.r4[1, :, n]
        ).astype(jnp.bfloat16)
        part = self.final.at[self.z, :, c]
        self.zs = [self.wires.copy(part, part, {"ctx": place(self.z + k)}) for k in (1, 3, 2)]

    def finish(self):
        for made in self.zs:
            made.wait_recv()


def greet(targets):
    barrier = pltpu.get_barrier_semaphore()
    for target in targets:
        pl.semaphore_signal(barrier, inc=1, device_id=target, device_id_type=MESH)
    pl.semaphore_wait(barrier, len(targets))


def spot():
    d = lax.axis_index("dp")
    return lax.rem(d, 4), lax.div(d, 4), lax.axis_index("ctx")


def dot(a, b, dims=NN):
    return lax.dot_general(a, b, (dims, ((), ())), preferred_element_type=F32)


def rms(field):
    return lax.rsqrt(jnp.mean(field * field, axis=-1, keepdims=True) + EPSILON)


def norm_back(field, gain, grad):
    r = rms(field)
    hat = field * r
    scaled = grad * gain
    back = r * (scaled - hat * jnp.mean(scaled * hat, axis=-1, keepdims=True))
    return back, jnp.sum(grad * hat, axis=0, keepdims=True)


def turn(field, cos, sin):
    a, b = field[:, :128], field[:, 128:]
    return jnp.concatenate([a * cos - b * sin, b * cos + a * sin], axis=1)


def turn_back(field, cos, sin):
    a, b = field[:, :128], field[:, 128:]
    return jnp.concatenate([a * cos + b * sin, b * cos - a * sin], axis=1)


def fold(block):
    half = block.shape[-1] // 2
    return jnp.concatenate([block[..., :half], block[..., half:]], axis=-2)


def unfold(block):
    rows = block.shape[-2] // 2
    return jnp.concatenate([block[..., :rows, :], block[..., rows:, :]], axis=-1)


def iota(shape, axis):
    return lax.broadcasted_iota(jnp.int32, shape, axis)


SCRATCH = dict(
    wire=((80, WIRE), LOW),
    whole=((4, 4, 80, WIRE), LOW),
    pad=((1024, 128), F32),
    tall=((128, D), F32),
    wq=((D, 512), LOW),
    wkv=((D, HD), LOW),
    wo=((D, 512), LOW),
    wg=((D, FFH), LOW),
    wu=((D, FFH), LOW),
    wd=((D, FFH), LOW),
    gains=((8, D), F32),
    heads=((8, HD), F32),
    dgains=((8, D), F32),
    dheads=((8, HD), F32),
    tokh=((ROWS, D), LOW),
    segp=((1, ROWS), jnp.int32),
    lo_col=((ROWS, 128), F32),
    lo_row=((8, ROWS), F32),
    cos=((1024, 128), F32),
    sin=((1024, 128), F32),
    n1=((1024, D), LOW),
    n1t=((D, ROWS), LOW),
    kvb=((2, 1024, HD), LOW),
    kvraw=((ROWS, HD), F32),
    qraw=((4, 256, HD), F32),
    q=((4, 256, HD), LOW),
    o=((ROWS, 512), LOW),
    go=((4, 256, HD), LOW),
    gqr=((ROWS, 512), LOW),
    a=((ROWS, D), F32),
    h=((ROWS, D), F32),
    n2=((ROWS, D), LOW),
    n2t=((D, ROWS), LOW),
    ga=((ROWS, FFH), F32),
    gb=((ROWS, FFH), F32),
    u=((ROWS, FFH), LOW),
    ggu=((ROWS, 2 * FFH), LOW),
    gf=((ROWS, D), LOW),
    gft=((D, ROWS), LOW),
    gal=((ROWS, D), LOW),
    gat=((D, ROWS), LOW),
    gh=((ROWS, D), F32),
    snd=((2, ROWS, D), LOW),
    rcv=((2, ROWS, D), LOW),
    gkv=((2, 1024, HD), F32),
    kvs=((1024, HD), LOW),
    kvr=((1024, HD), LOW),
    hs=((ROWS, HD), LOW),
    hr=((ROWS, HD), LOW),
    gkr=((ROWS, HD), LOW),
    final=((4, 80, WIRE), LOW),
    mine=((80, 256), F32),
    theirs=((80, 256), F32),
)


def layer_kernel(tok, seg_row, seg_col, cot, wq, wkv, wo, wgu, wd, ng, hg, out, igrad, grads, *rest):
    names = list(SCRATCH)
    g = types.SimpleNamespace(**dict(zip(names, rest[: len(names)])))
    rest = rest[len(names) :]
    bufs = (rest[0:5], rest[5:10])
    x, y, z = spot()
    core = lax.axis_index("tensor")
    mate = {"tensor": 1 - core}
    rings = (Ring("x", x, y), Ring("y", x, y))
    gather_wires = Wires(rest[10], rest[11])
    scatter_wires = Wires(rest[12], rest[13])
    other = Wires(rest[14], rest[15])
    greet(
        [r.to_f(k) for r in rings for k in (1, -1)]
        + [{"ctx": place(z + k)} for k in (1, 2, 3)]
        + [mate]
    )

    pieces = [
        [Gather(ring, gather_wires, g.wire, g.whole, *piece[i]) for i, ring in enumerate(rings)]
        for piece in GATHERS
    ]

    def step(part, name):
        for one in part:
            getattr(one, name)()

    p0, p1, p2, p3 = pieces

    g.pad[...] = jnp.zeros((1024, 128), F32)
    g.tall[...] = jnp.zeros((128, D), F32)
    g.wire[:, KV:QUERY] = fold(wkv[:, pl.ds(pl.multiple_of(core * HD, HD), HD)].astype(F32)).astype(LOW)
    g.wire[:, QUERY:EXTRA] = fold(wq[...].astype(F32)).astype(LOW)
    g.tall[0:4, 0:40] = ng[...].astype(F32)
    g.tall[0:2, 128:144] = hg[...].astype(F32)
    first = jnp.transpose(g.tall[:, 0:128])[:40]
    second = jnp.transpose(g.tall[:, 128:256])[:40]
    g.wire[:, EXTRA:OUT] = jnp.concatenate([first, second], axis=0).astype(LOW)
    step(p0, "one")
    g.whole[y, x, :, KV:OUT] = g.wire[:, KV:OUT]
    tok_wire = other.copy(tok, g.tokh, {"ctx": place(z + 1)})
    seg_wire = other.copy(seg_row, g.segp, {"ctx": place(z + 1)})
    g.pad[0:512, 0:40] = wo[...].astype(F32)
    g.wire[:, OUT:GATEUP] = fold(jnp.transpose(g.pad[0:512, :])[:40]).astype(LOW)
    step(p1, "one")
    g.whole[y, x, :, OUT:GATEUP] = g.wire[:, OUT:GATEUP]
    step(p0, "two")
    for i in range(2):
        g.wire[40 * i : 40 * i + 40, GATEUP:DOWN] = wgu[i]
    step(p2, "one")
    g.whole[y, x, :, GATEUP:DOWN] = g.wire[:, GATEUP:DOWN]
    step(p1, "two")
    step(p0, "three")
    g.pad[:, 0:40] = wd[...].astype(F32)
    g.wire[:, DOWN:WIRE] = fold(jnp.transpose(g.pad[...])[:40]).astype(LOW)
    step(p3, "one")
    g.whole[y, x, :, DOWN:WIRE] = g.wire[:, DOWN:WIRE]

    rates = jnp.exp(iota((1, 128), 1).astype(F32) * (-2.0 * math.log(10000.0) / HD))
    fine = iota((128, 128), 0).astype(F32) * rates
    fine_cos, fine_sin = jnp.cos(fine), jnp.sin(fine)
    coarse = (iota((8, 128), 0) * 128 + (z * ROWS - ROWS)).astype(F32) * rates
    coarse_cos, coarse_sin = jnp.cos(coarse), jnp.sin(coarse)
    for i in range(8):
        cc, cs = coarse_cos[i : i + 1], coarse_sin[i : i + 1]
        g.cos[128 * i : 128 * i + 128] = fine_cos * cc - fine_sin * cs
        g.sin[128 * i : 128 * i + 128] = fine_sin * cc + fine_cos * cs
    step(p1, "three")
    step(p2, "two")
    step(p0, "four")
    seg_wire.wait_recv()
    column = seg_col[...]
    below_prior = jnp.sum((g.segp[...] < column).astype(F32), axis=1, keepdims=True)
    below_prior = jnp.where(z == 0, float(ROWS), below_prior)
    below_own = jnp.sum((seg_row[...] < column).astype(F32), axis=1, keepdims=True)
    lowest = jnp.maximum(below_prior + below_own, iota((ROWS, 1), 0).astype(F32) + 1.0)
    lowest = jnp.broadcast_to(lowest, (ROWS, 128))
    g.lo_col[...] = lowest
    g.lo_row[...] = jnp.transpose(lowest)[0:8]
    g.dgains[...] = jnp.zeros((8, D), F32)
    g.dheads[...] = jnp.zeros((8, HD), F32)
    g.gkv[...] = jnp.zeros((2, 1024, HD), F32)
    step(p3, "two")
    step(p1, "four")
    step(p2, "three")

    def assemble(first, second, start, width, w=128):
        def one(i, carry):
            at = pl.multiple_of(i * w, w)
            block = g.whole[:, :, :, pl.ds(start + at, w)].astype(F32)
            first[:, pl.ds(at, w)] = block[:, :, :40].reshape(D, w).astype(LOW)
            if second is None:
                first[:, pl.ds(at + width, w)] = block[:, :, 40:].reshape(D, w).astype(LOW)
            else:
                second[:, pl.ds(at, w)] = block[:, :, 40:].reshape(D, w).astype(LOW)
            return carry

        lax.fori_loop(0, width // w, one, 0)

    step(p0, "finish")
    block = g.whole[:, :, :, EXTRA:OUT].astype(F32)
    g.gains[...] = jnp.transpose(block[:, :, :40].reshape(D, 128))[:8]
    spread_heads = jnp.transpose(block[:, :, 40:].reshape(D, 128))[:8]
    column_at, head_at = iota((D, HD), 0), iota((D, HD), 1)
    pick = (column_at == 40 * (head_at >> 4) + (head_at & 15)).astype(F32).astype(LOW)
    g.heads[...] = dot(spread_heads.astype(LOW), pick)
    assemble(g.wkv, None, KV, 128)
    assemble(g.wq, None, QUERY, 256)

    gain0, gain1, gain2, gain3 = (g.gains[i : i + 1] for i in range(4))
    qgain, kgain = g.heads[0:1], g.heads[1:2]

    def keys_of(start, normed):
        raw = dot(normed, g.wkv[...])
        at = slice(start, start + 256)
        if start >= ROWS:
            g.kvraw[start - ROWS : start - ROWS + 256] = raw
        turned = turn(raw * rms(raw) * kgain, g.cos[at], g.sin[at])
        g.kvb[core, at] = jnp.where(core == 0, turned, raw).astype(LOW)

    for i in range(2):
        block = tok[256 * i : 256 * i + 256].astype(F32)
        normed = block * rms(block) * gain0
        g.n1[ROWS + 256 * i : ROWS + 256 * i + 256] = normed.astype(LOW)
        g.n1t[:, 256 * i : 256 * i + 256] = jnp.transpose(normed).astype(LOW)
        keys_of(ROWS + 256 * i, normed.astype(LOW))
    own_kv = g.kvb.at[core, pl.ds(ROWS, ROWS)]
    own_wire = other.copy(own_kv, own_kv, mate)
    tok_wire.wait_recv()
    for i in range(2):
        block = g.tokh[256 * i : 256 * i + 256].astype(F32)
        keys_of(256 * i, (block * rms(block) * gain0).astype(LOW))
    prior_kv = g.kvb.at[core, pl.ds(0, ROWS)]
    prior_wire = other.copy(prior_kv, prior_kv, mate)
    for i in range(2):
        raw = dot(g.n1[ROWS + 256 * i : ROWS + 256 * i + 256], g.wq[...])
        at = slice(ROWS + 256 * i, ROWS + 256 * i + 256)
        for h in range(2):
            part = raw[:, HD * h : HD * h + HD]
            turned = turn(part * rms(part) * qgain, g.cos[at], g.sin[at]).astype(LOW)
            for j in range(2):
                g.qraw[2 * i + j, 128 * h : 128 * h + 128] = part[128 * j : 128 * j + 128]
                g.q[2 * i + j, 128 * h : 128 * h + 128] = turned[128 * j : 128 * j + 128]
    step(p3, "three")
    step(p2, "four")
    own_wire.wait_recv()
    prior_wire.wait_recv()

    def twice(block, axis):
        return jnp.concatenate([block, block], axis=axis)

    def attend(b, carry):
        start = pl.multiple_of(b * 128, 128)
        keys, values = g.kvb[0, pl.ds(start, D)], g.kvb[1, pl.ds(start, D)]
        scores = dot(g.q[b], keys, NT) * SCALE
        lowest = twice(g.lo_col[pl.ds(start, 128), 0:1], 0) - (b * 128).astype(F32)
        place_k = iota((256, D), 1).astype(F32)
        highest = (iota((256, 1), 0) & 127).astype(F32) + float(WINDOW)
        scores = jnp.where((place_k >= lowest) & (place_k <= highest), scores, -1e30)
        expo = jnp.exp(scores - jnp.max(scores, axis=-1, keepdims=True))
        probs = (expo / jnp.sum(expo, axis=-1, keepdims=True)).astype(LOW)
        mixed = dot(probs, values).astype(LOW)
        g.o[pl.ds(start, 128), 0:HD] = mixed[:128]
        g.o[pl.ds(start, 128), HD : 2 * HD] = mixed[128:]
        return carry

    lax.fori_loop(0, 4, attend, 0)
    step(p1, "finish")
    assemble(g.wo, None, OUT, 256)

    halves = [slice(0, 256), slice(256, 512)]

    def swap(number, rows, value):
        g.snd[number, rows] = value.astype(LOW)
        return other.copy(g.snd.at[number, rows], g.rcv.at[number, rows], mate)

    def total(number, rows):
        return g.snd[number, rows].astype(F32) + g.rcv[number, rows].astype(F32)

    sent = [swap(0, rows, dot(g.o[rows], g.wo[...], NT)) for rows in halves]
    step(p3, "four")
    for i, rows in enumerate(halves):
        sent[i].wait_recv()
        branch = total(0, rows)
        g.a[rows] = branch
        hidden = tok[rows].astype(F32) + branch * rms(branch) * gain1
        g.h[rows] = hidden
        normed = hidden * rms(hidden) * gain2
        g.n2[rows] = normed.astype(LOW)
        g.n2t[:, rows] = jnp.transpose(normed).astype(LOW)
    for made in sent:
        made.wait_send()
    step(p2, "finish")
    assemble(g.wg, g.wu, GATEUP, FFH)

    c0, c1 = math.sqrt(2.0 / math.pi), 0.044715

    def forward_ff(i, carry):
        at = pl.multiple_of(i * 256, 256)
        cols = pl.ds(at, 256)
        for rows in halves:
            gate = dot(g.n2[rows], g.wg[:, cols])
            up = dot(g.n2[rows], g.wu[:, cols])
            square = gate * gate
            t = jnp.tanh(c0 * gate * (1.0 + c1 * square))
            act = 0.5 * gate * (1.0 + t)
            slope = 0.5 * (1.0 + t) + 0.5 * gate * (1.0 - t * t) * (c0 * (1.0 + 3.0 * c1 * square))
            g.ga[rows, cols] = act
            g.gb[rows, cols] = up * slope
            g.u[rows, cols] = (act * up).astype(LOW)
        return carry

    lax.fori_loop(0, 4, forward_ff, 0)
    step(p3, "finish")
    gather_wires.drain()
    assemble(g.wd, None, DOWN, 512)

    sent = [swap(1, rows, dot(g.u[rows], g.wd[...], NT)) for rows in halves]
    for i, rows in enumerate(halves):
        sent[i].wait_recv()
        feed = total(1, rows)
        out[rows] = (g.h[rows] + feed * rms(feed) * gain3).astype(LOW)
        back, slope = norm_back(feed, gain3, cot[rows].astype(F32))
        g.dgains[3:4] += slope
        g.gf[rows] = back.astype(LOW)
        g.gft[:, rows] = jnp.transpose(back).astype(LOW)
    for made in sent:
        made.wait_send()

    def backward_ff(i, carry):
        at = pl.multiple_of(i * 256, 256)
        cols = pl.ds(at, 256)
        for rows in halves:
            inner = dot(g.gf[rows], g.wd[:, cols])
            g.ggu[rows, cols] = (inner * g.gb[rows, cols]).astype(LOW)
            g.ggu[rows, pl.ds(at + FFH, 256)] = (inner * g.ga[rows, cols]).astype(LOW)
        return carry

    lax.fori_loop(0, 4, backward_ff, 0)
    sent = [
        swap(
            0,
            rows,
            dot(g.ggu[rows, 0:FFH], g.wg[...], NT) + dot(g.ggu[rows, FFH:], g.wu[...], NT),
        )
        for rows in halves
    ]

    parts, offsets = [], [0, 0]
    for piece in SCATTERS:
        made = []
        for i, ring in enumerate(rings):
            if piece[i] is not None:
                start, width = piece[i]
                made.append(
                    Scatter(
                        ring, scatter_wires, g.whole, bufs[i], g.final, z, start, width, offsets[i]
                    )
                )
                offsets[i] += width
        parts.append(made)
    s0, s1, s2, s3, se = parts

    def put(left, right, start, begin, end, gap, w=256):
        def one(i, carry):
            at = pl.multiple_of(i * w, w)
            first = dot(left[...], right[:, pl.ds(at, w)]).reshape(16, 40, w)
            second = dot(left[...], right[:, pl.ds(at + gap, w)]).reshape(16, 40, w)
            block = jnp.concatenate([first, second], axis=1).astype(LOW)
            g.whole[:, :, :, pl.ds(start + at, w)] = block.reshape(4, 4, 80, w)
            return carry

        lax.fori_loop(begin // w, end // w, one, 0)

    put(g.gft, g.u, DOWN, 0, 512, 512)
    step(s3, "one")
    put(g.n2t, g.ggu, GATEUP, 0, 512, FFH)
    step(s2[:1], "one")
    step(s3, "two")
    put(g.n2t, g.ggu, GATEUP, 512, 1024, FFH)
    step(s2[1:], "one")
    for i, rows in enumerate(halves):
        sent[i].wait_recv()
        back, slope = norm_back(g.h[rows], gain2, total(0, rows))
        g.dgains[2:3] += slope
        hidden = cot[rows].astype(F32) + back
        g.gh[rows] = hidden
        back, slope = norm_back(g.a[rows], gain1, hidden)
        g.dgains[1:2] += slope
        low = back.astype(LOW)
        g.gat[:, rows] = jnp.transpose(back).astype(LOW)
        grad = dot(low, g.wo[...]).astype(LOW)
        for j in range(2):
            for h in range(2):
                g.go[2 * i + j, 128 * h : 128 * h + 128] = grad[
                    128 * j : 128 * j + 128, HD * h : HD * h + HD
                ]
    for made in sent:
        made.wait_send()
    step(s3, "three")
    step(s2[:1], "two")
    put(g.gat, g.o, OUT, 0, 256, 256)
    step(s1, "one")
    step(s2[1:], "two")

    def attend_back(b, carry):
        start = pl.multiple_of(b * 128, 128)
        keys, values = g.kvb[0, pl.ds(start, D)], g.kvb[1, pl.ds(start, D)]
        queries, grad = g.q[b], g.go[b]
        scores = dot(keys, queries, NT) * SCALE
        lowest = twice(g.lo_row[0:1, pl.ds(start, 128)], 1) - (b * 128).astype(F32)
        place_k = iota((D, 256), 0).astype(F32)
        highest = (iota((1, 256), 1) & 127).astype(F32) + float(WINDOW)
        scores = jnp.where((place_k >= lowest) & (place_k <= highest), scores, -1e30)
        expo = jnp.exp(scores - jnp.max(scores, axis=0, keepdims=True))
        probs = expo * (1.0 / jnp.sum(expo, axis=0, keepdims=True))
        grad_probs = dot(values, grad, NT)
        spread = jnp.sum(probs * grad_probs, axis=0, keepdims=True)
        grad_scores = (probs * (grad_probs - spread)).astype(LOW)
        g.gkv[0, pl.ds(start, D)] += dot(grad_scores, queries) * SCALE
        g.gkv[1, pl.ds(start, D)] += dot(probs.astype(LOW), grad)
        grad_q = dot(grad_scores, keys, TN) * SCALE
        at = pl.ds(pl.multiple_of(ROWS + start, 128), 128)
        grad_q = turn_back(grad_q, twice(g.cos[at], 0), twice(g.sin[at], 0))
        back, slope = norm_back(g.qraw[b], qgain, grad_q)
        g.dheads[0:1] += slope
        g.gqr[pl.ds(start, 128), 0:HD] = back[:128].astype(LOW)
        g.gqr[pl.ds(start, 128), HD : 2 * HD] = back[128:].astype(LOW)
        return carry

    lax.fori_loop(0, 2, attend_back, 0)
    step(s3, "four")
    step(s2[:1], "three")
    lax.fori_loop(2, 4, attend_back, 0)
    g.kvs[...] = g.gkv[1 - core].astype(LOW)
    kv_wire = other.copy(g.kvs, g.kvr, mate)
    step(s2[1:], "three")
    step(s1, "two")
    step(s3, "five")
    put(g.n1t, g.gqr, QUERY, 0, 256, 256)
    kv_wire.wait_recv()
    g.hs[...] = added(g.gkv[core, 0:ROWS], g.kvr[0:ROWS]).astype(LOW)
    halo_wire = other.copy(g.hs, g.hr, {"ctx": place(z - 1)})
    step(s2, "four")
    step(s1, "three")
    halo_wire.wait_recv()
    for i, rows in enumerate(halves):
        after = slice(ROWS + 256 * i, ROWS + 256 * i + 256)
        grad = added(g.gkv[core, after], g.kvr[after], g.hr[rows])
        back, slope = norm_back(g.kvraw[rows], kgain, turn_back(grad, g.cos[after], g.sin[after]))
        g.dheads[1:2] += jnp.where(core == 0, slope, 0.0)
        low = jnp.where(core == 0, back, grad).astype(LOW)
        g.gkr[rows] = low
    put(g.n1t, g.gkr, KV, 0, 128, 128, w=128)
    step(s0, "one")
    sent = [
        swap(1, rows, dot(g.gqr[rows], g.wq[...], NT) + dot(g.gkr[rows], g.wkv[...], NT))
        for rows in halves
    ]
    step(s2, "five")
    step(s1, "four")
    for i, rows in enumerate(halves):
        sent[i].wait_recv()
        back, slope = norm_back(tok[rows].astype(F32), gain0, total(1, rows))
        g.dgains[0:1] += slope
        igrad[rows] = g.gh[rows] + back
    g.tall[...] = jnp.zeros((128, D), F32)
    g.tall[0:8] = g.dgains[...]
    first = jnp.transpose(g.tall[...]).reshape(16, 40, 128)
    g.tall[0:8] = dot(g.dheads[...].astype(LOW), pick, NT)
    second = jnp.transpose(g.tall[...]).reshape(16, 40, 128)
    block = jnp.concatenate([first, second], axis=1).astype(LOW)
    g.whole[:, :, :, EXTRA:OUT] = block.reshape(4, 4, 80, 128)
    step(se, "one")
    step(s0, "two")
    step(s1, "five")
    step(se, "two")
    step(s0, "three")
    step(s3, "finish")

    def put_final(start, width):
        cols = pl.ds(start, width)
        return added(*(g.final[i, :, cols] for i in range(4)))

    grads[:, DOWN + 128 : WIRE + 128] = put_final(DOWN, 512)
    step(se, "three")
    step(s0, "four")
    step(s2, "finish")
    grads[:, GATEUP + 128 : DOWN + 128] = put_final(GATEUP, 1024)
    step(se, "four")
    step(s0, "five")
    step(s1, "finish")
    grads[:, OUT + 128 : GATEUP + 128] = put_final(OUT, 256)
    step(se, "five")
    step(s0, "finish")
    g.mine[:, 0:128] = put_final(KV, 128)
    grads[:, QUERY + 128 : EXTRA + 128] = put_final(QUERY, 256)
    step(se, "finish")
    ends = put_final(EXTRA, 128)
    g.mine[:, 128:256] = ends
    last_wire = other.copy(g.mine, g.theirs, mate)
    last_wire.wait_recv()
    own, far = g.mine[:, 0:128], g.theirs[:, 0:128]
    grads[:, 0:128] = jnp.where(core == 0, own, far)
    grads[:, 128:256] = jnp.where(core == 0, far, own)
    grads[0:40, EXTRA + 128 : OUT + 128] = ends[:40]
    grads[40:80, EXTRA + 128 : OUT + 128] = ends[40:] + g.theirs[40:80, 128:256]
    scatter_wires.drain()
    for made in (tok_wire, seg_wire, own_wire, prior_wire, kv_wire, halo_wire, last_wire, *sent):
        made.wait_send()


def vmem():
    return pl.BlockSpec(memory_space=pltpu.VMEM)


def ring_buffers():
    return [
        pltpu.VMEM((2, 2, 80, SET_COLS), LOW),
        pltpu.VMEM((2, 4, 80, SET_COLS), LOW),
        pltpu.VMEM((4, 80, SET_COLS), LOW),
        pltpu.VMEM((80, SET_COLS), LOW),
        pltpu.VMEM((2, 80, SET_COLS), LOW),
    ]


def shards(
    tokens, segments, cotangent, w_query, w_keyval, w_out, w_gateup, w_down, norm_gains, head_gains
):
    output, input_grad, done = pl.pallas_call(
        layer_kernel,
        out_shape=(
            jax.ShapeDtypeStruct((ROWS, D), LOW),
            jax.ShapeDtypeStruct((ROWS, D), F32),
            jax.ShapeDtypeStruct((80, WIRE + 128), F32),
        ),
        in_specs=[vmem()] * 11,
        out_specs=(vmem(),) * 3,
        scratch_shapes=[
            *(pltpu.VMEM(*shape) for shape in SCRATCH.values()),
            *ring_buffers(),
            *ring_buffers(),
            pltpu.SemaphoreType.DMA((64,)),
            pltpu.SemaphoreType.DMA((64,)),
            pltpu.SemaphoreType.DMA((99,)),
            pltpu.SemaphoreType.DMA((99,)),
            pltpu.SemaphoreType.DMA((16,)),
            pltpu.SemaphoreType.DMA((16,)),
        ],
        compiler_params=pltpu.CompilerParams(
            collective_id=0, has_side_effects=True, vmem_limit_bytes=VMEM_BYTES
        ),
    )(
        tokens[0],
        segments,
        segments.reshape(ROWS, 1),
        cotangent[0],
        w_query,
        w_keyval,
        w_out,
        w_gateup,
        w_down,
        norm_gains,
        head_gains,
    )
    kv, query, extra, wide, gateup, down = 0, 256, 512, 640, 896, 1920
    keyval = jnp.concatenate([unfold(done[:, 0:128]), unfold(done[:, 128:256])], axis=1)
    return (
        output[None],
        input_grad[None],
        unfold(done[:, query:extra]),
        keyval,
        unfold(done[:, wide:gateup]).T,
        done[:, gateup:down].reshape(2, 40, -1),
        unfold(done[:, down:]).T,
        done[:40, extra : extra + 4].T,
        done[40:56, extra : extra + 2].T,
    )


def solution(mesh):
    placed = (
        P("dp", "ctx", None),
        P("dp", "ctx"),
        P("dp", "ctx", None),
        P("dp", "tensor"),
        P("dp", None),
        P("tensor", "dp"),
        P(None, "dp", "tensor"),
        P("tensor", "dp"),
        P(None, "dp"),
        P(None, "dp"),
    )
    return jax.shard_map(
        shards,
        mesh=mesh,
        in_specs=placed,
        out_specs=(
            P("dp", "ctx", None),
            P("dp", "ctx", None),
            P("dp", "tensor"),
            P("dp", None),
            P("tensor", "dp"),
            P(None, "dp", "tensor"),
            P("tensor", "dp"),
            P(None, "dp"),
            P(None, "dp"),
        ),
        check_vma=False,
    )
```

```python
import math
import types

import jax
import jax.numpy as jnp
from jax import lax
from jax.experimental import pallas as pl
from jax.experimental.pallas import tpu as pltpu
from jax.sharding import PartitionSpec as P

WINDOW = 512
EPSILON = 1e-06
MESH = pl.DeviceIdType.MESH
VMEM_BYTES = 60 * 1024 * 1024

KV, QUERY, EXTRA, OUT, GATEUP, DOWN, WIRE = 0, 128, 384, 512, 768, 1792, 2304
GATHERS = (
    ((0, 256), (256, 256)),
    ((512, 128), (640, 128)),
    ((768, 512), (1280, 512)),
    ((1792, 256), (2048, 256)),
)
SCATTERS = (
    ((0, 256), (256, 128)),
    ((512, 128), (640, 128)),
    ((768, 512), (1280, 512)),
    ((1792, 256), (2048, 256)),
    (None, (384, 128)),
)
SET_COLS = 1152
CUT = 48
ROWS, D, HD, FFH = 512, 640, 256, 1024
SCALE = 1.0 / math.sqrt(HD)
LOW = jnp.bfloat16
F32 = jnp.float32
NN, NT, TN = ((1,), (0,)), ((1,), (1,)), ((0,), (0,))


def place(u):
    return lax.rem(u + 8, 4)


class Wires:
    def __init__(self, send, recv):
        self.send, self.recv, self.used = send, recv, 0
        self.started = []

    def copy(self, src, dst, target):
        index = self.used
        self.used += 1
        made = pltpu.make_async_remote_copy(
            src_ref=src,
            dst_ref=dst,
            send_sem=self.send.at[index],
            recv_sem=self.recv.at[index],
            device_id=target,
            device_id_type=MESH,
        )
        made.start()
        self.started.append(made)
        return made

    def drain(self):
        for made in self.started:
            made.wait_send()
        self.started = []


class Ring:
    def __init__(self, first, x, y):
        self.first = first
        self.f, self.s = (x, y) if first == "x" else (y, x)

    def slot(self, ref, f, s, *rest):
        return ref.at[(s, f) + rest] if self.first == "x" else ref.at[(f, s) + rest]

    def index(self, f, s):
        return (s, f) if self.first == "x" else (f, s)

    def to_f(self, step):
        f = place(self.f + step)
        return {"dp": self.s * 4 + f} if self.first == "x" else {"dp": f * 4 + self.s}

    def to_s(self, step):
        s = place(self.s + step)
        return {"dp": s * 4 + self.f} if self.first == "x" else {"dp": self.f * 4 + s}


class Gather:
    def __init__(self, ring, wires, shard, whole, start, width):
        self.ring, self.wires, self.shard, self.whole = ring, wires, shard, whole
        self.cols = pl.ds(start, width)

    def one(self):
        r, c = self.ring, self.cols
        src = self.shard.at[:, c]
        dst = r.slot(self.whole, r.f, r.s, slice(None), c)
        self.a = self.wires.copy(src, dst, r.to_f(1))
        self.b = self.wires.copy(src, dst, r.to_f(-1))

    def two(self):
        r, c = self.ring, self.cols
        self.a.wait_recv()
        part = r.slot(self.whole, place(r.f - 1), r.s, pl.ds(0, CUT), c)
        a = self.wires.copy(part, part, r.to_f(1))
        self.b.wait_recv()
        part = r.slot(self.whole, place(r.f + 1), r.s, pl.ds(CUT, 80 - CUT), c)
        b = self.wires.copy(part, part, r.to_f(-1))
        self.a, self.b = a, b

    def three(self):
        r, c = self.ring, self.cols
        self.a.wait_recv()
        self.b.wait_recv()
        part = r.slot(self.whole, slice(None), r.s, slice(None), c)
        self.a = self.wires.copy(part, part, r.to_s(1))
        self.b = self.wires.copy(part, part, r.to_s(-1))

    def four(self):
        r, c = self.ring, self.cols
        self.a.wait_recv()
        part = r.slot(self.whole, pl.ds(0, 2), place(r.s - 1), slice(None), c)
        a = self.wires.copy(part, part, r.to_s(1))
        self.b.wait_recv()
        part = r.slot(self.whole, pl.ds(2, 2), place(r.s + 1), slice(None), c)
        b = self.wires.copy(part, part, r.to_s(-1))
        self.a, self.b = a, b

    def finish(self):
        self.a.wait_recv()
        self.b.wait_recv()


def added(*terms):
    total = terms[0].astype(jnp.float32)
    for term in terms[1:]:
        total = total + term.astype(jnp.float32)
    return total


class Scatter:
    def __init__(self, ring, wires, grads, bufs, final, z, start, width, offset, far):
        self.ring, self.wires, self.grads, self.final, self.z = ring, wires, grads, final, z
        self.r1, self.r2, self.sums, self.r3, self.r4 = bufs
        self.cols = pl.ds(start, width)
        self.near = pl.ds(offset, width)
        self.far, self.start = far, start

    def one(self):
        r, c, n = self.ring, self.cols, self.near
        far = place(r.s + 2)
        self.a = self.wires.copy(
            r.slot(self.grads, pl.ds(0, 2), far, slice(None), c), self.r1.at[0, :, :, n], r.to_s(1)
        )
        self.b = self.wires.copy(
            r.slot(self.grads, pl.ds(2, 2), far, slice(None), c), self.r1.at[1, :, :, n], r.to_s(-1)
        )

    def two(self):
        r, c, n = self.ring, self.cols, self.near
        after, before = place(r.s + 1), place(r.s - 1)
        self.a.wait_recv()
        for i in range(2):
            at = r.index(i, after) + (slice(None), c)
            self.grads[at] = added(self.grads[at], self.r1[0, i, :, n]).astype(jnp.bfloat16)
        a = self.wires.copy(
            r.slot(self.grads, slice(None), after, slice(None), c), self.r2.at[0, :, :, n], r.to_s(1)
        )
        self.b.wait_recv()
        for i in range(2):
            at = r.index(2 + i, before) + (slice(None), c)
            self.grads[at] = added(self.grads[at], self.r1[1, i, :, n]).astype(jnp.bfloat16)
        b = self.wires.copy(
            r.slot(self.grads, slice(None), before, slice(None), c),
            self.r2.at[1, :, :, n],
            r.to_s(-1),
        )
        self.a, self.b = a, b

    def three(self):
        r, c, n = self.ring, self.cols, self.near
        self.a.wait_recv()
        self.b.wait_recv()
        for i in range(4):
            at = r.index(i, r.s) + (slice(None), c)
            self.sums[i, :, n] = added(
                self.grads[at], self.r2[0, i, :, n], self.r2[1, i, :, n]
            ).astype(jnp.bfloat16)
        far = place(r.f + 2)
        self.a = self.wires.copy(
            self.sums.at[far, pl.ds(0, CUT), n], self.r3.at[pl.ds(0, CUT), n], r.to_f(1)
        )
        self.b = self.wires.copy(
            self.sums.at[far, pl.ds(CUT, 80 - CUT), n],
            self.r3.at[pl.ds(CUT, 80 - CUT), n],
            r.to_f(-1),
        )

    def four(self):
        r, n = self.ring, self.near
        after, before = place(r.f + 1), place(r.f - 1)
        top, low = pl.ds(0, CUT), pl.ds(CUT, 80 - CUT)
        self.a.wait_recv()
        self.sums[after, top, n] = added(self.sums[after, top, n], self.r3[top, n]).astype(
            jnp.bfloat16
        )
        a = self.wires.copy(self.sums.at[after, :, n], self.r4.at[0, :, n], r.to_f(1))
        self.b.wait_recv()
        self.sums[before, low, n] = added(self.sums[before, low, n], self.r3[low, n]).astype(
            jnp.bfloat16
        )
        b = self.wires.copy(self.sums.at[before, :, n], self.r4.at[1, :, n], r.to_f(-1))
        self.a, self.b = a, b

    def five(self):
        r, c, n = self.ring, self.cols, self.near
        self.a.wait_recv()
        self.b.wait_recv()
        self.final[self.z, :, c] = added(
            self.sums[r.f, :, n], self.r4[0, :, n], self.r4[1, :, n]
        ).astype(jnp.bfloat16)
        part = self.final.at[self.z, :, c]
        self.zs = [self.wires.copy(part, part, {"ctx": place(self.z + k)}) for k in (1, 3, 2)]
        if self.far is not None:
            part = self.final.at[self.z, :, pl.ds(self.start, 128)]
            self.zs += [self.wires.copy(part, self.far[0], target) for target in self.far[1]]

    def finish(self):
        for made in self.zs:
            made.wait_recv()


def spot():
    d = lax.axis_index("dp")
    return lax.rem(d, 4), lax.div(d, 4), lax.axis_index("ctx")


def dot(a, b, dims=NN):
    return lax.dot_general(a, b, (dims, ((), ())), preferred_element_type=F32)


def rms(field):
    return lax.rsqrt(jnp.mean(field * field, axis=-1, keepdims=True) + EPSILON)


def norm_back(field, gain, grad):
    r = rms(field)
    hat = field * r
    scaled = grad * gain
    back = r * (scaled - hat * jnp.mean(scaled * hat, axis=-1, keepdims=True))
    return back, jnp.sum(grad * hat, axis=0, keepdims=True)


def turn(field, cos, sin):
    a, b = field[:, :128], field[:, 128:]
    return jnp.concatenate([a * cos - b * sin, b * cos + a * sin], axis=1)


def turn_back(field, cos, sin):
    a, b = field[:, :128], field[:, 128:]
    return jnp.concatenate([a * cos + b * sin, b * cos - a * sin], axis=1)


def fold(block):
    half = block.shape[-1] // 2
    return jnp.concatenate([block[..., :half], block[..., half:]], axis=-2)


def unfold(block):
    rows = block.shape[-2] // 2
    return jnp.concatenate([block[..., :rows, :], block[..., rows:, :]], axis=-1)


def iota(shape, axis):
    return lax.broadcasted_iota(jnp.int32, shape, axis)


SCRATCH = dict(
    wire=((80, WIRE), LOW),
    whole=((4, 4, 80, WIRE), LOW),
    tall=((128, D), F32),
    wq=((D, 512), LOW),
    wkv=((D, HD), LOW),
    wo=((D, 512), LOW),
    wg=((D, FFH), LOW),
    wu=((D, FFH), LOW),
    wd=((D, FFH), LOW),
    gains=((8, D), F32),
    heads=((8, HD), F32),
    dgains=((8, D), F32),
    dheads=((8, HD), F32),
    tokh=((ROWS, D), LOW),
    segp=((1, ROWS), jnp.int32),
    lo_col=((ROWS, 128), F32),
    lo_row=((8, ROWS), F32),
    cos=((1024, 128), F32),
    sin=((1024, 128), F32),
    n1=((1024, D), LOW),
    n1t=((D, ROWS), LOW),
    kvb=((2, 1024, HD), LOW),
    kvraw=((ROWS, HD), F32),
    qraw=((4, 256, HD), F32),
    q=((4, 256, HD), LOW),
    o=((ROWS, 512), LOW),
    go=((4, 256, HD), LOW),
    gqr=((ROWS, 512), LOW),
    a=((ROWS, D), F32),
    h=((ROWS, D), F32),
    n2=((ROWS, D), LOW),
    n2t=((D, ROWS), LOW),
    ga=((ROWS, FFH), F32),
    gb=((ROWS, FFH), F32),
    u=((ROWS, FFH), LOW),
    ggu=((ROWS, 2 * FFH), LOW),
    gf=((ROWS, D), LOW),
    gft=((D, ROWS), LOW),
    gal=((ROWS, D), LOW),
    gat=((D, ROWS), LOW),
    gh=((ROWS, D), F32),
    snd=((2, ROWS, D), LOW),
    rcv=((2, ROWS, D), LOW),
    gkv=((2, 1024, HD), F32),
    kvs=((1024, HD), LOW),
    kvr=((1024, HD), LOW),
    hs=((ROWS, HD), LOW),
    hr=((ROWS, HD), LOW),
    gkr=((ROWS, HD), LOW),
    final=((4, 80, WIRE), LOW),
    far=((4, 80, 256), LOW),
)


def layer_kernel(tok, seg_row, cot, wq, wkv, wo, wgu, wd, ng, hg, out, igrad, grads, *rest):
    names = list(SCRATCH)
    g = types.SimpleNamespace(**dict(zip(names, rest[: len(names)])))
    rest = rest[len(names) :]
    bufs = (rest[0:5], rest[5:10])
    x, y, z = spot()
    core = lax.axis_index("tensor")
    mate = {"tensor": 1 - core}
    rings = (Ring("x", x, y), Ring("y", x, y))
    gather_wires = Wires(rest[10], rest[11])
    scatter_wires = Wires(rest[12], rest[13])
    other = Wires(rest[14], rest[15])
    targets = (
        [r.to_f(k) for r in rings for k in (1, -1)]
        + [{"ctx": place(z + k)} for k in (1, 2, 3)]
        + [{"ctx": place(z + k), "tensor": 1 - core} for k in range(4)]
    )
    barrier = pltpu.get_barrier_semaphore()
    for target in targets:
        pl.semaphore_signal(barrier, inc=1, device_id=target, device_id_type=MESH)

    pieces = [
        [Gather(ring, gather_wires, g.wire, g.whole, *piece[i]) for i, ring in enumerate(rings)]
        for piece in GATHERS
    ]

    def step(part, name):
        for one in part:
            getattr(one, name)()

    p0, p1, p2, p3 = pieces

    g.tall[...] = jnp.zeros((128, D), F32)
    g.wire[:, KV:QUERY] = fold(wkv[:, pl.ds(pl.multiple_of(core * HD, HD), HD)].astype(F32)).astype(LOW)
    g.wire[:, QUERY:EXTRA] = fold(wq[...].astype(F32)).astype(LOW)
    g.tall[0:4, 0:40] = ng[...].astype(F32)
    g.tall[0:2, 128:144] = hg[...].astype(F32)
    first = jnp.transpose(g.tall[:, 0:128])[:40]
    second = jnp.transpose(g.tall[:, 128:256])[:40]
    g.wire[:, EXTRA:OUT] = jnp.concatenate([first, second], axis=0).astype(LOW)
    pl.semaphore_wait(barrier, len(targets))
    step(p0, "one")
    seg_wire = other.copy(seg_row, g.segp, {"ctx": place(z + 1)})
    g.wire[:, OUT:GATEUP] = fold(wo[...].astype(F32)).astype(LOW)
    step(p1, "one")
    tok_wire = other.copy(tok, g.tokh, {"ctx": place(z + 1)})
    g.whole[y, x, :, KV:GATEUP] = g.wire[:, KV:GATEUP]
    g.wire[:, GATEUP:DOWN] = jnp.concatenate([wgu[0].astype(F32), wgu[1].astype(F32)], axis=0).astype(LOW)
    step(p0, "two")
    step(p2, "one")
    step(p1, "two")
    step(p0, "three")
    g.wire[:, DOWN:WIRE] = fold(wd[...].astype(F32)).astype(LOW)
    step(p3, "one")
    g.whole[y, x, :, GATEUP:WIRE] = g.wire[:, GATEUP:WIRE]

    rates = jnp.exp(iota((1, 128), 1).astype(F32) * (-2.0 * math.log(10000.0) / HD))
    fine = iota((128, 128), 0).astype(F32) * rates
    fine_cos, fine_sin = jnp.cos(fine), jnp.sin(fine)
    coarse = (iota((8, 128), 0) * 128 + (z * ROWS - ROWS)).astype(F32) * rates
    coarse_cos, coarse_sin = jnp.cos(coarse), jnp.sin(coarse)
    for i in range(8):
        cc, cs = coarse_cos[i : i + 1], coarse_sin[i : i + 1]
        g.cos[128 * i : 128 * i + 128] = fine_cos * cc - fine_sin * cs
        g.sin[128 * i : 128 * i + 128] = fine_sin * cc + fine_cos * cs
    step(p1, "three")
    step(p2, "two")
    step(p0, "four")
    seg_wire.wait_recv()
    own_ids, prior_ids = seg_row[...].astype(F32), g.segp[...].astype(F32)
    column = jnp.transpose(jnp.broadcast_to(own_ids, (128, ROWS)))[:, 0:1]
    below_prior = jnp.sum((prior_ids < column).astype(F32), axis=1, keepdims=True)
    below_prior = jnp.where(z == 0, float(ROWS), below_prior)
    below_own = jnp.sum((own_ids < column).astype(F32), axis=1, keepdims=True)
    lowest = jnp.maximum(below_prior + below_own, iota((ROWS, 1), 0).astype(F32) + 1.0)
    lowest = jnp.broadcast_to(lowest, (ROWS, 128))
    g.lo_col[...] = lowest
    g.lo_row[...] = jnp.transpose(lowest)[0:8]
    g.dgains[...] = jnp.zeros((8, D), F32)
    g.dheads[...] = jnp.zeros((8, HD), F32)
    g.gkv[...] = jnp.zeros((2, 1024, HD), F32)
    step(p3, "two")
    step(p1, "four")
    step(p2, "three")

    def assemble(first, second, start, width, w=128):
        def one(i, carry):
            at = pl.multiple_of(i * w, w)
            block = g.whole[:, :, :, pl.ds(start + at, w)].astype(F32)
            first[:, pl.ds(at, w)] = block[:, :, :40].reshape(D, w).astype(LOW)
            if second is None:
                first[:, pl.ds(at + width, w)] = block[:, :, 40:].reshape(D, w).astype(LOW)
            else:
                second[:, pl.ds(at, w)] = block[:, :, 40:].reshape(D, w).astype(LOW)
            return carry

        lax.fori_loop(0, width // w, one, 0)

    step(p0, "finish")
    block = g.whole[:, :, :, EXTRA:OUT].astype(F32)
    g.gains[...] = jnp.transpose(block[:, :, :40].reshape(D, 128))[:8]
    spread_heads = jnp.transpose(block[:, :, 40:].reshape(D, 128))[:8]
    column_at, head_at = iota((D, HD), 0), iota((D, HD), 1)
    pick = (column_at == 40 * (head_at >> 4) + (head_at & 15)).astype(F32).astype(LOW)
    g.heads[...] = dot(spread_heads.astype(LOW), pick)
    assemble(g.wkv, None, KV, 128)
    assemble(g.wq, None, QUERY, 256)

    gain0, gain1, gain2, gain3 = (g.gains[i : i + 1] for i in range(4))
    qgain, kgain = g.heads[0:1], g.heads[1:2]

    def keys_of(start, normed):
        raw = dot(normed, g.wkv[...])
        at = slice(start, start + 256)
        if start >= ROWS:
            g.kvraw[start - ROWS : start - ROWS + 256] = raw
        turned = turn(raw * rms(raw) * kgain, g.cos[at], g.sin[at])
        g.kvb[core, at] = jnp.where(core == 0, turned, raw).astype(LOW)

    for i in range(2):
        block = tok[256 * i : 256 * i + 256].astype(F32)
        normed = block * rms(block) * gain0
        g.n1[ROWS + 256 * i : ROWS + 256 * i + 256] = normed.astype(LOW)
        g.n1t[:, 256 * i : 256 * i + 256] = jnp.transpose(normed).astype(LOW)
        keys_of(ROWS + 256 * i, normed.astype(LOW))
    own_kv = g.kvb.at[core, pl.ds(ROWS, ROWS)]
    own_wire = other.copy(own_kv, own_kv, mate)
    tok_wire.wait_recv()
    for i in range(2):
        block = g.tokh[256 * i : 256 * i + 256].astype(F32)
        keys_of(256 * i, (block * rms(block) * gain0).astype(LOW))
    prior_kv = g.kvb.at[core, pl.ds(0, ROWS)]
    prior_wire = other.copy(prior_kv, prior_kv, mate)
    for i in range(2):
        raw = dot(g.n1[ROWS + 256 * i : ROWS + 256 * i + 256], g.wq[...])
        at = slice(ROWS + 256 * i, ROWS + 256 * i + 256)
        for h in range(2):
            part = raw[:, HD * h : HD * h + HD]
            turned = turn(part * rms(part) * qgain, g.cos[at], g.sin[at]).astype(LOW)
            for j in range(2):
                g.qraw[2 * i + j, 128 * h : 128 * h + 128] = part[128 * j : 128 * j + 128]
                g.q[2 * i + j, 128 * h : 128 * h + 128] = turned[128 * j : 128 * j + 128]
    step(p3, "three")
    own_wire.wait_recv()
    prior_wire.wait_recv()

    def twice(block, axis):
        return jnp.concatenate([block, block], axis=axis)

    def attend(b, carry):
        start = pl.multiple_of(b * 128, 128)
        keys, values = g.kvb[0, pl.ds(start, D)], g.kvb[1, pl.ds(start, D)]
        scores = dot(g.q[b], keys, NT) * SCALE
        lowest = twice(g.lo_col[pl.ds(start, 128), 0:1], 0) - (b * 128).astype(F32)
        place_k = iota((256, D), 1).astype(F32)
        highest = (iota((256, 1), 0) & 127).astype(F32) + float(WINDOW)
        scores = jnp.where((place_k >= lowest) & (place_k <= highest), scores, -1e30)
        expo = jnp.exp(scores - jnp.max(scores, axis=-1, keepdims=True))
        probs = (expo / jnp.sum(expo, axis=-1, keepdims=True)).astype(LOW)
        mixed = dot(probs, values).astype(LOW)
        g.o[pl.ds(start, 128), 0:HD] = mixed[:128]
        g.o[pl.ds(start, 128), HD : 2 * HD] = mixed[128:]
        return carry

    lax.fori_loop(0, 4, attend, 0)
    step(p2, "four")
    step(p1, "finish")
    assemble(g.wo, None, OUT, 256)

    halves = [slice(0, 256), slice(256, 512)]

    def swap(number, rows, value):
        g.snd[number, rows] = value.astype(LOW)
        return other.copy(g.snd.at[number, rows], g.rcv.at[number, rows], mate)

    def total(number, rows):
        return g.snd[number, rows].astype(F32) + g.rcv[number, rows].astype(F32)

    sent = [swap(0, rows, dot(g.o[rows], g.wo[...], NT)) for rows in halves]
    for i, rows in enumerate(halves):
        sent[i].wait_recv()
        branch = total(0, rows)
        g.a[rows] = branch
        hidden = tok[rows].astype(F32) + branch * rms(branch) * gain1
        g.h[rows] = hidden
        normed = hidden * rms(hidden) * gain2
        g.n2[rows] = normed.astype(LOW)
        g.n2t[:, rows] = jnp.transpose(normed).astype(LOW)
    for made in sent:
        made.wait_send()
    step(p3, "four")
    step(p2, "finish")
    assemble(g.wg, g.wu, GATEUP, FFH)

    c0, c1 = math.sqrt(2.0 / math.pi), 0.044715

    def forward_ff(i, carry):
        at = pl.multiple_of(i * 256, 256)
        cols = pl.ds(at, 256)
        for rows in halves:
            gate = dot(g.n2[rows], g.wg[:, cols])
            up = dot(g.n2[rows], g.wu[:, cols])
            square = gate * gate
            t = jnp.tanh(c0 * gate * (1.0 + c1 * square))
            act = 0.5 * gate * (1.0 + t)
            slope = 0.5 * (1.0 + t) + 0.5 * gate * (1.0 - t * t) * (c0 * (1.0 + 3.0 * c1 * square))
            g.ga[rows, cols] = act
            g.gb[rows, cols] = up * slope
            g.u[rows, cols] = (act * up).astype(LOW)
        return carry

    lax.fori_loop(0, 4, forward_ff, 0)
    step(p3, "finish")
    gather_wires.drain()
    assemble(g.wd, None, DOWN, 512)

    sent = [swap(1, rows, dot(g.u[rows], g.wd[...], NT)) for rows in halves]
    for i, rows in enumerate(halves):
        sent[i].wait_recv()
        feed = total(1, rows)
        out[rows] = (g.h[rows] + feed * rms(feed) * gain3).astype(LOW)
        back, slope = norm_back(feed, gain3, cot[rows].astype(F32))
        g.dgains[3:4] += slope
        g.gf[rows] = back.astype(LOW)
        g.gft[:, rows] = jnp.transpose(back).astype(LOW)
    for made in sent:
        made.wait_send()

    def cross(start):
        if start not in (KV, EXTRA):
            return None
        at = 0 if start == KV else 128
        return g.far.at[z, :, pl.ds(at, 128)], [
            {"ctx": place(z + k), "tensor": 1 - core} for k in range(4)
        ]

    parts, offsets = [], [0, 0]
    for piece in SCATTERS:
        made = []
        for i, ring in enumerate(rings):
            if piece[i] is not None:
                start, width = piece[i]
                made.append(
                    Scatter(
                        ring, scatter_wires, g.whole, bufs[i], g.final, z, start, width, offsets[i], cross(start)
                    )
                )
                offsets[i] += width
        parts.append(made)
    s0, s1, s2, s3, se = parts

    def put(left, right, start, begin, end, gap, w=256):
        def one(i, carry):
            at = pl.multiple_of(i * w, w)
            first = dot(left[...], right[:, pl.ds(at, w)]).reshape(16, 40, w)
            second = dot(left[...], right[:, pl.ds(at + gap, w)]).reshape(16, 40, w)
            block = jnp.concatenate([first, second], axis=1).astype(LOW)
            g.whole[:, :, :, pl.ds(start + at, w)] = block.reshape(4, 4, 80, w)
            return carry

        lax.fori_loop(begin // w, end // w, one, 0)

    put(g.gft, g.u, DOWN, 0, 512, 512)
    step(s3, "one")

    def backward_ff(i, carry):
        at = pl.multiple_of(i * 256, 256)
        cols = pl.ds(at, 256)
        for rows in halves:
            inner = dot(g.gf[rows], g.wd[:, cols])
            g.ggu[rows, cols] = (inner * g.gb[rows, cols]).astype(LOW)
            g.ggu[rows, pl.ds(at + FFH, 256)] = (inner * g.ga[rows, cols]).astype(LOW)
        return carry

    lax.fori_loop(0, 4, backward_ff, 0)
    step(s3, "two")
    sent = [
        swap(
            0,
            rows,
            dot(g.ggu[rows, 0:FFH], g.wg[...], NT) + dot(g.ggu[rows, FFH:], g.wu[...], NT),
        )
        for rows in halves
    ]

    put(g.n2t, g.ggu, GATEUP, 0, 512, FFH)
    step(s2[:1], "one")
    put(g.n2t, g.ggu, GATEUP, 512, 1024, FFH)
    step(s2[1:], "one")
    for i, rows in enumerate(halves):
        sent[i].wait_recv()
        back, slope = norm_back(g.h[rows], gain2, total(0, rows))
        g.dgains[2:3] += slope
        hidden = cot[rows].astype(F32) + back
        g.gh[rows] = hidden
        back, slope = norm_back(g.a[rows], gain1, hidden)
        g.dgains[1:2] += slope
        low = back.astype(LOW)
        g.gat[:, rows] = jnp.transpose(back).astype(LOW)
        grad = dot(low, g.wo[...]).astype(LOW)
        for j in range(2):
            for h in range(2):
                g.go[2 * i + j, 128 * h : 128 * h + 128] = grad[
                    128 * j : 128 * j + 128, HD * h : HD * h + HD
                ]
    for made in sent:
        made.wait_send()
    step(s3, "three")
    put(g.gat, g.o, OUT, 0, 256, 256)
    step(s1, "one")

    def attend_back(b, carry):
        start = pl.multiple_of(b * 128, 128)
        keys, values = g.kvb[0, pl.ds(start, D)], g.kvb[1, pl.ds(start, D)]
        queries, grad = g.q[b], g.go[b]
        scores = dot(keys, queries, NT) * SCALE
        lowest = twice(g.lo_row[0:1, pl.ds(start, 128)], 1) - (b * 128).astype(F32)
        place_k = iota((D, 256), 0).astype(F32)
        highest = (iota((1, 256), 1) & 127).astype(F32) + float(WINDOW)
        scores = jnp.where((place_k >= lowest) & (place_k <= highest), scores, -1e30)
        expo = jnp.exp(scores - jnp.max(scores, axis=0, keepdims=True))
        probs = expo * (1.0 / jnp.sum(expo, axis=0, keepdims=True))
        grad_probs = dot(values, grad, NT)
        spread = jnp.sum(probs * grad_probs, axis=0, keepdims=True)
        grad_scores = (probs * (grad_probs - spread)).astype(LOW)
        g.gkv[0, pl.ds(start, D)] += dot(grad_scores, queries) * SCALE
        g.gkv[1, pl.ds(start, D)] += dot(probs.astype(LOW), grad)
        grad_q = dot(grad_scores, keys, TN) * SCALE
        at = pl.ds(pl.multiple_of(ROWS + start, 128), 128)
        grad_q = turn_back(grad_q, twice(g.cos[at], 0), twice(g.sin[at], 0))
        back, slope = norm_back(g.qraw[b], qgain, grad_q)
        g.dheads[0:1] += slope
        g.gqr[pl.ds(start, 128), 0:HD] = back[:128].astype(LOW)
        g.gqr[pl.ds(start, 128), HD : 2 * HD] = back[128:].astype(LOW)
        return carry

    lax.fori_loop(0, 1, attend_back, 0)
    step(s2, "two")
    lax.fori_loop(1, 3, attend_back, 0)
    step(s3, "four")
    step(s1, "two")
    lax.fori_loop(3, 4, attend_back, 0)
    g.kvs[...] = g.gkv[1 - core].astype(LOW)
    kv_wire = other.copy(g.kvs, g.kvr, mate)
    step(s3, "five")
    put(g.n1t, g.gqr, QUERY, 0, 256, 256)
    kv_wire.wait_recv()
    g.hs[...] = added(g.gkv[core, 0:ROWS], g.kvr[0:ROWS]).astype(LOW)
    halo_wire = other.copy(g.hs, g.hr, {"ctx": place(z - 1)})
    step(s1, "three")
    halo_wire.wait_recv()
    for i, rows in enumerate(halves):
        after = slice(ROWS + 256 * i, ROWS + 256 * i + 256)
        grad = added(g.gkv[core, after], g.kvr[after], g.hr[rows])
        back, slope = norm_back(g.kvraw[rows], kgain, turn_back(grad, g.cos[after], g.sin[after]))
        g.dheads[1:2] += jnp.where(core == 0, slope, 0.0)
        low = jnp.where(core == 0, back, grad).astype(LOW)
        g.gkr[rows] = low
    put(g.n1t, g.gkr, KV, 0, 128, 128, w=128)
    step(s0, "one")
    sent = [
        swap(1, rows, dot(g.gqr[rows], g.wq[...], NT) + dot(g.gkr[rows], g.wkv[...], NT))
        for rows in halves
    ]
    step(s2, "three")
    step(s0, "two")
    step(s1, "four")
    for i, rows in enumerate(halves):
        sent[i].wait_recv()
        back, slope = norm_back(tok[rows].astype(F32), gain0, total(1, rows))
        g.dgains[0:1] += slope
        igrad[rows] = g.gh[rows] + back
    g.tall[...] = jnp.zeros((128, D), F32)
    g.tall[0:8] = g.dgains[...]
    first = jnp.transpose(g.tall[...]).reshape(16, 40, 128)
    g.tall[0:8] = dot(g.dheads[...].astype(LOW), pick, NT)
    second = jnp.transpose(g.tall[...]).reshape(16, 40, 128)
    block = jnp.concatenate([first, second], axis=1).astype(LOW)
    g.whole[:, :, :, EXTRA:OUT] = block.reshape(4, 4, 80, 128)
    step(se, "one")
    step(s2, "four")
    step(s0, "three")
    step(se, "two")
    step(s1, "five")
    step(s2, "five")
    step(s0, "four")
    step(se, "three")
    step(s0, "five")
    step(se, "four")

    def put_final(start, width, source=None):
        cols = pl.ds(start, width)
        return added(*((g.final if source is None else source)[i, :, cols] for i in range(4)))

    step(s3, "finish")
    grads[:, DOWN + 128 : WIRE + 128] = put_final(DOWN, 512)
    step(s1, "finish")
    grads[:, OUT + 128 : GATEUP + 128] = put_final(OUT, 256)
    step(se, "five")
    step(s2, "finish")
    grads[:, GATEUP + 128 : DOWN + 128] = put_final(GATEUP, 1024)
    step(s0, "finish")
    own, far = put_final(KV, 128), put_final(0, 128, g.far)
    grads[:, 0:128] = jnp.where(core == 0, own, far)
    grads[:, 128:256] = jnp.where(core == 0, far, own)
    grads[:, QUERY + 128 : EXTRA + 128] = put_final(QUERY, 256)
    step(se, "finish")
    own, far = put_final(EXTRA, 128), put_final(128, 128, g.far)
    grads[0:40, EXTRA + 128 : OUT + 128] = own[:40]
    grads[40:80, EXTRA + 128 : OUT + 128] = own[40:] + far[40:]
    scatter_wires.drain()
    for made in (tok_wire, seg_wire, own_wire, prior_wire, kv_wire, halo_wire, *sent):
        made.wait_send()


def hand_out(output, input_grad, done, out, igrad, query, keyval, wide, gateup, down, norms, heads, sems):
    copies = [
        pltpu.make_async_copy(output, out, sems.at[0]),
        pltpu.make_async_copy(input_grad, igrad, sems.at[1]),
    ]
    for made in copies:
        made.start()
    keyval[:, 0:256] = unfold(done[:, 0:128])
    keyval[:, 256:512] = unfold(done[:, 128:256])
    query[...] = unfold(done[:, 256:512])
    wide[...] = unfold(done[:, 640:896])
    gateup[0] = done[:40, 896:1920]
    gateup[1] = done[40:, 896:1920]
    down[...] = unfold(done[:, 1920:])
    square = jnp.concatenate([done[:, 512:640], jnp.zeros((48, 128), F32)], axis=0)
    turned = jnp.transpose(square)
    norms[...] = turned[:4, :40]
    heads[...] = turned[:2, 40:56]
    for made in copies:
        made.wait()


def vmem():
    return pl.BlockSpec(memory_space=pltpu.VMEM)


def ring_buffers():
    return [
        pltpu.VMEM((2, 2, 80, SET_COLS), LOW),
        pltpu.VMEM((2, 4, 80, SET_COLS), LOW),
        pltpu.VMEM((4, 80, SET_COLS), LOW),
        pltpu.VMEM((80, SET_COLS), LOW),
        pltpu.VMEM((2, 80, SET_COLS), LOW),
    ]


def shards(
    tokens, segments, cotangent, w_query, w_keyval, w_out, w_gateup, w_down, norm_gains, head_gains
):
    output, input_grad, done = pl.pallas_call(
        layer_kernel,
        out_shape=(
            jax.ShapeDtypeStruct((ROWS, D), LOW),
            jax.ShapeDtypeStruct((ROWS, D), F32),
            jax.ShapeDtypeStruct((80, WIRE + 128), F32),
        ),
        in_specs=[vmem()] * 10,
        out_specs=(vmem(),) * 3,
        scratch_shapes=[
            *(pltpu.VMEM(*shape) for shape in SCRATCH.values()),
            *ring_buffers(),
            *ring_buffers(),
            pltpu.SemaphoreType.DMA((64,)),
            pltpu.SemaphoreType.DMA((64,)),
            pltpu.SemaphoreType.DMA((112,)),
            pltpu.SemaphoreType.DMA((112,)),
            pltpu.SemaphoreType.DMA((16,)),
            pltpu.SemaphoreType.DMA((16,)),
        ],
        compiler_params=pltpu.CompilerParams(
            collective_id=0, has_side_effects=True, vmem_limit_bytes=VMEM_BYTES
        ),
    )(
        tokens[0],
        segments,
        cotangent[0],
        w_query,
        w_keyval,
        w_out.T,
        w_gateup,
        w_down.T,
        norm_gains,
        head_gains,
    )
    whole = pl.BlockSpec(memory_space=pl.ANY)
    results = pl.pallas_call(
        hand_out,
        out_shape=(
            jax.ShapeDtypeStruct((ROWS, D), LOW),
            jax.ShapeDtypeStruct((ROWS, D), F32),
            jax.ShapeDtypeStruct((40, 512), F32),
            jax.ShapeDtypeStruct((40, 512), F32),
            jax.ShapeDtypeStruct((40, 512), F32),
            jax.ShapeDtypeStruct((2, 40, FFH), F32),
            jax.ShapeDtypeStruct((40, FFH), F32),
            jax.ShapeDtypeStruct((4, 40), F32),
            jax.ShapeDtypeStruct((2, 16), F32),
        ),
        in_specs=[whole, whole, vmem()],
        out_specs=(whole, whole) + (vmem(),) * 7,
        scratch_shapes=[pltpu.SemaphoreType.DMA((2,))],
        compiler_params=pltpu.CompilerParams(vmem_limit_bytes=16 * 1024 * 1024),
    )(output, input_grad, done)
    return (
        results[0][None],
        results[1][None],
        results[2],
        results[3],
        results[4].T,
        results[5],
        results[6].T,
        results[7],
        results[8],
    )


def solution(mesh):
    placed = (
        P("dp", "ctx", None),
        P("dp", "ctx"),
        P("dp", "ctx", None),
        P("dp", "tensor"),
        P("dp", None),
        P("tensor", "dp"),
        P(None, "dp", "tensor"),
        P("tensor", "dp"),
        P(None, "dp"),
        P(None, "dp"),
    )
    return jax.shard_map(
        shards,
        mesh=mesh,
        in_specs=placed,
        out_specs=(
            P("dp", "ctx", None),
            P("dp", "ctx", None),
            P("dp", "tensor"),
            P("dp", None),
            P("tensor", "dp"),
            P(None, "dp", "tensor"),
            P("tensor", "dp"),
            P(None, "dp"),
            P(None, "dp"),
        ),
        check_vma=False,
    )
```

```python
import math
import types

import jax
import jax.numpy as jnp
from jax import lax
from jax.experimental import pallas as pl
from jax.experimental.pallas import tpu as pltpu
from jax.sharding import PartitionSpec as P

WINDOW = 512
EPSILON = 1e-06
MESH = pl.DeviceIdType.MESH
VMEM_BYTES = 60 * 1024 * 1024

KV, QUERY, EXTRA, OUT, GATEUP, DOWN, WIRE = 0, 128, 384, 512, 768, 1792, 2304
GATHERS = (
    ((0, 256), (256, 256)),
    ((512, 128), (640, 128)),
    ((768, 512), (1280, 512)),
    ((1792, 256), (2048, 256)),
)
SCATTERS = (
    ("s3", (1792, 256), (2048, 256)),
    ("sa", (768, 256), (1024, 256)),
    ("sb", (1280, 256), (1536, 256)),
    ("s1", (512, 128), (640, 128)),
    ("s0", (0, 256), (256, 128)),
)
SET_COLS = (1152, 1024)
CUT = 48
ROWS, D, HD, FFH = 512, 640, 256, 1024
SCALE = 1.0 / math.sqrt(HD)
LOW = jnp.bfloat16
F32 = jnp.float32
NN, NT, TN = ((1,), (0,)), ((1,), (1,)), ((0,), (0,))


def place(u):
    return lax.rem(u + 8, 4)


class Wires:
    def __init__(self, send, recv):
        self.send, self.recv, self.used = send, recv, 0
        self.started = []

    def copy(self, src, dst, target):
        index = self.used
        self.used += 1
        made = pltpu.make_async_remote_copy(
            src_ref=src,
            dst_ref=dst,
            send_sem=self.send.at[index],
            recv_sem=self.recv.at[index],
            device_id=target,
            device_id_type=MESH,
        )
        made.start()
        self.started.append(made)
        return made

    def drain(self):
        for made in self.started:
            made.wait_send()
        self.started = []


class Ring:
    def __init__(self, first, x, y):
        self.first = first
        self.f, self.s = (x, y) if first == "x" else (y, x)

    def slot(self, ref, f, s, *rest):
        return ref.at[(s, f) + rest] if self.first == "x" else ref.at[(f, s) + rest]

    def index(self, f, s):
        return (s, f) if self.first == "x" else (f, s)

    def to_f(self, step):
        f = place(self.f + step)
        return {"dp": self.s * 4 + f} if self.first == "x" else {"dp": f * 4 + self.s}

    def to_s(self, step):
        s = place(self.s + step)
        return {"dp": s * 4 + self.f} if self.first == "x" else {"dp": self.f * 4 + s}


class Gather:
    def __init__(self, ring, wires, shard, whole, direct, start, width):
        self.ring, self.wires, self.shard, self.whole = ring, wires, shard, whole
        self.direct = direct
        self.cols = pl.ds(start, width)

    def one(self):
        r, c = self.ring, self.cols
        src = self.shard.at[:, c]
        dst = r.slot(self.whole, r.f, r.s, slice(None), c)
        self.a = self.wires.copy(src, dst, r.to_f(1))
        self.b = self.wires.copy(src, dst, r.to_f(-1))
        if self.direct:
            self.c = self.wires.copy(src, dst, r.to_f(2))

    def two(self):
        r, c = self.ring, self.cols
        self.a.wait_recv()
        part = r.slot(self.whole, place(r.f - 1), r.s, pl.ds(0, CUT), c)
        a = self.wires.copy(part, part, r.to_f(1))
        self.b.wait_recv()
        part = r.slot(self.whole, place(r.f + 1), r.s, pl.ds(CUT, 80 - CUT), c)
        b = self.wires.copy(part, part, r.to_f(-1))
        self.a, self.b = a, b

    def three(self):
        r, c = self.ring, self.cols
        self.a.wait_recv()
        self.b.wait_recv()
        if self.direct:
            self.c.wait_recv()
        part = r.slot(self.whole, slice(None), r.s, slice(None), c)
        self.a = self.wires.copy(part, part, r.to_s(1))
        self.b = self.wires.copy(part, part, r.to_s(-1))

    def four(self):
        r, c = self.ring, self.cols
        self.a.wait_recv()
        part = r.slot(self.whole, pl.ds(0, 2), place(r.s - 1), slice(None), c)
        a = self.wires.copy(part, part, r.to_s(1))
        self.b.wait_recv()
        part = r.slot(self.whole, pl.ds(2, 2), place(r.s + 1), slice(None), c)
        b = self.wires.copy(part, part, r.to_s(-1))
        self.a, self.b = a, b

    def finish(self):
        self.a.wait_recv()
        self.b.wait_recv()


def added(*terms):
    total = terms[0].astype(jnp.float32)
    for term in terms[1:]:
        total = total + term.astype(jnp.float32)
    return total


class Scatter:
    def __init__(self, ring, wires, grads, bufs, final, z, start, width, offset, far):
        self.ring, self.wires, self.grads, self.final, self.z = ring, wires, grads, final, z
        self.r1, self.r2, self.sums, self.r3, self.r4 = bufs
        self.cols = pl.ds(start, width)
        self.near = pl.ds(offset, width)
        self.far, self.start = far, start

    def one(self):
        r, c, n = self.ring, self.cols, self.near
        far = place(r.s + 2)
        self.a = self.wires.copy(
            r.slot(self.grads, pl.ds(0, 2), far, slice(None), c), self.r1.at[0, :, :, n], r.to_s(1)
        )
        self.b = self.wires.copy(
            r.slot(self.grads, pl.ds(2, 2), far, slice(None), c), self.r1.at[1, :, :, n], r.to_s(-1)
        )

    def two(self):
        r, c, n = self.ring, self.cols, self.near
        after, before = place(r.s + 1), place(r.s - 1)
        self.a.wait_recv()
        for i in range(2):
            at = r.index(i, after) + (slice(None), c)
            self.grads[at] = added(self.grads[at], self.r1[0, i, :, n]).astype(jnp.bfloat16)
        a = self.wires.copy(
            r.slot(self.grads, slice(None), after, slice(None), c), self.r2.at[0, :, :, n], r.to_s(1)
        )
        self.b.wait_recv()
        for i in range(2):
            at = r.index(2 + i, before) + (slice(None), c)
            self.grads[at] = added(self.grads[at], self.r1[1, i, :, n]).astype(jnp.bfloat16)
        b = self.wires.copy(
            r.slot(self.grads, slice(None), before, slice(None), c),
            self.r2.at[1, :, :, n],
            r.to_s(-1),
        )
        self.a, self.b = a, b

    def three(self):
        r, c, n = self.ring, self.cols, self.near
        self.a.wait_recv()
        self.b.wait_recv()
        for i in range(4):
            at = r.index(i, r.s) + (slice(None), c)
            self.sums[i, :, n] = added(
                self.grads[at], self.r2[0, i, :, n], self.r2[1, i, :, n]
            ).astype(jnp.bfloat16)
        far = place(r.f + 2)
        self.a = self.wires.copy(
            self.sums.at[far, pl.ds(0, CUT), n], self.r3.at[pl.ds(0, CUT), n], r.to_f(1)
        )
        self.b = self.wires.copy(
            self.sums.at[far, pl.ds(CUT, 80 - CUT), n],
            self.r3.at[pl.ds(CUT, 80 - CUT), n],
            r.to_f(-1),
        )

    def four(self):
        r, n = self.ring, self.near
        after, before = place(r.f + 1), place(r.f - 1)
        top, low = pl.ds(0, CUT), pl.ds(CUT, 80 - CUT)
        self.a.wait_recv()
        self.sums[after, top, n] = added(self.sums[after, top, n], self.r3[top, n]).astype(
            jnp.bfloat16
        )
        a = self.wires.copy(self.sums.at[after, :, n], self.r4.at[0, :, n], r.to_f(1))
        self.b.wait_recv()
        self.sums[before, low, n] = added(self.sums[before, low, n], self.r3[low, n]).astype(
            jnp.bfloat16
        )
        b = self.wires.copy(self.sums.at[before, :, n], self.r4.at[1, :, n], r.to_f(-1))
        self.a, self.b = a, b

    def five(self):
        r, c, n = self.ring, self.cols, self.near
        self.a.wait_recv()
        self.b.wait_recv()
        self.final[self.z, :, c] = added(
            self.sums[r.f, :, n], self.r4[0, :, n], self.r4[1, :, n]
        ).astype(jnp.bfloat16)
        part = self.final.at[self.z, :, c]
        self.zs = [self.wires.copy(part, part, {"ctx": place(self.z + k)}) for k in (1, 3, 2)]
        if self.far is not None:
            part = self.final.at[self.z, :, pl.ds(self.start, 128)]
            self.zs += [self.wires.copy(part, self.far[0], target) for target in self.far[1]]

    def finish(self):
        for made in self.zs:
            made.wait_recv()


def spot():
    d = lax.axis_index("dp")
    return lax.rem(d, 4), lax.div(d, 4), lax.axis_index("ctx")


def dot(a, b, dims=NN):
    return lax.dot_general(a, b, (dims, ((), ())), preferred_element_type=F32)


def rms(field):
    return lax.rsqrt(jnp.mean(field * field, axis=-1, keepdims=True) + EPSILON)


def norm_back(field, gain, grad):
    r = rms(field)
    hat = field * r
    scaled = grad * gain
    back = r * (scaled - hat * jnp.mean(scaled * hat, axis=-1, keepdims=True))
    return back, jnp.sum(grad * hat, axis=0, keepdims=True)


def turn(field, cos, sin):
    a, b = field[:, :128], field[:, 128:]
    return jnp.concatenate([a * cos - b * sin, b * cos + a * sin], axis=1)


def turn_back(field, cos, sin):
    a, b = field[:, :128], field[:, 128:]
    return jnp.concatenate([a * cos + b * sin, b * cos - a * sin], axis=1)


def fold(block):
    half = block.shape[-1] // 2
    return jnp.concatenate([block[..., :half], block[..., half:]], axis=-2)


def unfold(block):
    rows = block.shape[-2] // 2
    return jnp.concatenate([block[..., :rows, :], block[..., rows:, :]], axis=-1)


def iota(shape, axis):
    return lax.broadcasted_iota(jnp.int32, shape, axis)


SCRATCH = dict(
    wire=((80, WIRE), LOW),
    whole=((4, 4, 80, WIRE), LOW),
    tall=((128, 256), F32),
    wq=((D, 512), LOW),
    wkv=((D, HD), LOW),
    wo=((D, 512), LOW),
    wg=((D, FFH), LOW),
    wu=((D, FFH), LOW),
    wd=((D, FFH), LOW),
    gains=((8, D), F32),
    heads=((8, HD), F32),
    dgains=((8, D), F32),
    ends=((16, 16, 128), F32),
    end_snd=((4, 4, 16, 128), LOW),
    end_rcv=((4, 4, 16, 128), LOW),
    end_mid=((4, 16, 128), LOW),
    end_mrc=((4, 16, 128), LOW),
    end_z=((4, 16, 128), LOW),
    end_far=((4, 16, 128), LOW),
    dheads=((8, HD), F32),
    tokh=((ROWS, D), LOW),
    segp=((1, ROWS), jnp.int32),
    lo_col=((ROWS, 128), F32),
    lo_row=((8, ROWS), F32),
    cos=((1024, 128), F32),
    sin=((1024, 128), F32),
    n1=((1024, D), LOW),
    n1t=((D, 1024), LOW),
    kvb=((2, 1024, HD), LOW),
    kvraw=((1024, HD), F32),
    qraw=((4, 256, HD), F32),
    q=((4, 256, HD), LOW),
    o=((ROWS, 512), LOW),
    go=((4, 256, HD), LOW),
    gqr=((ROWS, 512), LOW),
    a=((ROWS, D), F32),
    h=((ROWS, D), F32),
    n2=((ROWS, D), LOW),
    n2t=((D, ROWS), LOW),
    ga=((ROWS, FFH), F32),
    gb=((ROWS, FFH), F32),
    u=((ROWS, FFH), LOW),
    ggu=((ROWS, 2 * FFH), LOW),
    gf=((ROWS, D), LOW),
    gft=((D, ROWS), LOW),
    gal=((ROWS, D), LOW),
    gat=((D, ROWS), LOW),
    gh=((ROWS, D), F32),
    snd=((2, ROWS, D), LOW),
    rcv=((2, ROWS, D), LOW),
    gkv=((2, 1024, HD), F32),
    kvs=((1024, HD), LOW),
    kvr=((1024, HD), LOW),
    hs=((ROWS, HD), LOW),
    hr=((ROWS, HD), LOW),
    gkr=((1024, HD), LOW),
    gko=((ROWS, HD), LOW),
    final=((4, 80, WIRE), LOW),
    far=((4, 80, 128), LOW),
)


ORDER = (
    "w0", "w1", "p1.one", "p0.one", "w2", "p2.one", "tab", "w3", "p1.two", "p3.one", "p0.three",
    "p2.two", "p1.three", "p3.two", "p0.four", "p2.three", "p1.four", "p3.three", "c0", "c1",
    "mask", "c2", "A0", "A1", "p2.four", "c3", "A2", "A3", "h0", "c4", "p3.four", "h1", "c6",
    "F0", "c8", "F1", "c9", "o0", "FB0", "G0", "o1", "FB1", "PA", "sa.one", "G1", "PB",
    "sb.one", "N0", "B0", "sa.two", "P3", "s3.one", "sb.two", "N1", "P1", "s1.one", "B1",
    "sa.three", "s3.two", "B2", "B3", "sb.three", "sa.four", "PQ", "V0", "V1", "KB", "s0.one",
    "sb.four", "s1.two", "s3.three", "QS", "NN0", "s0.two", "sb.five", "NN1", "sa.five",
    "s1.three", "s3.four", "I0", "I1", "EX", "se.one", "s0.three", "sb.fin", "s1.four",
    "s3.five", "se.two", "s0.four", "sa.fin", "s1.five", "se.five", "s0.five", "s3.fin",
    "s1.fin", "se.fin", "s0.fin",
)


def layer_kernel(tok, seg_row, cot, wq, wkv, wo, wgu, wd, ng, hg, out, igrad, grads, ends, *rest):
    names = list(SCRATCH)
    g = types.SimpleNamespace(**dict(zip(names, rest[: len(names)])))
    rest = rest[len(names) :]
    bufs = (rest[0:5], rest[5:10])
    x, y, z = spot()
    core = lax.axis_index("tensor")
    mate = {"tensor": 1 - core}
    rings = (Ring("x", x, y), Ring("y", x, y))
    gather_wires = Wires(rest[10], rest[11])
    scatter_wires = Wires(rest[12], rest[13])
    other = Wires(rest[14], rest[15])
    along_z = [{"ctx": place(z + k)} for k in (1, 3, 2)]
    across = [{"ctx": place(z + k), "tensor": 1 - core} for k in range(4)]
    targets = [r.to_f(k) for r in rings for k in (1, -1, 2)] + along_z + across
    barrier = pltpu.get_barrier_semaphore()
    for target in targets:
        pl.semaphore_signal(barrier, inc=1, device_id=target, device_id_type=MESH)

    jobs, held = {}, {}

    def job(name):
        def keep(work):
            jobs[name] = work
            return work

        return keep

    def steps(name, members, methods):
        for method in methods:
            jobs[name + "." + method] = lambda method=method: [getattr(m, method)() for m in members]

    for number, piece in enumerate(GATHERS):
        steps(
            "p%d" % number,
            [
                Gather(ring, gather_wires, g.wire, g.whole, number == 0, *piece[i])
                for i, ring in enumerate(rings)
            ],
            ("one", "two", "three", "four", "finish"),
        )
    offsets = [0, 0]
    for name, *piece in SCATTERS:
        made = []
        for i, ring in enumerate(rings):
            start, width = piece[i]
            far = (g.far.at[z], across) if start == KV else None
            made.append(
                Scatter(ring, scatter_wires, g.whole, bufs[i], g.final, z, start, width, offsets[i], far)
            )
            offsets[i] += width
        steps(name, made, ("one", "two", "three", "four", "five", "finish"))

    halves = [slice(0, 256), slice(256, 512)]

    def swap(name, number, rows, value):
        g.snd[number, rows] = value.astype(LOW)
        held[name] = other.copy(g.snd.at[number, rows], g.rcv.at[number, rows], mate)

    def total(name, number, rows):
        held[name].wait_recv()
        held[name].wait_send()
        return g.snd[number, rows].astype(F32) + g.rcv[number, rows].astype(F32)

    @job("w0")
    def _():
        g.tall[...] = jnp.zeros((128, 256), F32)
        mine = wkv[:, pl.ds(pl.multiple_of(core * HD, HD), HD)]
        g.wire[:, KV:QUERY] = fold(mine.astype(F32)).astype(LOW)
        g.wire[:, QUERY:EXTRA] = fold(wq[...].astype(F32)).astype(LOW)
        g.tall[0:4, 0:40] = ng[...].astype(F32)
        g.tall[0:2, 128:144] = hg[...].astype(F32)
        first = jnp.transpose(g.tall[:, 0:128])[:40]
        second = jnp.transpose(g.tall[:, 128:256])[:40]
        g.wire[:, EXTRA:OUT] = jnp.concatenate([first, second], axis=0).astype(LOW)
        g.whole[y, x, :, KV:OUT] = g.wire[:, KV:OUT]
        pl.semaphore_wait(barrier, len(targets))

    @job("w1")
    def _():
        held["seg"] = other.copy(seg_row, g.segp, {"ctx": place(z + 1)})
        held["tok"] = other.copy(tok, g.tokh, {"ctx": place(z + 1)})
        g.wire[:, OUT:GATEUP] = fold(wo[...].astype(F32)).astype(LOW)
        g.whole[y, x, :, OUT:GATEUP] = g.wire[:, OUT:GATEUP]

    @job("w2")
    def _():
        both = jnp.concatenate([wgu[0].astype(F32), wgu[1].astype(F32)], axis=0)
        g.wire[:, GATEUP:DOWN] = both.astype(LOW)
        g.whole[y, x, :, GATEUP:DOWN] = g.wire[:, GATEUP:DOWN]

    @job("w3")
    def _():
        g.wire[:, DOWN:WIRE] = fold(wd[...].astype(F32)).astype(LOW)
        g.whole[y, x, :, DOWN:WIRE] = g.wire[:, DOWN:WIRE]

    @job("tab")
    def _():
        rates = jnp.exp(iota((1, 128), 1).astype(F32) * (-2.0 * math.log(10000.0) / HD))
        fine = iota((128, 128), 0).astype(F32) * rates
        fine_cos, fine_sin = jnp.cos(fine), jnp.sin(fine)
        coarse = (iota((8, 128), 0) * 128 + (z * ROWS - ROWS)).astype(F32) * rates
        coarse_cos, coarse_sin = jnp.cos(coarse), jnp.sin(coarse)
        for i in range(8):
            cc, cs = coarse_cos[i : i + 1], coarse_sin[i : i + 1]
            g.cos[128 * i : 128 * i + 128] = fine_cos * cc - fine_sin * cs
            g.sin[128 * i : 128 * i + 128] = fine_sin * cc + fine_cos * cs
        g.dgains[...] = jnp.zeros((8, D), F32)
        g.dheads[...] = jnp.zeros((8, HD), F32)
        g.gkv[...] = jnp.zeros((2, 1024, HD), F32)
        g.ends[...] = jnp.zeros((16, 16, 128), F32)

    @job("mask")
    def _():
        held["seg"].wait_recv()
        own_ids, prior_ids = seg_row[...].astype(F32), g.segp[...].astype(F32)
        column = jnp.transpose(jnp.broadcast_to(own_ids, (128, ROWS)))[:, 0:1]
        below_prior = jnp.sum((prior_ids < column).astype(F32), axis=1, keepdims=True)
        below_prior = jnp.where(z == 0, float(ROWS), below_prior)
        below_own = jnp.sum((own_ids < column).astype(F32), axis=1, keepdims=True)
        lowest = jnp.maximum(below_prior + below_own, iota((ROWS, 1), 0).astype(F32) + 1.0)
        lowest = jnp.broadcast_to(lowest, (ROWS, 128))
        g.lo_col[...] = lowest
        g.lo_row[...] = jnp.transpose(lowest)[0:8]

    def assemble(first, second, start, width, w=128):
        def one(i, carry):
            at = pl.multiple_of(i * w, w)
            block = g.whole[:, :, :, pl.ds(start + at, w)].astype(F32)
            first[:, pl.ds(at, w)] = block[:, :, :40].reshape(D, w).astype(LOW)
            if second is None:
                first[:, pl.ds(at + width, w)] = block[:, :, 40:].reshape(D, w).astype(LOW)
            else:
                second[:, pl.ds(at, w)] = block[:, :, 40:].reshape(D, w).astype(LOW)
            return carry

        lax.fori_loop(0, width // w, one, 0)

    def gain(i):
        return g.gains[i : i + 1]

    def keys_of(start, normed):
        at = slice(start, start + 256)
        low = normed.astype(LOW)
        g.n1[at] = low
        raw = dot(low, g.wkv[...])
        g.kvraw[at] = raw
        turned = turn(raw * rms(raw) * g.heads[1:2], g.cos[at], g.sin[at])
        g.kvb[core, at] = jnp.where(core == 0, turned, raw).astype(LOW)
        g.n1t[:, at] = jnp.transpose(normed).astype(LOW)

    @job("c0")
    def _():
        jobs["p0.finish"]()
        block = g.whole[:, :, :, EXTRA:OUT].astype(F32)
        g.gains[...] = jnp.transpose(block[:, :, :40].reshape(D, 128))[:8]
        spread = jnp.transpose(block[:, :, 40:].reshape(D, 128))[:8]
        column_at, head_at = iota((D, HD), 0), iota((D, HD), 1)
        pick = (column_at == 40 * (head_at >> 4) + (head_at & 15)).astype(F32).astype(LOW)
        g.heads[...] = dot(spread.astype(LOW), pick)
        assemble(g.wkv, None, KV, 128)
        for rows in halves:
            block = tok[rows].astype(F32)
            keys_of(ROWS + rows.start, block * rms(block) * gain(0))
        part = g.kvb.at[core, pl.ds(ROWS, ROWS)]
        held["kv1"] = other.copy(part, part, mate)

    @job("c1")
    def _():
        held["tok"].wait_recv()
        for rows in halves:
            block = g.tokh[rows].astype(F32)
            keys_of(rows.start, block * rms(block) * gain(0))
        part = g.kvb.at[core, pl.ds(0, ROWS)]
        held["kv2"] = other.copy(part, part, mate)

    @job("c2")
    def _():
        assemble(g.wq, None, QUERY, 256)
        for i in range(2):
            at = slice(ROWS + 256 * i, ROWS + 256 * i + 256)
            raw = dot(g.n1[at], g.wq[...])
            for h in range(2):
                part = raw[:, HD * h : HD * h + HD]
                turned = turn(part * rms(part) * g.heads[0:1], g.cos[at], g.sin[at]).astype(LOW)
                for j in range(2):
                    g.qraw[2 * i + j, 128 * h : 128 * h + 128] = part[128 * j : 128 * j + 128]
                    g.q[2 * i + j, 128 * h : 128 * h + 128] = turned[128 * j : 128 * j + 128]

    def twice(block, axis):
        return jnp.concatenate([block, block], axis=axis)

    def attend(b, carry):
        start = pl.multiple_of(b * 128, 128)
        keys, values = g.kvb[0, pl.ds(start, D)], g.kvb[1, pl.ds(start, D)]
        scores = dot(g.q[b], keys, NT) * SCALE
        lowest = twice(g.lo_col[pl.ds(start, 128), 0:1], 0) - (b * 128).astype(F32)
        place_k = iota((256, D), 1).astype(F32)
        highest = (iota((256, 1), 0) & 127).astype(F32) + float(WINDOW)
        scores = jnp.where((place_k >= lowest) & (place_k <= highest), scores, -1e30)
        expo = jnp.exp(scores - jnp.max(scores, axis=-1, keepdims=True))
        probs = (expo / jnp.sum(expo, axis=-1, keepdims=True)).astype(LOW)
        mixed = dot(probs, values).astype(LOW)
        g.o[pl.ds(start, 128), 0:HD] = mixed[:128]
        g.o[pl.ds(start, 128), HD : 2 * HD] = mixed[128:]
        return carry

    @job("A0")
    def _():
        held["kv1"].wait_recv()
        held["kv2"].wait_recv()
        lax.fori_loop(0, 1, attend, 0)

    for b in (1, 2, 3):
        jobs["A%d" % b] = lambda b=b: lax.fori_loop(b, b + 1, attend, 0)

    @job("c3")
    def _():
        jobs["p1.finish"]()
        assemble(g.wo, None, OUT, 256)
        swap("a0", 0, halves[0], dot(g.o[halves[0]], g.wo[...], NT))

    @job("c4")
    def _():
        swap("a1", 0, halves[1], dot(g.o[halves[1]], g.wo[...], NT))

    def hidden_rows(i):
        rows = halves[i]
        branch = total("a%d" % i, 0, rows)
        g.a[rows] = branch
        hidden = tok[rows].astype(F32) + branch * rms(branch) * gain(1)
        g.h[rows] = hidden
        normed = hidden * rms(hidden) * gain(2)
        g.n2[rows] = normed.astype(LOW)
        g.n2t[:, rows] = jnp.transpose(normed).astype(LOW)

    c0, c1 = math.sqrt(2.0 / math.pi), 0.044715

    def forward_rows(k):
        rows = halves[k]

        def one(i, carry):
            cols = pl.ds(pl.multiple_of(i * 256, 256), 256)
            gate = dot(g.n2[rows], g.wg[:, cols])
            up = dot(g.n2[rows], g.wu[:, cols])
            square = gate * gate
            t = jnp.tanh(c0 * gate * (1.0 + c1 * square))
            act = 0.5 * gate * (1.0 + t)
            slope = 0.5 * (1.0 + t) + 0.5 * gate * (1.0 - t * t) * (c0 * (1.0 + 3.0 * c1 * square))
            g.ga[rows, cols] = act
            g.gb[rows, cols] = up * slope
            g.u[rows, cols] = (act * up).astype(LOW)
            return carry

        lax.fori_loop(0, 4, one, 0)

    @job("c6")
    def _():
        jobs["p2.finish"]()
        assemble(g.wg, g.wu, GATEUP, FFH)

    @job("c8")
    def _():
        jobs["p3.finish"]()
        gather_wires.drain()
        assemble(g.wd, None, DOWN, 512)
        swap("f0", 1, halves[0], dot(g.u[halves[0]], g.wd[...], NT))

    @job("c9")
    def _():
        swap("f1", 1, halves[1], dot(g.u[halves[1]], g.wd[...], NT))

    def output_rows(i):
        rows = halves[i]
        feed = total("f%d" % i, 1, rows)
        out[rows] = (g.h[rows] + feed * rms(feed) * gain(3)).astype(LOW)
        back, slope = norm_back(feed, gain(3), cot[rows].astype(F32))
        g.dgains[3:4] += slope
        g.gf[rows] = back.astype(LOW)
        g.gft[:, rows] = jnp.transpose(back).astype(LOW)

    def put(left, right, start, begin, end, gap, w=256):
        def one(i, carry):
            at = pl.multiple_of(i * w, w)
            first = dot(left[...], right[:, pl.ds(at, w)]).reshape(16, 40, w)
            second = dot(left[...], right[:, pl.ds(at + gap, w)]).reshape(16, 40, w)
            block = jnp.concatenate([first, second], axis=1).astype(LOW)
            g.whole[:, :, :, pl.ds(start + at, w)] = block.reshape(4, 4, 80, w)
            return carry

        lax.fori_loop(begin // w, end // w, one, 0)

    jobs["P3"] = lambda: put(g.gft, g.u, DOWN, 0, 512, 512)
    jobs["PA"] = lambda: put(g.n2t, g.ggu, GATEUP, 0, 512, FFH)
    jobs["PB"] = lambda: put(g.n2t, g.ggu, GATEUP, 512, 1024, FFH)
    jobs["P1"] = lambda: put(g.gat, g.o, OUT, 0, 256, 256)
    jobs["PQ"] = lambda: put(g.n1t.at[:, ROWS:], g.gqr, QUERY, 0, 256, 256)

    def backward_rows(k):
        rows = halves[k]

        def one(i, carry):
            at = pl.multiple_of(i * 256, 256)
            cols = pl.ds(at, 256)
            inner = dot(g.gf[rows], g.wd[:, cols])
            g.ggu[rows, cols] = (inner * g.gb[rows, cols]).astype(LOW)
            g.ggu[rows, pl.ds(at + FFH, 256)] = (inner * g.ga[rows, cols]).astype(LOW)
            return carry

        lax.fori_loop(0, 4, one, 0)

    def second_rows(i):
        rows = halves[i]
        part = dot(g.ggu[rows, 0:FFH], g.wg[...], NT) + dot(g.ggu[rows, FFH:], g.wu[...], NT)
        swap("g%d" % i, 0, rows, part)

    def norm_rows(i):
        rows = halves[i]
        back, slope = norm_back(g.h[rows], gain(2), total("g%d" % i, 0, rows))
        g.dgains[2:3] += slope
        hidden = cot[rows].astype(F32) + back
        g.gh[rows] = hidden
        back, slope = norm_back(g.a[rows], gain(1), hidden)
        g.dgains[1:2] += slope
        g.gat[:, rows] = jnp.transpose(back).astype(LOW)
        grad = dot(back.astype(LOW), g.wo[...]).astype(LOW)
        for j in range(2):
            for h in range(2):
                g.go[2 * i + j, 128 * h : 128 * h + 128] = grad[
                    128 * j : 128 * j + 128, HD * h : HD * h + HD
                ]

    for i in range(2):
        jobs["h%d" % i] = lambda i=i: hidden_rows(i)
        jobs["F%d" % i] = lambda i=i: forward_rows(i)
        jobs["o%d" % i] = lambda i=i: output_rows(i)
        jobs["FB%d" % i] = lambda i=i: backward_rows(i)
        jobs["G%d" % i] = lambda i=i: second_rows(i)
        jobs["N%d" % i] = lambda i=i: norm_rows(i)

    def attend_back(b, carry):
        start = pl.multiple_of(b * 128, 128)
        keys, values = g.kvb[0, pl.ds(start, D)], g.kvb[1, pl.ds(start, D)]
        queries, grad = g.q[b], g.go[b]
        scores = dot(keys, queries, NT) * SCALE
        lowest = twice(g.lo_row[0:1, pl.ds(start, 128)], 1) - (b * 128).astype(F32)
        place_k = iota((D, 256), 0).astype(F32)
        highest = (iota((1, 256), 1) & 127).astype(F32) + float(WINDOW)
        scores = jnp.where((place_k >= lowest) & (place_k <= highest), scores, -1e30)
        expo = jnp.exp(scores - jnp.max(scores, axis=0, keepdims=True))
        probs = expo * (1.0 / jnp.sum(expo, axis=0, keepdims=True))
        grad_probs = dot(values, grad, NT)
        spread = jnp.sum(probs * grad_probs, axis=0, keepdims=True)
        grad_scores = (probs * (grad_probs - spread)).astype(LOW)
        g.gkv[0, pl.ds(start, D)] += dot(grad_scores, queries) * SCALE
        g.gkv[1, pl.ds(start, D)] += dot(probs.astype(LOW), grad)
        grad_q = dot(grad_scores, keys, TN) * SCALE
        at = pl.ds(pl.multiple_of(ROWS + start, 128), 128)
        grad_q = turn_back(grad_q, twice(g.cos[at], 0), twice(g.sin[at], 0))
        back, slope = norm_back(g.qraw[b], g.heads[0:1], grad_q)
        g.dheads[0:1] += slope
        g.gqr[pl.ds(start, 128), 0:HD] = back[:128].astype(LOW)
        g.gqr[pl.ds(start, 128), HD : 2 * HD] = back[128:].astype(LOW)
        return carry

    def back_block(b):
        lax.fori_loop(b, b + 1, attend_back, 0)
        if b in (1, 3):
            rows = pl.ds(0, 256) if b == 1 else pl.ds(256, 768)
            g.kvs[rows] = g.gkv[1 - core, rows].astype(LOW)
            held["kvx%d" % (b // 2)] = other.copy(g.kvs.at[rows], g.kvr.at[rows], mate)

    for b in range(4):
        jobs["B%d" % b] = lambda b=b: back_block(b)

    def summed_rows(i):
        rows = slice(0, 256) if i == 0 else slice(256, 1024)
        held["kvx%d" % i].wait_recv()
        g.gkv[core, rows] = added(g.gkv[core, rows], g.kvr[rows])
        g.hs[halves[i]] = g.gkv[core, halves[i]].astype(LOW)
        held["ha%d" % i] = other.copy(
            g.hs.at[halves[i]], g.hr.at[halves[i]], {"ctx": place(z - 1)}
        )

    def keys_back(start, grad):
        at = slice(start, start + 256)
        turned = turn_back(grad, g.cos[at], g.sin[at])
        back, slope = norm_back(g.kvraw[at], g.heads[1:2], turned)
        return jnp.where(core == 0, back, grad).astype(LOW), jnp.where(core == 0, slope, 0.0)

    @job("KB")
    def _():
        for start in range(0, 1024, 256):
            low, slope = keys_back(start, g.gkv[core, start : start + 256])
            g.dheads[1:2] += slope
            g.gkr[start : start + 256] = low
        put(g.n1t, g.gkr, KV, 0, 128, 128, w=128)

    @job("QS")
    def _():
        for rows in halves:
            g.a[rows] = dot(g.gqr[rows], g.wq[...], NT)

    def first_rows(i):
        rows = halves[i]
        held["ha%d" % i].wait_recv()
        start = ROWS + rows.start
        grad = added(g.gkv[core, start : start + 256], g.hr[rows])
        low, _ = keys_back(start, grad)
        swap("n%d" % i, 1, rows, g.a[rows] + dot(low, g.wkv[...], NT))

    def input_rows(i):
        rows = halves[i]
        back, slope = norm_back(tok[rows].astype(F32), gain(0), total("n%d" % i, 1, rows))
        g.dgains[0:1] += slope
        igrad[rows] = g.gh[rows] + back

    for i in range(2):
        jobs["V%d" % i] = lambda i=i: summed_rows(i)
        jobs["NN%d" % i] = lambda i=i: first_rows(i)
        jobs["I%d" % i] = lambda i=i: input_rows(i)

    @job("EX")
    def _():
        for d in range(16):
            g.ends[d, 0:8, 0:40] = g.dgains[:, 40 * d : 40 * d + 40]
            g.ends[d, 8:16, 0:16] = g.dheads[:, 16 * d : 16 * d + 16]
        g.end_snd[...] = g.ends[...].astype(LOW).reshape(4, 4, 16, 128)

    @job("se.one")
    def _():
        held["se"] = [
            other.copy(g.end_snd.at[place(y + k)], g.end_rcv.at[y], {"dp": place(y + k) * 4 + x})
            for k in (1, 3, 2)
        ]

    @job("se.two")
    def _():
        for made in held["se"]:
            made.wait_recv()
        g.end_rcv[y] = g.end_snd[y]
        g.end_mid[...] = added(*(g.end_rcv[i] for i in range(4))).astype(LOW)
        held["se"] = [
            other.copy(g.end_mid.at[place(x + k)], g.end_mrc.at[x], {"dp": y * 4 + place(x + k)})
            for k in (1, 3, 2)
        ]

    @job("se.five")
    def _():
        for made in held["se"]:
            made.wait_recv()
        g.end_mrc[x] = g.end_mid[x]
        g.end_z[z] = added(*(g.end_mrc[i] for i in range(4))).astype(LOW)
        held["se"] = [other.copy(g.end_z.at[z], g.end_z.at[z], target) for target in along_z] + [
            other.copy(g.end_z.at[z], g.end_far.at[z], target) for target in across
        ]

    @job("se.fin")
    def _():
        for made in held["se"]:
            made.wait_recv()
        own = added(*(g.end_z[i] for i in range(4)))
        far = added(*(g.end_far[i] for i in range(4)))
        ends[0:8] = own[0:8]
        ends[8:16] = own[8:16] + far[8:16]

    def put_final(name, source, start, at, width):
        def work():
            jobs[name + ".finish"]()
            cols = pl.ds(start, width)
            grads[:, at : at + width] = added(*(source[i, :, cols] for i in range(4)))

        jobs[name + ".fin"] = work

    put_final("s3", g.final, DOWN, DOWN, 512)
    put_final("sa", g.final, GATEUP, GATEUP, 512)
    put_final("sb", g.final, GATEUP + 512, GATEUP + 512, 512)
    put_final("s1", g.final, OUT, OUT, 256)

    @job("s0.fin")
    def _():
        jobs["s0.finish"]()
        own = added(*(g.final[i, :, KV:QUERY] for i in range(4)))
        far = added(*(g.far[i] for i in range(4)))
        grads[:, 0:128] = jnp.where(core == 0, own, far)
        grads[:, EXTRA:OUT] = jnp.where(core == 0, far, own)
        grads[:, QUERY:EXTRA] = added(*(g.final[i, :, QUERY:EXTRA] for i in range(4)))

    for name in ORDER:
        jobs[name]()
    scatter_wires.drain()
    waited = [held[n + str(i)] for n in "afgn" for i in (0, 1)]
    for made in other.started:
        if not any(made is one for one in waited):
            made.wait_send()


def hand_out(output, input_grad, done, ends, out, igrad, query, keyval, wide, gateup, down, norms, heads, sems):
    copies = [
        pltpu.make_async_copy(output, out, sems.at[0]),
        pltpu.make_async_copy(input_grad, igrad, sems.at[1]),
    ]
    for made in copies:
        made.start()
    keyval[:, 0:256] = unfold(done[:, KV:QUERY])
    keyval[:, 256:512] = unfold(done[:, EXTRA:OUT])
    query[...] = unfold(done[:, QUERY:EXTRA])
    wide[...] = unfold(done[:, OUT:GATEUP])
    gateup[0] = done[:40, GATEUP:DOWN]
    gateup[1] = done[40:, GATEUP:DOWN]
    down[...] = unfold(done[:, DOWN:WIRE])
    norms[...] = ends[0:4, 0:40]
    heads[...] = ends[8:10, 0:16]
    for made in copies:
        made.wait()


def vmem():
    return pl.BlockSpec(memory_space=pltpu.VMEM)


def ring_buffers(cols):
    return [
        pltpu.VMEM((2, 2, 80, cols), LOW),
        pltpu.VMEM((2, 4, 80, cols), LOW),
        pltpu.VMEM((4, 80, cols), LOW),
        pltpu.VMEM((80, cols), LOW),
        pltpu.VMEM((2, 80, cols), LOW),
    ]


def shards(
    tokens, segments, cotangent, w_query, w_keyval, w_out, w_gateup, w_down, norm_gains, head_gains
):
    output, input_grad, done, ends = pl.pallas_call(
        layer_kernel,
        out_shape=(
            jax.ShapeDtypeStruct((ROWS, D), LOW),
            jax.ShapeDtypeStruct((ROWS, D), F32),
            jax.ShapeDtypeStruct((80, WIRE), F32),
            jax.ShapeDtypeStruct((16, 128), F32),
        ),
        in_specs=[vmem()] * 10,
        out_specs=(vmem(),) * 4,
        scratch_shapes=[
            *(pltpu.VMEM(*shape) for shape in SCRATCH.values()),
            *ring_buffers(SET_COLS[0]),
            *ring_buffers(SET_COLS[1]),
            pltpu.SemaphoreType.DMA((64,)),
            pltpu.SemaphoreType.DMA((64,)),
            pltpu.SemaphoreType.DMA((128,)),
            pltpu.SemaphoreType.DMA((128,)),
            pltpu.SemaphoreType.DMA((40,)),
            pltpu.SemaphoreType.DMA((40,)),
        ],
        compiler_params=pltpu.CompilerParams(
            collective_id=0, has_side_effects=True, vmem_limit_bytes=VMEM_BYTES
        ),
    )(
        tokens[0],
        segments,
        cotangent[0],
        w_query,
        w_keyval,
        w_out.T,
        w_gateup,
        w_down.T,
        norm_gains,
        head_gains,
    )
    whole = pl.BlockSpec(memory_space=pl.ANY)
    results = pl.pallas_call(
        hand_out,
        out_shape=(
            jax.ShapeDtypeStruct((ROWS, D), LOW),
            jax.ShapeDtypeStruct((ROWS, D), F32),
            jax.ShapeDtypeStruct((40, 512), F32),
            jax.ShapeDtypeStruct((40, 512), F32),
            jax.ShapeDtypeStruct((40, 512), F32),
            jax.ShapeDtypeStruct((2, 40, FFH), F32),
            jax.ShapeDtypeStruct((40, FFH), F32),
            jax.ShapeDtypeStruct((4, 40), F32),
            jax.ShapeDtypeStruct((2, 16), F32),
        ),
        in_specs=[whole, whole, vmem(), vmem()],
        out_specs=(whole, whole) + (vmem(),) * 7,
        scratch_shapes=[pltpu.SemaphoreType.DMA((2,))],
        compiler_params=pltpu.CompilerParams(vmem_limit_bytes=VMEM_BYTES),
    )(output, input_grad, done, ends)
    return (
        results[0][None],
        results[1][None],
        results[2],
        results[3],
        results[4].T,
        results[5],
        results[6].T,
        results[7],
        results[8],
    )


def solution(mesh):
    placed = (
        P("dp", "ctx", None),
        P("dp", "ctx"),
        P("dp", "ctx", None),
        P("dp", "tensor"),
        P("dp", None),
        P("tensor", "dp"),
        P(None, "dp", "tensor"),
        P("tensor", "dp"),
        P(None, "dp"),
        P(None, "dp"),
    )
    return jax.shard_map(
        shards,
        mesh=mesh,
        in_specs=placed,
        out_specs=(
            P("dp", "ctx", None),
            P("dp", "ctx", None),
            P("dp", "tensor"),
            P("dp", None),
            P("tensor", "dp"),
            P(None, "dp", "tensor"),
            P("tensor", "dp"),
            P(None, "dp"),
            P(None, "dp"),
        ),
        check_vma=False,
    )
```

```python
import math
import types

import jax
import jax.numpy as jnp
from jax import lax
from jax.experimental import pallas as pl
from jax.experimental.pallas import tpu as pltpu
from jax.sharding import PartitionSpec as P

WINDOW = 512
EPSILON = 1e-06
MESH = pl.DeviceIdType.MESH
VMEM_BYTES = 60 * 1024 * 1024

KV, QUERY, EXTRA, OUT, GATEUP, DOWN, WIRE = 0, 128, 384, 512, 768, 1792, 2304
GATHERS = (
    ((0, 256), (256, 256)),
    ((512, 128), (640, 128)),
    ((768, 512), (1280, 512)),
    ((1792, 256), (2048, 256)),
)
SCATTERS = (
    ("s3", (1792, 256), (2048, 256)),
    ("sa", (768, 256), (1024, 256)),
    ("sb", (1280, 256), (1536, 256)),
    ("s1", (512, 128), (640, 128)),
    ("s0", (0, 256), (256, 128)),
)
SET_COLS = (1152, 1024)
CUT = 48
ROWS, D, HD, FFH = 512, 640, 256, 1024
SCALE = 1.0 / math.sqrt(HD)
LOW = jnp.bfloat16
F32 = jnp.float32
NN, NT, TN = ((1,), (0,)), ((1,), (1,)), ((0,), (0,))


def place(u):
    return lax.rem(u + 8, 4)


class Wires:
    def __init__(self, send, recv):
        self.send, self.recv, self.used = send, recv, 0
        self.started = []

    def copy(self, src, dst, target):
        index = self.used
        self.used += 1
        made = pltpu.make_async_remote_copy(
            src_ref=src,
            dst_ref=dst,
            send_sem=self.send.at[index],
            recv_sem=self.recv.at[index],
            device_id=target,
            device_id_type=MESH,
        )
        made.start()
        self.started.append(made)
        return made

    def drain(self):
        for made in self.started:
            made.wait_send()
        self.started = []


class Ring:
    def __init__(self, first, x, y):
        self.first = first
        self.f, self.s = (x, y) if first == "x" else (y, x)

    def slot(self, ref, f, s, *rest):
        return ref.at[(s, f) + rest] if self.first == "x" else ref.at[(f, s) + rest]

    def index(self, f, s):
        return (s, f) if self.first == "x" else (f, s)

    def to_f(self, step):
        f = place(self.f + step)
        return {"dp": self.s * 4 + f} if self.first == "x" else {"dp": f * 4 + self.s}

    def to_s(self, step):
        s = place(self.s + step)
        return {"dp": s * 4 + self.f} if self.first == "x" else {"dp": self.f * 4 + s}


class Gather:
    def __init__(self, ring, wires, shard, whole, direct, start, width):
        self.ring, self.wires, self.shard, self.whole = ring, wires, shard, whole
        self.direct = direct
        self.cols = pl.ds(start, width)

    def one(self):
        r, c = self.ring, self.cols
        src = self.shard.at[:, c]
        dst = r.slot(self.whole, r.f, r.s, slice(None), c)
        self.a = self.wires.copy(src, dst, r.to_f(1))
        self.b = self.wires.copy(src, dst, r.to_f(-1))
        if self.direct:
            self.c = self.wires.copy(src, dst, r.to_f(2))

    def two(self):
        r, c = self.ring, self.cols
        self.a.wait_recv()
        part = r.slot(self.whole, place(r.f - 1), r.s, pl.ds(0, CUT), c)
        a = self.wires.copy(part, part, r.to_f(1))
        self.b.wait_recv()
        part = r.slot(self.whole, place(r.f + 1), r.s, pl.ds(CUT, 80 - CUT), c)
        b = self.wires.copy(part, part, r.to_f(-1))
        self.a, self.b = a, b

    def three(self):
        r, c = self.ring, self.cols
        self.a.wait_recv()
        self.b.wait_recv()
        if self.direct:
            self.c.wait_recv()
        part = r.slot(self.whole, slice(None), r.s, slice(None), c)
        self.a = self.wires.copy(part, part, r.to_s(1))
        self.b = self.wires.copy(part, part, r.to_s(-1))

    def four(self):
        r, c = self.ring, self.cols
        self.a.wait_recv()
        part = r.slot(self.whole, pl.ds(0, 2), place(r.s - 1), slice(None), c)
        a = self.wires.copy(part, part, r.to_s(1))
        self.b.wait_recv()
        part = r.slot(self.whole, pl.ds(2, 2), place(r.s + 1), slice(None), c)
        b = self.wires.copy(part, part, r.to_s(-1))
        self.a, self.b = a, b

    def finish(self):
        self.a.wait_recv()
        self.b.wait_recv()


def added(*terms):
    total = terms[0].astype(jnp.float32)
    for term in terms[1:]:
        total = total + term.astype(jnp.float32)
    return total


class Scatter:
    def __init__(self, ring, wires, grads, bufs, final, z, start, width, offset, far):
        self.ring, self.wires, self.grads, self.final, self.z = ring, wires, grads, final, z
        self.r1, self.r2, self.sums, self.r3, self.r4 = bufs
        self.cols = pl.ds(start, width)
        self.near = pl.ds(offset, width)
        self.far, self.start = far, start

    def one(self):
        r, c, n = self.ring, self.cols, self.near
        far = place(r.s + 2)
        self.a = self.wires.copy(
            r.slot(self.grads, pl.ds(0, 2), far, slice(None), c), self.r1.at[0, :, :, n], r.to_s(1)
        )
        self.b = self.wires.copy(
            r.slot(self.grads, pl.ds(2, 2), far, slice(None), c), self.r1.at[1, :, :, n], r.to_s(-1)
        )

    def two(self):
        r, c, n = self.ring, self.cols, self.near
        after, before = place(r.s + 1), place(r.s - 1)
        self.a.wait_recv()
        for i in range(2):
            at = r.index(i, after) + (slice(None), c)
            self.grads[at] = added(self.grads[at], self.r1[0, i, :, n]).astype(jnp.bfloat16)
        a = self.wires.copy(
            r.slot(self.grads, slice(None), after, slice(None), c), self.r2.at[0, :, :, n], r.to_s(1)
        )
        self.b.wait_recv()
        for i in range(2):
            at = r.index(2 + i, before) + (slice(None), c)
            self.grads[at] = added(self.grads[at], self.r1[1, i, :, n]).astype(jnp.bfloat16)
        b = self.wires.copy(
            r.slot(self.grads, slice(None), before, slice(None), c),
            self.r2.at[1, :, :, n],
            r.to_s(-1),
        )
        self.a, self.b = a, b

    def three(self):
        r, c, n = self.ring, self.cols, self.near
        self.a.wait_recv()
        self.b.wait_recv()
        for i in range(4):
            at = r.index(i, r.s) + (slice(None), c)
            self.sums[i, :, n] = added(
                self.grads[at], self.r2[0, i, :, n], self.r2[1, i, :, n]
            ).astype(jnp.bfloat16)
        far = place(r.f + 2)
        self.a = self.wires.copy(
            self.sums.at[far, pl.ds(0, CUT), n], self.r3.at[pl.ds(0, CUT), n], r.to_f(1)
        )
        self.b = self.wires.copy(
            self.sums.at[far, pl.ds(CUT, 80 - CUT), n],
            self.r3.at[pl.ds(CUT, 80 - CUT), n],
            r.to_f(-1),
        )

    def four(self):
        r, n = self.ring, self.near
        after, before = place(r.f + 1), place(r.f - 1)
        top, low = pl.ds(0, CUT), pl.ds(CUT, 80 - CUT)
        self.a.wait_recv()
        self.sums[after, top, n] = added(self.sums[after, top, n], self.r3[top, n]).astype(
            jnp.bfloat16
        )
        a = self.wires.copy(self.sums.at[after, :, n], self.r4.at[0, :, n], r.to_f(1))
        self.b.wait_recv()
        self.sums[before, low, n] = added(self.sums[before, low, n], self.r3[low, n]).astype(
            jnp.bfloat16
        )
        b = self.wires.copy(self.sums.at[before, :, n], self.r4.at[1, :, n], r.to_f(-1))
        self.a, self.b = a, b

    def five(self):
        r, c, n = self.ring, self.cols, self.near
        self.a.wait_recv()
        self.b.wait_recv()
        self.final[self.z, :, c] = added(
            self.sums[r.f, :, n], self.r4[0, :, n], self.r4[1, :, n]
        ).astype(jnp.bfloat16)
        part = self.final.at[self.z, :, c]
        self.zs = [self.wires.copy(part, part, {"ctx": place(self.z + k)}) for k in (1, 3, 2)]
        if self.far is not None:
            part = self.final.at[self.z, :, pl.ds(self.start, 128)]
            self.zs += [self.wires.copy(part, self.far[0], target) for target in self.far[1]]

    def finish(self):
        for made in self.zs:
            made.wait_recv()


def spot():
    d = lax.axis_index("dp")
    return lax.rem(d, 4), lax.div(d, 4), lax.axis_index("ctx")


def dot(a, b, dims=NN):
    return lax.dot_general(a, b, (dims, ((), ())), preferred_element_type=F32)


def rms(field):
    return lax.rsqrt(jnp.mean(field * field, axis=-1, keepdims=True) + EPSILON)


def norm_back(field, gain, grad):
    r = rms(field)
    hat = field * r
    scaled = grad * gain
    back = r * (scaled - hat * jnp.mean(scaled * hat, axis=-1, keepdims=True))
    return back, jnp.sum(grad * hat, axis=0, keepdims=True)


def turn(field, cos, sin):
    a, b = field[:, :128], field[:, 128:]
    return jnp.concatenate([a * cos - b * sin, b * cos + a * sin], axis=1)


def turn_back(field, cos, sin):
    a, b = field[:, :128], field[:, 128:]
    return jnp.concatenate([a * cos + b * sin, b * cos - a * sin], axis=1)


def fold(block):
    half = block.shape[-1] // 2
    return jnp.concatenate([block[..., :half], block[..., half:]], axis=-2)


def unfold(block):
    rows = block.shape[-2] // 2
    return jnp.concatenate([block[..., :rows, :], block[..., rows:, :]], axis=-1)


def iota(shape, axis):
    return lax.broadcasted_iota(jnp.int32, shape, axis)


SCRATCH = dict(
    wire=((80, WIRE), LOW),
    whole=((4, 4, 80, WIRE), LOW),
    tall=((128, 256), F32),
    wq=((D, 512), LOW),
    wkv=((D, HD), LOW),
    wo=((D, 512), LOW),
    wg=((D, FFH), LOW),
    wu=((D, FFH), LOW),
    wd=((D, FFH), LOW),
    gains=((8, D), F32),
    heads=((8, HD), F32),
    dgains=((8, D), F32),
    ends=((16, 16, 128), F32),
    end_snd=((4, 4, 16, 128), LOW),
    end_rcv=((4, 4, 16, 128), LOW),
    end_mid=((4, 16, 128), LOW),
    end_mrc=((4, 16, 128), LOW),
    end_z=((4, 16, 128), LOW),
    end_far=((4, 16, 128), LOW),
    dheads=((8, HD), F32),
    tokh=((ROWS, D), LOW),
    segp=((1, ROWS), jnp.int32),
    lo_col=((ROWS, 128), F32),
    lo_row=((8, ROWS), F32),
    cos=((1024, 128), F32),
    sin=((1024, 128), F32),
    n1=((1024, D), LOW),
    n1t=((D, 1024), LOW),
    kvb=((2, 1024, HD), LOW),
    kvraw=((1024, HD), F32),
    qraw=((4, 256, HD), F32),
    q=((4, 256, HD), LOW),
    o=((ROWS, 512), LOW),
    go=((4, 256, HD), LOW),
    gqr=((ROWS, 512), LOW),
    a=((ROWS, D), F32),
    h=((ROWS, D), F32),
    n2=((ROWS, D), LOW),
    n2t=((D, ROWS), LOW),
    ga=((ROWS, FFH), F32),
    gb=((ROWS, FFH), F32),
    u=((ROWS, FFH), LOW),
    ggu=((ROWS, 2 * FFH), LOW),
    gf=((ROWS, D), LOW),
    gft=((D, ROWS), LOW),
    gal=((ROWS, D), LOW),
    gat=((D, ROWS), LOW),
    gh=((ROWS, D), F32),
    snd=((2, ROWS, D), LOW),
    rcv=((2, ROWS, D), LOW),
    gkv=((2, 1024, HD), F32),
    kvs=((1024, HD), LOW),
    kvr=((1024, HD), LOW),
    hs=((ROWS, HD), LOW),
    hr=((ROWS, HD), LOW),
    gkr=((1024, HD), LOW),
    gko=((ROWS, HD), LOW),
    final=((4, 80, WIRE), LOW),
    far=((4, 80, 128), LOW),
)


ORDER = (
    "w0", "w1", "p1.one", "p0.one", "w2", "p2.one", "tab", "w3", "p1.two", "p3.one", "p0.three",
    "p2.two", "p1.three", "p3.two", "p0.four", "p2.three", "p1.four", "p3.three", "c0", "c1",
    "mask", "c2", "A0", "A1", "p2.four", "c3", "A2", "A3", "h0", "c4", "p3.four", "h1", "c6",
    "F0", "c8", "F1", "c9", "o0", "FB0", "G0", "o1", "FB1", "PA", "sa.one", "G1", "PB",
    "sb.one", "N0", "B0", "sa.two", "P3", "s3.one", "sb.two", "N1", "P1", "s1.one", "B1",
    "sa.three", "s3.two", "B2", "B3", "sb.three", "sa.four", "PQ", "V0", "V1", "KB", "s0.one",
    "sb.four", "s1.two", "s3.three", "QS", "NN0", "s0.two", "sb.five", "NN1", "sa.five",
    "s1.three", "s3.four", "I0", "I1", "EX", "se.one", "s0.three", "sb.fin", "s1.four",
    "s3.five", "se.two", "s0.four", "sa.fin", "s1.five", "se.five", "s0.five", "s3.fin",
    "s1.fin", "se.fin", "s0.fin",
)


def layer_kernel(tok, seg_row, cot, wq, wkv, wo, wgu, wd, ng, hg, out, igrad, grads, ends, *rest):
    names = list(SCRATCH)
    g = types.SimpleNamespace(**dict(zip(names, rest[: len(names)])))
    rest = rest[len(names) :]
    bufs = (rest[0:5], rest[5:10])
    x, y, z = spot()
    core = lax.axis_index("tensor")
    mate = {"tensor": 1 - core}
    rings = (Ring("x", x, y), Ring("y", x, y))
    gather_wires = Wires(rest[10], rest[11])
    scatter_wires = Wires(rest[12], rest[13])
    other = Wires(rest[14], rest[15])
    along_z = [{"ctx": place(z + k)} for k in (1, 3, 2)]
    across = [{"ctx": place(z + k), "tensor": 1 - core} for k in range(4)]
    targets = [r.to_f(k) for r in rings for k in (1, -1, 2)] + along_z + across
    barrier = pltpu.get_barrier_semaphore()
    for target in targets:
        pl.semaphore_signal(barrier, inc=1, device_id=target, device_id_type=MESH)

    jobs, held = {}, {}

    def job(name):
        def keep(work):
            jobs[name] = work
            return work

        return keep

    def steps(name, members, methods):
        for method in methods:
            jobs[name + "." + method] = lambda method=method: [getattr(m, method)() for m in members]

    for number, piece in enumerate(GATHERS):
        steps(
            "p%d" % number,
            [
                Gather(ring, gather_wires, g.wire, g.whole, number == 0, *piece[i])
                for i, ring in enumerate(rings)
            ],
            ("one", "two", "three", "four", "finish"),
        )
    offsets = [0, 0]
    for name, *piece in SCATTERS:
        made = []
        for i, ring in enumerate(rings):
            start, width = piece[i]
            far = (g.far.at[z], across) if start == KV else None
            made.append(
                Scatter(ring, scatter_wires, g.whole, bufs[i], g.final, z, start, width, offsets[i], far)
            )
            offsets[i] += width
        steps(name, made, ("one", "two", "three", "four", "five", "finish"))

    halves = [slice(0, 256), slice(256, 512)]

    def swap(name, number, rows, value):
        g.snd[number, rows] = value.astype(LOW)
        held[name] = other.copy(g.snd.at[number, rows], g.rcv.at[number, rows], mate)

    def total(name, number, rows):
        held[name].wait_recv()
        held[name].wait_send()
        return g.snd[number, rows].astype(F32) + g.rcv[number, rows].astype(F32)

    @job("w0")
    def _():
        g.tall[...] = jnp.zeros((128, 256), F32)
        mine = wkv[:, pl.ds(pl.multiple_of(core * HD, HD), HD)]
        g.wire[:, KV:QUERY] = fold(mine.astype(F32)).astype(LOW)
        g.wire[:, QUERY:EXTRA] = fold(wq[...].astype(F32)).astype(LOW)
        g.tall[0:4, 0:40] = ng[...].astype(F32)
        g.tall[0:2, 128:144] = hg[...].astype(F32)
        first = jnp.transpose(g.tall[:, 0:128])[:40]
        second = jnp.transpose(g.tall[:, 128:256])[:40]
        g.wire[:, EXTRA:OUT] = jnp.concatenate([first, second], axis=0).astype(LOW)
        g.whole[y, x, :, KV:OUT] = g.wire[:, KV:OUT]
        pl.semaphore_wait(barrier, len(targets))

    @job("w1")
    def _():
        held["seg"] = other.copy(seg_row, g.segp, {"ctx": place(z + 1)})
        held["tok"] = other.copy(tok, g.tokh, {"ctx": place(z + 1)})
        g.wire[:, OUT:GATEUP] = fold(wo[...].astype(F32)).astype(LOW)
        g.whole[y, x, :, OUT:GATEUP] = g.wire[:, OUT:GATEUP]

    @job("w2")
    def _():
        both = jnp.concatenate([wgu[0].astype(F32), wgu[1].astype(F32)], axis=0)
        g.wire[:, GATEUP:DOWN] = both.astype(LOW)
        g.whole[y, x, :, GATEUP:DOWN] = g.wire[:, GATEUP:DOWN]

    @job("w3")
    def _():
        g.wire[:, DOWN:WIRE] = fold(wd[...].astype(F32)).astype(LOW)
        g.whole[y, x, :, DOWN:WIRE] = g.wire[:, DOWN:WIRE]

    @job("tab")
    def _():
        rates = jnp.exp(iota((1, 128), 1).astype(F32) * (-2.0 * math.log(10000.0) / HD))
        fine = iota((128, 128), 0).astype(F32) * rates
        fine_cos, fine_sin = jnp.cos(fine), jnp.sin(fine)
        coarse = (iota((8, 128), 0) * 128 + (z * ROWS - ROWS)).astype(F32) * rates
        coarse_cos, coarse_sin = jnp.cos(coarse), jnp.sin(coarse)
        for i in range(8):
            cc, cs = coarse_cos[i : i + 1], coarse_sin[i : i + 1]
            g.cos[128 * i : 128 * i + 128] = fine_cos * cc - fine_sin * cs
            g.sin[128 * i : 128 * i + 128] = fine_sin * cc + fine_cos * cs
        g.dgains[...] = jnp.zeros((8, D), F32)
        g.dheads[...] = jnp.zeros((8, HD), F32)
        g.gkv[...] = jnp.zeros((2, 1024, HD), F32)
        g.ends[...] = jnp.zeros((16, 16, 128), F32)

    @job("mask")
    def _():
        held["seg"].wait_recv()
        own_ids, prior_ids = seg_row[...].astype(F32), g.segp[...].astype(F32)
        column = jnp.transpose(jnp.broadcast_to(own_ids, (128, ROWS)))[:, 0:1]
        below_prior = jnp.sum((prior_ids < column).astype(F32), axis=1, keepdims=True)
        below_prior = jnp.where(z == 0, float(ROWS), below_prior)
        below_own = jnp.sum((own_ids < column).astype(F32), axis=1, keepdims=True)
        lowest = jnp.maximum(below_prior + below_own, iota((ROWS, 1), 0).astype(F32) + 1.0)
        lowest = jnp.broadcast_to(lowest, (ROWS, 128))
        g.lo_col[...] = lowest
        g.lo_row[...] = jnp.transpose(lowest)[0:8]

    def assemble(first, second, start, width, w=128):
        def one(i, carry):
            at = pl.multiple_of(i * w, w)
            block = g.whole[:, :, :, pl.ds(start + at, w)].astype(F32)
            first[:, pl.ds(at, w)] = block[:, :, :40].reshape(D, w).astype(LOW)
            if second is None:
                first[:, pl.ds(at + width, w)] = block[:, :, 40:].reshape(D, w).astype(LOW)
            else:
                second[:, pl.ds(at, w)] = block[:, :, 40:].reshape(D, w).astype(LOW)
            return carry

        lax.fori_loop(0, width // w, one, 0)

    def gain(i):
        return g.gains[i : i + 1]

    def keys_of(start, normed):
        at = slice(start, start + 256)
        low = normed.astype(LOW)
        g.n1[at] = low
        raw = dot(low, g.wkv[...])
        g.kvraw[at] = raw
        turned = turn(raw * rms(raw) * g.heads[1:2], g.cos[at], g.sin[at])
        g.kvb[core, at] = jnp.where(core == 0, turned, raw).astype(LOW)
        g.n1t[:, at] = jnp.transpose(normed).astype(LOW)

    @job("c0")
    def _():
        jobs["p0.finish"]()
        block = g.whole[:, :, :, EXTRA:OUT].astype(F32)
        g.gains[...] = jnp.transpose(block[:, :, :40].reshape(D, 128))[:8]
        spread = jnp.transpose(block[:, :, 40:].reshape(D, 128))[:8]
        column_at, head_at = iota((D, HD), 0), iota((D, HD), 1)
        pick = (column_at == 40 * (head_at >> 4) + (head_at & 15)).astype(F32).astype(LOW)
        g.heads[...] = dot(spread.astype(LOW), pick)
        assemble(g.wkv, None, KV, 128)
        for rows in halves:
            block = tok[rows].astype(F32)
            keys_of(ROWS + rows.start, block * rms(block) * gain(0))
        part = g.kvb.at[core, pl.ds(ROWS, ROWS)]
        held["kv1"] = other.copy(part, part, mate)

    @job("c1")
    def _():
        held["tok"].wait_recv()
        for rows in halves:
            block = g.tokh[rows].astype(F32)
            keys_of(rows.start, block * rms(block) * gain(0))
        part = g.kvb.at[core, pl.ds(0, ROWS)]
        held["kv2"] = other.copy(part, part, mate)

    @job("c2")
    def _():
        assemble(g.wq, None, QUERY, 256)
        for i in range(2):
            at = slice(ROWS + 256 * i, ROWS + 256 * i + 256)
            raw = dot(g.n1[at], g.wq[...])
            for h in range(2):
                part = raw[:, HD * h : HD * h + HD]
                turned = turn(part * rms(part) * g.heads[0:1], g.cos[at], g.sin[at]).astype(LOW)
                for j in range(2):
                    g.qraw[2 * i + j, 128 * h : 128 * h + 128] = part[128 * j : 128 * j + 128]
                    g.q[2 * i + j, 128 * h : 128 * h + 128] = turned[128 * j : 128 * j + 128]

    def twice(block, axis):
        return jnp.concatenate([block, block], axis=axis)

    def attend(b, carry):
        start = pl.multiple_of(b * 128, 128)
        keys, values = g.kvb[0, pl.ds(start, D)], g.kvb[1, pl.ds(start, D)]
        scores = dot(g.q[b], keys, NT) * SCALE
        lowest = twice(g.lo_col[pl.ds(start, 128), 0:1], 0) - (b * 128).astype(F32)
        place_k = iota((256, D), 1).astype(F32)
        highest = (iota((256, 1), 0) & 127).astype(F32) + float(WINDOW)
        scores = jnp.where((place_k >= lowest) & (place_k <= highest), scores, -1e30)
        expo = jnp.exp(scores - jnp.max(scores, axis=-1, keepdims=True))
        probs = (expo / jnp.sum(expo, axis=-1, keepdims=True)).astype(LOW)
        mixed = dot(probs, values).astype(LOW)
        g.o[pl.ds(start, 128), 0:HD] = mixed[:128]
        g.o[pl.ds(start, 128), HD : 2 * HD] = mixed[128:]
        return carry

    @job("A0")
    def _():
        held["kv1"].wait_recv()
        held["kv2"].wait_recv()
        lax.fori_loop(0, 1, attend, 0)

    for b in (1, 2, 3):
        jobs["A%d" % b] = lambda b=b: lax.fori_loop(b, b + 1, attend, 0)

    @job("c3")
    def _():
        jobs["p1.finish"]()
        assemble(g.wo, None, OUT, 256)
        swap("a0", 0, halves[0], dot(g.o[halves[0]], g.wo[...], NT))

    @job("c4")
    def _():
        swap("a1", 0, halves[1], dot(g.o[halves[1]], g.wo[...], NT))

    def hidden_rows(i):
        rows = halves[i]
        branch = total("a%d" % i, 0, rows)
        g.a[rows] = branch
        hidden = tok[rows].astype(F32) + branch * rms(branch) * gain(1)
        g.h[rows] = hidden
        normed = hidden * rms(hidden) * gain(2)
        g.n2[rows] = normed.astype(LOW)
        g.n2t[:, rows] = jnp.transpose(normed).astype(LOW)

    c0, c1 = math.sqrt(2.0 / math.pi), 0.044715

    def forward_rows(k):
        rows = halves[k]

        def one(i, carry):
            cols = pl.ds(pl.multiple_of(i * 256, 256), 256)
            gate = dot(g.n2[rows], g.wg[:, cols])
            up = dot(g.n2[rows], g.wu[:, cols])
            square = gate * gate
            t = jnp.tanh(c0 * gate * (1.0 + c1 * square))
            act = 0.5 * gate * (1.0 + t)
            slope = 0.5 * (1.0 + t) + 0.5 * gate * (1.0 - t * t) * (c0 * (1.0 + 3.0 * c1 * square))
            g.ga[rows, cols] = act
            g.gb[rows, cols] = up * slope
            g.u[rows, cols] = (act * up).astype(LOW)
            return carry

        lax.fori_loop(0, 4, one, 0)

    @job("c6")
    def _():
        jobs["p2.finish"]()
        assemble(g.wg, g.wu, GATEUP, FFH)

    @job("c8")
    def _():
        jobs["p3.finish"]()
        gather_wires.drain()
        assemble(g.wd, None, DOWN, 512)
        swap("f0", 1, halves[0], dot(g.u[halves[0]], g.wd[...], NT))

    @job("c9")
    def _():
        swap("f1", 1, halves[1], dot(g.u[halves[1]], g.wd[...], NT))

    def output_rows(i):
        rows = halves[i]
        feed = total("f%d" % i, 1, rows)
        out[rows] = (g.h[rows] + feed * rms(feed) * gain(3)).astype(LOW)
        back, slope = norm_back(feed, gain(3), cot[rows].astype(F32))
        g.dgains[3:4] += slope
        g.gf[rows] = back.astype(LOW)
        g.gft[:, rows] = jnp.transpose(back).astype(LOW)

    def put(left, right, start, begin, end, gap, w=256):
        def one(i, carry):
            at = pl.multiple_of(i * w, w)
            first = dot(left[...], right[:, pl.ds(at, w)]).reshape(16, 40, w)
            second = dot(left[...], right[:, pl.ds(at + gap, w)]).reshape(16, 40, w)
            block = jnp.concatenate([first, second], axis=1).astype(LOW)
            g.whole[:, :, :, pl.ds(start + at, w)] = block.reshape(4, 4, 80, w)
            return carry

        lax.fori_loop(begin // w, end // w, one, 0)

    jobs["P3"] = lambda: put(g.gft, g.u, DOWN, 0, 512, 512)
    jobs["PA"] = lambda: put(g.n2t, g.ggu, GATEUP, 0, 512, FFH)
    jobs["PB"] = lambda: put(g.n2t, g.ggu, GATEUP, 512, 1024, FFH)
    jobs["P1"] = lambda: put(g.gat, g.o, OUT, 0, 256, 256)
    jobs["PQ"] = lambda: put(g.n1t.at[:, ROWS:], g.gqr, QUERY, 0, 256, 256)

    def backward_rows(k):
        rows = halves[k]

        def one(i, carry):
            at = pl.multiple_of(i * 256, 256)
            cols = pl.ds(at, 256)
            inner = dot(g.gf[rows], g.wd[:, cols])
            g.ggu[rows, cols] = (inner * g.gb[rows, cols]).astype(LOW)
            g.ggu[rows, pl.ds(at + FFH, 256)] = (inner * g.ga[rows, cols]).astype(LOW)
            return carry

        lax.fori_loop(0, 4, one, 0)

    def second_rows(i):
        rows = halves[i]
        part = dot(g.ggu[rows, 0:FFH], g.wg[...], NT) + dot(g.ggu[rows, FFH:], g.wu[...], NT)
        swap("g%d" % i, 0, rows, part)

    def norm_rows(i):
        rows = halves[i]
        back, slope = norm_back(g.h[rows], gain(2), total("g%d" % i, 0, rows))
        g.dgains[2:3] += slope
        hidden = cot[rows].astype(F32) + back
        g.gh[rows] = hidden
        back, slope = norm_back(g.a[rows], gain(1), hidden)
        g.dgains[1:2] += slope
        g.gat[:, rows] = jnp.transpose(back).astype(LOW)
        grad = dot(back.astype(LOW), g.wo[...]).astype(LOW)
        for j in range(2):
            for h in range(2):
                g.go[2 * i + j, 128 * h : 128 * h + 128] = grad[
                    128 * j : 128 * j + 128, HD * h : HD * h + HD
                ]

    for i in range(2):
        jobs["h%d" % i] = lambda i=i: hidden_rows(i)
        jobs["F%d" % i] = lambda i=i: forward_rows(i)
        jobs["o%d" % i] = lambda i=i: output_rows(i)
        jobs["FB%d" % i] = lambda i=i: backward_rows(i)
        jobs["G%d" % i] = lambda i=i: second_rows(i)
        jobs["N%d" % i] = lambda i=i: norm_rows(i)

    def attend_back(b, carry):
        start = pl.multiple_of(b * 128, 128)
        keys, values = g.kvb[0, pl.ds(start, D)], g.kvb[1, pl.ds(start, D)]
        queries, grad = g.q[b], g.go[b]
        scores = dot(keys, queries, NT) * SCALE
        lowest = twice(g.lo_row[0:1, pl.ds(start, 128)], 1) - (b * 128).astype(F32)
        place_k = iota((D, 256), 0).astype(F32)
        highest = (iota((1, 256), 1) & 127).astype(F32) + float(WINDOW)
        scores = jnp.where((place_k >= lowest) & (place_k <= highest), scores, -1e30)
        expo = jnp.exp(scores - jnp.max(scores, axis=0, keepdims=True))
        probs = expo * (1.0 / jnp.sum(expo, axis=0, keepdims=True))
        grad_probs = dot(values, grad, NT)
        spread = jnp.sum(probs * grad_probs, axis=0, keepdims=True)
        grad_scores = (probs * (grad_probs - spread)).astype(LOW)
        g.gkv[0, pl.ds(start, D)] += dot(grad_scores, queries) * SCALE
        g.gkv[1, pl.ds(start, D)] += dot(probs.astype(LOW), grad)
        grad_q = dot(grad_scores, keys, TN) * SCALE
        at = pl.ds(pl.multiple_of(ROWS + start, 128), 128)
        grad_q = turn_back(grad_q, twice(g.cos[at], 0), twice(g.sin[at], 0))
        back, slope = norm_back(g.qraw[b], g.heads[0:1], grad_q)
        g.dheads[0:1] += slope
        g.gqr[pl.ds(start, 128), 0:HD] = back[:128].astype(LOW)
        g.gqr[pl.ds(start, 128), HD : 2 * HD] = back[128:].astype(LOW)
        return carry

    def back_block(b):
        lax.fori_loop(b, b + 1, attend_back, 0)
        if b in (1, 3):
            rows = pl.ds(0, 256) if b == 1 else pl.ds(256, 768)
            g.kvs[rows] = g.gkv[1 - core, rows].astype(LOW)
            held["kvx%d" % (b // 2)] = other.copy(g.kvs.at[rows], g.kvr.at[rows], mate)

    for b in range(4):
        jobs["B%d" % b] = lambda b=b: back_block(b)

    def summed_rows(i):
        rows = slice(0, 256) if i == 0 else slice(256, 1024)
        held["kvx%d" % i].wait_recv()
        g.gkv[core, rows] = added(g.gkv[core, rows], g.kvr[rows])
        g.hs[halves[i]] = g.gkv[core, halves[i]].astype(LOW)
        held["ha%d" % i] = other.copy(
            g.hs.at[halves[i]], g.hr.at[halves[i]], {"ctx": place(z - 1)}
        )

    def keys_back(start, grad):
        at = slice(start, start + 256)
        turned = turn_back(grad, g.cos[at], g.sin[at])
        back, slope = norm_back(g.kvraw[at], g.heads[1:2], turned)
        return jnp.where(core == 0, back, grad).astype(LOW), jnp.where(core == 0, slope, 0.0)

    @job("KB")
    def _():
        for start in range(0, 1024, 256):
            low, slope = keys_back(start, g.gkv[core, start : start + 256])
            g.dheads[1:2] += slope
            g.gkr[start : start + 256] = low
        put(g.n1t, g.gkr, KV, 0, 128, 128, w=128)

    @job("QS")
    def _():
        for rows in halves:
            g.a[rows] = dot(g.gqr[rows], g.wq[...], NT)

    def first_rows(i):
        rows = halves[i]
        held["ha%d" % i].wait_recv()
        start = ROWS + rows.start
        grad = added(g.gkv[core, start : start + 256], g.hr[rows])
        low, _ = keys_back(start, grad)
        swap("n%d" % i, 1, rows, g.a[rows] + dot(low, g.wkv[...], NT))

    def input_rows(i):
        rows = halves[i]
        back, slope = norm_back(tok[rows].astype(F32), gain(0), total("n%d" % i, 1, rows))
        g.dgains[0:1] += slope
        igrad[rows] = g.gh[rows] + back

    for i in range(2):
        jobs["V%d" % i] = lambda i=i: summed_rows(i)
        jobs["NN%d" % i] = lambda i=i: first_rows(i)
        jobs["I%d" % i] = lambda i=i: input_rows(i)

    @job("EX")
    def _():
        for d in range(16):
            g.ends[d, 0:8, 0:40] = g.dgains[:, 40 * d : 40 * d + 40]
            g.ends[d, 8:16, 0:16] = g.dheads[:, 16 * d : 16 * d + 16]
        g.end_snd[...] = g.ends[...].astype(LOW).reshape(4, 4, 16, 128)

    @job("se.one")
    def _():
        held["se"] = [
            other.copy(g.end_snd.at[place(y + k)], g.end_rcv.at[y], {"dp": place(y + k) * 4 + x})
            for k in (1, 3, 2)
        ]

    @job("se.two")
    def _():
        for made in held["se"]:
            made.wait_recv()
        g.end_rcv[y] = g.end_snd[y]
        g.end_mid[...] = added(*(g.end_rcv[i] for i in range(4))).astype(LOW)
        held["se"] = [
            other.copy(g.end_mid.at[place(x + k)], g.end_mrc.at[x], {"dp": y * 4 + place(x + k)})
            for k in (1, 3, 2)
        ]

    @job("se.five")
    def _():
        for made in held["se"]:
            made.wait_recv()
        g.end_mrc[x] = g.end_mid[x]
        g.end_z[z] = added(*(g.end_mrc[i] for i in range(4))).astype(LOW)
        held["se"] = [other.copy(g.end_z.at[z], g.end_z.at[z], target) for target in along_z] + [
            other.copy(g.end_z.at[z], g.end_far.at[z], target) for target in across
        ]

    @job("se.fin")
    def _():
        for made in held["se"]:
            made.wait_recv()
        own = added(*(g.end_z[i] for i in range(4)))
        far = added(*(g.end_far[i] for i in range(4)))
        ends[0:8] = own[0:8]
        ends[8:16] = own[8:16] + far[8:16]

    def put_final(name, source, start, at, width):
        def work():
            jobs[name + ".finish"]()
            cols = pl.ds(start, width)
            grads[:, at : at + width] = added(*(source[i, :, cols] for i in range(4)))

        jobs[name + ".fin"] = work

    put_final("s3", g.final, DOWN, DOWN, 512)
    put_final("sa", g.final, GATEUP, GATEUP, 512)
    put_final("sb", g.final, GATEUP + 512, GATEUP + 512, 512)
    put_final("s1", g.final, OUT, OUT, 256)

    @job("s0.fin")
    def _():
        jobs["s0.finish"]()
        own = added(*(g.final[i, :, KV:QUERY] for i in range(4)))
        far = added(*(g.far[i] for i in range(4)))
        grads[:, 0:128] = jnp.where(core == 0, own, far)
        grads[:, EXTRA:OUT] = jnp.where(core == 0, far, own)
        grads[:, QUERY:EXTRA] = added(*(g.final[i, :, QUERY:EXTRA] for i in range(4)))

    for name in ORDER:
        jobs[name]()
    scatter_wires.drain()
    waited = [held[n + str(i)] for n in "afgn" for i in (0, 1)]
    for made in other.started:
        if not any(made is one for one in waited):
            made.wait_send()


def hand_out(output, input_grad, done, ends, out, igrad, query, keyval, wide, gateup, down, norms, heads):
    out[...] = output[...]
    igrad[...] = input_grad[...]
    keyval[:, 0:256] = unfold(done[:, KV:QUERY])
    keyval[:, 256:512] = unfold(done[:, EXTRA:OUT])
    query[...] = unfold(done[:, QUERY:EXTRA])
    wide[...] = unfold(done[:, OUT:GATEUP])
    gateup[0] = done[:40, GATEUP:DOWN]
    gateup[1] = done[40:, GATEUP:DOWN]
    down[...] = unfold(done[:, DOWN:WIRE])
    norms[...] = ends[0:4, 0:40]
    heads[...] = ends[8:10, 0:16]


def vmem():
    return pl.BlockSpec(memory_space=pltpu.VMEM)


def ring_buffers(cols):
    return [
        pltpu.VMEM((2, 2, 80, cols), LOW),
        pltpu.VMEM((2, 4, 80, cols), LOW),
        pltpu.VMEM((4, 80, cols), LOW),
        pltpu.VMEM((80, cols), LOW),
        pltpu.VMEM((2, 80, cols), LOW),
    ]


def shards(
    tokens, segments, cotangent, w_query, w_keyval, w_out, w_gateup, w_down, norm_gains, head_gains
):
    output, input_grad, done, ends = pl.pallas_call(
        layer_kernel,
        out_shape=(
            jax.ShapeDtypeStruct((ROWS, D), LOW),
            jax.ShapeDtypeStruct((ROWS, D), F32),
            jax.ShapeDtypeStruct((80, WIRE), F32),
            jax.ShapeDtypeStruct((16, 128), F32),
        ),
        in_specs=[vmem()] * 10,
        out_specs=(vmem(),) * 4,
        scratch_shapes=[
            *(pltpu.VMEM(*shape) for shape in SCRATCH.values()),
            *ring_buffers(SET_COLS[0]),
            *ring_buffers(SET_COLS[1]),
            pltpu.SemaphoreType.DMA((64,)),
            pltpu.SemaphoreType.DMA((64,)),
            pltpu.SemaphoreType.DMA((128,)),
            pltpu.SemaphoreType.DMA((128,)),
            pltpu.SemaphoreType.DMA((40,)),
            pltpu.SemaphoreType.DMA((40,)),
        ],
        compiler_params=pltpu.CompilerParams(
            collective_id=0, has_side_effects=True, vmem_limit_bytes=VMEM_BYTES
        ),
    )(
        tokens[0],
        segments,
        cotangent[0],
        w_query,
        w_keyval,
        w_out.T,
        w_gateup,
        w_down.T,
        norm_gains,
        head_gains,
    )
    results = pl.pallas_call(
        hand_out,
        out_shape=(
            jax.ShapeDtypeStruct((ROWS, D), LOW),
            jax.ShapeDtypeStruct((ROWS, D), F32),
            jax.ShapeDtypeStruct((40, 512), F32),
            jax.ShapeDtypeStruct((40, 512), F32),
            jax.ShapeDtypeStruct((40, 512), F32),
            jax.ShapeDtypeStruct((2, 40, FFH), F32),
            jax.ShapeDtypeStruct((40, FFH), F32),
            jax.ShapeDtypeStruct((4, 40), F32),
            jax.ShapeDtypeStruct((2, 16), F32),
        ),
        in_specs=[vmem()] * 4,
        out_specs=(vmem(),) * 9,
        compiler_params=pltpu.CompilerParams(vmem_limit_bytes=VMEM_BYTES),
    )(output, input_grad, done, ends)
    return (
        results[0][None],
        results[1][None],
        results[2],
        results[3],
        results[4].T,
        results[5],
        results[6].T,
        results[7],
        results[8],
    )


def solution(mesh):
    placed = (
        P("dp", "ctx", None),
        P("dp", "ctx"),
        P("dp", "ctx", None),
        P("dp", "tensor"),
        P("dp", None),
        P("tensor", "dp"),
        P(None, "dp", "tensor"),
        P("tensor", "dp"),
        P(None, "dp"),
        P(None, "dp"),
    )
    return jax.shard_map(
        shards,
        mesh=mesh,
        in_specs=placed,
        out_specs=(
            P("dp", "ctx", None),
            P("dp", "ctx", None),
            P("dp", "tensor"),
            P("dp", None),
            P("tensor", "dp"),
            P(None, "dp", "tensor"),
            P("tensor", "dp"),
            P(None, "dp"),
            P(None, "dp"),
        ),
        check_vma=False,
    )
```

```python
import math
import types

import jax
import jax.numpy as jnp
from jax import lax
from jax.experimental import pallas as pl
from jax.experimental.pallas import tpu as pltpu
from jax.sharding import PartitionSpec as P

WINDOW = 512
EPSILON = 1e-06
MESH = pl.DeviceIdType.MESH
VMEM_BYTES = 60 * 1024 * 1024

KV, QUERY, EXTRA, OUT, GATEUP, DOWN, WIRE = 0, 128, 384, 512, 768, 1792, 2304
GATHERS = (
    ((0, 256), (256, 256)),
    ((512, 128), (640, 128)),
    ((768, 512), (1280, 512)),
    ((1792, 256), (2048, 256)),
)
SCATTERS = (
    ("s3", (1792, 256), (2048, 256)),
    ("sa", (768, 256), (1024, 256)),
    ("sb", (1280, 256), (1536, 256)),
    ("s1", (512, 128), (640, 128)),
    ("s0", (0, 256), (256, 128)),
)
SET_COLS = (1152, 1024)
CUT = 48
ROWS, D, HD, FFH = 512, 640, 256, 1024
SCALE = 1.0 / math.sqrt(HD)
LOW = jnp.bfloat16
F32 = jnp.float32
NN, NT, TN = ((1,), (0,)), ((1,), (1,)), ((0,), (0,))


def place(u):
    return lax.rem(u + 8, 4)


class Wires:
    def __init__(self, send, recv):
        self.send, self.recv, self.used = send, recv, 0
        self.started = []

    def copy(self, src, dst, target):
        index = self.used
        self.used += 1
        made = pltpu.make_async_remote_copy(
            src_ref=src,
            dst_ref=dst,
            send_sem=self.send.at[index],
            recv_sem=self.recv.at[index],
            device_id=target,
            device_id_type=MESH,
        )
        made.start()
        self.started.append(made)
        return made

    def drain(self):
        for made in self.started:
            made.wait_send()
        self.started = []


class Ring:
    def __init__(self, first, x, y):
        self.first = first
        self.f, self.s = (x, y) if first == "x" else (y, x)

    def slot(self, ref, f, s, *rest):
        return ref.at[(s, f) + rest] if self.first == "x" else ref.at[(f, s) + rest]

    def index(self, f, s):
        return (s, f) if self.first == "x" else (f, s)

    def to_f(self, step):
        f = place(self.f + step)
        return {"dp": self.s * 4 + f} if self.first == "x" else {"dp": f * 4 + self.s}

    def to_s(self, step):
        s = place(self.s + step)
        return {"dp": s * 4 + self.f} if self.first == "x" else {"dp": self.f * 4 + s}


class Gather:
    def __init__(self, ring, wires, shard, whole, direct, start, width):
        self.ring, self.wires, self.shard, self.whole = ring, wires, shard, whole
        self.direct = direct
        self.cols = pl.ds(start, width)

    def one(self):
        r, c = self.ring, self.cols
        src = self.shard.at[:, c]
        dst = r.slot(self.whole, r.f, r.s, slice(None), c)
        self.a = self.wires.copy(src, dst, r.to_f(1))
        self.b = self.wires.copy(src, dst, r.to_f(-1))
        if self.direct:
            self.c = self.wires.copy(src, dst, r.to_f(2))

    def two(self):
        r, c = self.ring, self.cols
        self.a.wait_recv()
        part = r.slot(self.whole, place(r.f - 1), r.s, pl.ds(0, CUT), c)
        a = self.wires.copy(part, part, r.to_f(1))
        self.b.wait_recv()
        part = r.slot(self.whole, place(r.f + 1), r.s, pl.ds(CUT, 80 - CUT), c)
        b = self.wires.copy(part, part, r.to_f(-1))
        self.a, self.b = a, b

    def three(self):
        r, c = self.ring, self.cols
        self.a.wait_recv()
        self.b.wait_recv()
        if self.direct:
            self.c.wait_recv()
        part = r.slot(self.whole, slice(None), r.s, slice(None), c)
        self.a = self.wires.copy(part, part, r.to_s(1))
        self.b = self.wires.copy(part, part, r.to_s(-1))

    def four(self):
        r, c = self.ring, self.cols
        self.a.wait_recv()
        part = r.slot(self.whole, pl.ds(0, 2), place(r.s - 1), slice(None), c)
        a = self.wires.copy(part, part, r.to_s(1))
        self.b.wait_recv()
        part = r.slot(self.whole, pl.ds(2, 2), place(r.s + 1), slice(None), c)
        b = self.wires.copy(part, part, r.to_s(-1))
        self.a, self.b = a, b

    def finish(self):
        self.a.wait_recv()
        self.b.wait_recv()


def added(*terms):
    total = terms[0].astype(jnp.float32)
    for term in terms[1:]:
        total = total + term.astype(jnp.float32)
    return total


class Scatter:
    def __init__(self, ring, wires, grads, bufs, final, z, start, width, offset, far):
        self.ring, self.wires, self.grads, self.final, self.z = ring, wires, grads, final, z
        self.r1, self.r2, self.sums, self.r3, self.r4 = bufs
        self.cols = pl.ds(start, width)
        self.near = pl.ds(offset, width)
        self.far, self.start = far, start

    def one(self):
        r, c, n = self.ring, self.cols, self.near
        far = place(r.s + 2)
        self.a = self.wires.copy(
            r.slot(self.grads, pl.ds(0, 2), far, slice(None), c), self.r1.at[0, :, :, n], r.to_s(1)
        )
        self.b = self.wires.copy(
            r.slot(self.grads, pl.ds(2, 2), far, slice(None), c), self.r1.at[1, :, :, n], r.to_s(-1)
        )

    def two(self):
        r, c, n = self.ring, self.cols, self.near
        after, before = place(r.s + 1), place(r.s - 1)
        self.a.wait_recv()
        for i in range(2):
            at = r.index(i, after) + (slice(None), c)
            self.grads[at] = added(self.grads[at], self.r1[0, i, :, n]).astype(jnp.bfloat16)
        a = self.wires.copy(
            r.slot(self.grads, slice(None), after, slice(None), c), self.r2.at[0, :, :, n], r.to_s(1)
        )
        self.b.wait_recv()
        for i in range(2):
            at = r.index(2 + i, before) + (slice(None), c)
            self.grads[at] = added(self.grads[at], self.r1[1, i, :, n]).astype(jnp.bfloat16)
        b = self.wires.copy(
            r.slot(self.grads, slice(None), before, slice(None), c),
            self.r2.at[1, :, :, n],
            r.to_s(-1),
        )
        self.a, self.b = a, b

    def three(self):
        r, c, n = self.ring, self.cols, self.near
        self.a.wait_recv()
        self.b.wait_recv()
        for i in range(4):
            at = r.index(i, r.s) + (slice(None), c)
            self.sums[i, :, n] = added(
                self.grads[at], self.r2[0, i, :, n], self.r2[1, i, :, n]
            ).astype(jnp.bfloat16)
        far = place(r.f + 2)
        self.a = self.wires.copy(
            self.sums.at[far, pl.ds(0, CUT), n], self.r3.at[pl.ds(0, CUT), n], r.to_f(1)
        )
        self.b = self.wires.copy(
            self.sums.at[far, pl.ds(CUT, 80 - CUT), n],
            self.r3.at[pl.ds(CUT, 80 - CUT), n],
            r.to_f(-1),
        )

    def four(self):
        r, n = self.ring, self.near
        after, before = place(r.f + 1), place(r.f - 1)
        top, low = pl.ds(0, CUT), pl.ds(CUT, 80 - CUT)
        self.a.wait_recv()
        self.sums[after, top, n] = added(self.sums[after, top, n], self.r3[top, n]).astype(
            jnp.bfloat16
        )
        a = self.wires.copy(self.sums.at[after, :, n], self.r4.at[0, :, n], r.to_f(1))
        self.b.wait_recv()
        self.sums[before, low, n] = added(self.sums[before, low, n], self.r3[low, n]).astype(
            jnp.bfloat16
        )
        b = self.wires.copy(self.sums.at[before, :, n], self.r4.at[1, :, n], r.to_f(-1))
        self.a, self.b = a, b

    def five(self):
        r, c, n = self.ring, self.cols, self.near
        self.a.wait_recv()
        self.b.wait_recv()
        self.final[self.z, :, c] = added(
            self.sums[r.f, :, n], self.r4[0, :, n], self.r4[1, :, n]
        ).astype(jnp.bfloat16)
        part = self.final.at[self.z, :, c]
        self.zs = [self.wires.copy(part, part, {"ctx": place(self.z + k)}) for k in (1, 3, 2)]
        if self.far is not None:
            part = self.final.at[self.z, :, pl.ds(self.start, 128)]
            self.zs += [self.wires.copy(part, self.far[0], target) for target in self.far[1]]

    def finish(self):
        for made in self.zs:
            made.wait_recv()


def spot():
    d = lax.axis_index("dp")
    return lax.rem(d, 4), lax.div(d, 4), lax.axis_index("ctx")


def dot(a, b, dims=NN):
    return lax.dot_general(a, b, (dims, ((), ())), preferred_element_type=F32)


def rms(field):
    return lax.rsqrt(jnp.mean(field * field, axis=-1, keepdims=True) + EPSILON)


def norm_back(field, gain, grad):
    r = rms(field)
    hat = field * r
    scaled = grad * gain
    back = r * (scaled - hat * jnp.mean(scaled * hat, axis=-1, keepdims=True))
    return back, jnp.sum(grad * hat, axis=0, keepdims=True)


def turn(field, cos, sin):
    a, b = field[:, :128], field[:, 128:]
    return jnp.concatenate([a * cos - b * sin, b * cos + a * sin], axis=1)


def turn_back(field, cos, sin):
    a, b = field[:, :128], field[:, 128:]
    return jnp.concatenate([a * cos + b * sin, b * cos - a * sin], axis=1)


def fold(block):
    half = block.shape[-1] // 2
    return jnp.concatenate([block[..., :half], block[..., half:]], axis=-2)


def unfold(block):
    rows = block.shape[-2] // 2
    return jnp.concatenate([block[..., :rows, :], block[..., rows:, :]], axis=-1)


def iota(shape, axis):
    return lax.broadcasted_iota(jnp.int32, shape, axis)


SCRATCH = dict(
    wire=((80, WIRE), LOW),
    whole=((4, 4, 80, WIRE), LOW),
    tall=((128, 256), F32),
    wq=((D, 512), LOW),
    wkv=((D, HD), LOW),
    wo=((D, 512), LOW),
    wg=((D, FFH), LOW),
    wu=((D, FFH), LOW),
    wd=((D, FFH), LOW),
    gains=((8, D), F32),
    heads=((8, HD), F32),
    dgains=((8, D), F32),
    ends=((16, 16, 128), F32),
    end_snd=((4, 4, 16, 128), LOW),
    end_rcv=((4, 4, 16, 128), LOW),
    end_mid=((4, 16, 128), LOW),
    end_mrc=((4, 16, 128), LOW),
    end_z=((4, 16, 128), LOW),
    end_far=((4, 16, 128), LOW),
    dheads=((8, HD), F32),
    tokh=((ROWS, D), LOW),
    segp=((1, ROWS), jnp.int32),
    lo_col=((ROWS, 128), F32),
    lo_row=((8, ROWS), F32),
    cos=((1024, 128), F32),
    sin=((1024, 128), F32),
    n1=((1024, D), LOW),
    n1t=((D, 1024), LOW),
    kvb=((2, 1024, HD), LOW),
    kvraw=((1024, HD), F32),
    qraw=((4, 256, HD), F32),
    q=((4, 256, HD), LOW),
    o=((ROWS, 512), LOW),
    go=((4, 256, HD), LOW),
    gqr=((ROWS, 512), LOW),
    a=((ROWS, D), F32),
    h=((ROWS, D), F32),
    n2=((ROWS, D), LOW),
    n2t=((D, ROWS), LOW),
    ga=((ROWS, FFH), F32),
    gb=((ROWS, FFH), F32),
    u=((ROWS, FFH), LOW),
    ggu=((ROWS, 2 * FFH), LOW),
    gf=((ROWS, D), LOW),
    gft=((D, ROWS), LOW),
    gal=((ROWS, D), LOW),
    gat=((D, ROWS), LOW),
    gh=((ROWS, D), F32),
    snd=((2, ROWS, D), LOW),
    rcv=((2, ROWS, D), LOW),
    gkv=((2, 1024, HD), F32),
    kvs=((1024, HD), LOW),
    kvr=((1024, HD), LOW),
    hs=((ROWS, HD), LOW),
    hr=((ROWS, HD), LOW),
    gkr=((1024, HD), LOW),
    gko=((ROWS, HD), LOW),
    final=((4, 80, WIRE), LOW),
    far=((4, 80, 128), LOW),
)


ORDER = (
    "w0", "w1", "p1.one", "p0.one", "w2", "p2.one", "tab", "mask", "p1.two", "w3", "p3.one",
    "p0.three", "p2.two", "p1.three", "p3.two", "p0.four", "p2.three", "p1.four", "c0", "c1",
    "p3.three", "c2", "A0", "A1", "p2.four", "c3", "A2", "A3", "c4", "h0", "p3.four", "h1",
    "c6", "F0", "c8", "F1", "c9", "o0", "FB0", "G0", "o1", "P3", "s3.one", "FB1", "PA",
    "sa.one", "PB", "sb.one", "G1", "N0", "s3.two", "B0", "sa.two", "B1", "sb.two", "N1", "B2",
    "B3", "s3.three", "V0", "P1", "s1.one", "QS", "V1", "sa.three", "PQ", "KB", "s0.one",
    "sb.three", "s3.four", "s1.two", "sa.four", "NN0", "s0.two", "sb.four", "s3.five", "NN1",
    "I0", "s1.three", "sa.five", "I1", "EX", "se.one", "s0.three", "s3.fin", "s1.four",
    "sb.five", "se.two", "s0.four", "sa.fin", "s1.five", "se.five", "s0.five", "sb.fin",
    "s1.fin", "se.fin", "s0.fin",
)


def layer_kernel(
    tok_hbm, seg_row, cot_hbm, wq, wkv, wo, wgu, wd, ng, hg, out_hbm, igrad_hbm, grads_hbm, ends, *rest
):
    names = list(SCRATCH)
    g = types.SimpleNamespace(**dict(zip(names, rest[: len(names)])))
    rest = rest[len(names) :]
    bufs = (rest[0:5], rest[5:10])
    tok, cot, out, igrad, grads, local = rest[16:22]
    tok_read = pltpu.make_async_copy(tok_hbm, tok, local.at[0])
    cot_read = pltpu.make_async_copy(cot_hbm, cot, local.at[1])
    tok_read.start()
    cot_read.start()
    writes = []

    def write(source, target):
        made = pltpu.make_async_copy(source, target, local.at[2 + len(writes)])
        made.start()
        writes.append(made)

    x, y, z = spot()
    core = lax.axis_index("tensor")
    mate = {"tensor": 1 - core}
    rings = (Ring("x", x, y), Ring("y", x, y))
    gather_wires = Wires(rest[10], rest[11])
    scatter_wires = Wires(rest[12], rest[13])
    other = Wires(rest[14], rest[15])
    along_z = [{"ctx": place(z + k)} for k in (1, 3, 2)]
    across = [{"ctx": place(z + k), "tensor": 1 - core} for k in range(4)]
    targets = [r.to_f(k) for r in rings for k in (1, -1, 2)] + along_z + across
    barrier = pltpu.get_barrier_semaphore()
    for target in targets:
        pl.semaphore_signal(barrier, inc=1, device_id=target, device_id_type=MESH)

    jobs, held = {}, {}

    def job(name):
        def keep(work):
            jobs[name] = work
            return work

        return keep

    def steps(name, members, methods):
        for method in methods:
            jobs[name + "." + method] = lambda method=method: [getattr(m, method)() for m in members]

    for number, piece in enumerate(GATHERS):
        steps(
            "p%d" % number,
            [
                Gather(ring, gather_wires, g.wire, g.whole, number == 0, *piece[i])
                for i, ring in enumerate(rings)
            ],
            ("one", "two", "three", "four", "finish"),
        )
    offsets = [0, 0]
    for name, *piece in SCATTERS:
        made = []
        for i, ring in enumerate(rings):
            start, width = piece[i]
            far = (g.far.at[z], across) if start == KV else None
            made.append(
                Scatter(ring, scatter_wires, g.whole, bufs[i], g.final, z, start, width, offsets[i], far)
            )
            offsets[i] += width
        steps(name, made, ("one", "two", "three", "four", "five", "finish"))

    halves = [slice(0, 256), slice(256, 512)]

    def swap(name, number, rows, value):
        g.snd[number, rows] = value.astype(LOW)
        held[name] = other.copy(g.snd.at[number, rows], g.rcv.at[number, rows], mate)

    def total(name, number, rows):
        held[name].wait_recv()
        held[name].wait_send()
        return g.snd[number, rows].astype(F32) + g.rcv[number, rows].astype(F32)

    @job("w0")
    def _():
        g.tall[...] = jnp.zeros((128, 256), F32)
        mine = wkv[:, pl.ds(pl.multiple_of(core * HD, HD), HD)]
        g.wire[:, KV:QUERY] = fold(mine.astype(F32)).astype(LOW)
        g.wire[:, QUERY:EXTRA] = fold(wq[...].astype(F32)).astype(LOW)
        g.tall[0:4, 0:40] = ng[...].astype(F32)
        g.tall[0:2, 128:144] = hg[...].astype(F32)
        first = jnp.transpose(g.tall[:, 0:128])[:40]
        second = jnp.transpose(g.tall[:, 128:256])[:40]
        g.wire[:, EXTRA:OUT] = jnp.concatenate([first, second], axis=0).astype(LOW)
        g.whole[y, x, :, KV:OUT] = g.wire[:, KV:OUT]
        pl.semaphore_wait(barrier, len(targets))

    @job("w1")
    def _():
        held["seg"] = other.copy(seg_row, g.segp, {"ctx": place(z + 1)})
        tok_read.wait()
        held["tok"] = other.copy(tok, g.tokh, {"ctx": place(z + 1)})
        g.wire[:, OUT:GATEUP] = fold(wo[...].astype(F32)).astype(LOW)
        g.whole[y, x, :, OUT:GATEUP] = g.wire[:, OUT:GATEUP]

    @job("w2")
    def _():
        both = jnp.concatenate([wgu[0].astype(F32), wgu[1].astype(F32)], axis=0)
        g.wire[:, GATEUP:DOWN] = both.astype(LOW)
        g.whole[y, x, :, GATEUP:DOWN] = g.wire[:, GATEUP:DOWN]

    @job("w3")
    def _():
        g.wire[:, DOWN:WIRE] = fold(wd[...].astype(F32)).astype(LOW)
        g.whole[y, x, :, DOWN:WIRE] = g.wire[:, DOWN:WIRE]

    @job("tab")
    def _():
        rates = jnp.exp(iota((1, 128), 1).astype(F32) * (-2.0 * math.log(10000.0) / HD))
        fine = iota((128, 128), 0).astype(F32) * rates
        fine_cos, fine_sin = jnp.cos(fine), jnp.sin(fine)
        coarse = (iota((8, 128), 0) * 128 + (z * ROWS - ROWS)).astype(F32) * rates
        coarse_cos, coarse_sin = jnp.cos(coarse), jnp.sin(coarse)
        for i in range(8):
            cc, cs = coarse_cos[i : i + 1], coarse_sin[i : i + 1]
            g.cos[128 * i : 128 * i + 128] = fine_cos * cc - fine_sin * cs
            g.sin[128 * i : 128 * i + 128] = fine_sin * cc + fine_cos * cs
        g.dgains[...] = jnp.zeros((8, D), F32)
        g.dheads[...] = jnp.zeros((8, HD), F32)
        g.gkv[...] = jnp.zeros((2, 1024, HD), F32)
        g.ends[...] = jnp.zeros((16, 16, 128), F32)

    @job("mask")
    def _():
        held["seg"].wait_recv()
        own_ids, prior_ids = seg_row[...].astype(F32), g.segp[...].astype(F32)
        column = jnp.transpose(jnp.broadcast_to(own_ids, (128, ROWS)))[:, 0:1]
        below_prior = jnp.sum((prior_ids < column).astype(F32), axis=1, keepdims=True)
        below_prior = jnp.where(z == 0, float(ROWS), below_prior)
        below_own = jnp.sum((own_ids < column).astype(F32), axis=1, keepdims=True)
        lowest = jnp.maximum(below_prior + below_own, iota((ROWS, 1), 0).astype(F32) + 1.0)
        lowest = jnp.broadcast_to(lowest, (ROWS, 128))
        g.lo_col[...] = lowest
        g.lo_row[...] = jnp.transpose(lowest)[0:8]

    def assemble(first, second, start, width, w=128):
        def one(i):
            at = i * w
            block = g.whole[:, :, :, pl.ds(start + at, w)].astype(F32)
            first[:, pl.ds(at, w)] = block[:, :, :40].reshape(D, w).astype(LOW)
            if second is None:
                first[:, pl.ds(at + width, w)] = block[:, :, 40:].reshape(D, w).astype(LOW)
            else:
                second[:, pl.ds(at, w)] = block[:, :, 40:].reshape(D, w).astype(LOW)

        for i in range(width // w):
            one(i)

    def gain(i):
        return g.gains[i : i + 1]

    def keys_of(start, normed):
        at = slice(start, start + 256)
        low = normed.astype(LOW)
        g.n1[at] = low
        raw = dot(low, g.wkv[...])
        g.kvraw[at] = raw
        turned = turn(raw * rms(raw) * g.heads[1:2], g.cos[at], g.sin[at])
        g.kvb[core, at] = jnp.where(core == 0, turned, raw).astype(LOW)
        g.n1t[:, at] = jnp.transpose(normed).astype(LOW)

    @job("c0")
    def _():
        jobs["p0.finish"]()
        block = g.whole[:, :, :, EXTRA:OUT].astype(F32)
        g.gains[...] = jnp.transpose(block[:, :, :40].reshape(D, 128))[:8]
        spread = jnp.transpose(block[:, :, 40:].reshape(D, 128))[:8]
        column_at, head_at = iota((D, HD), 0), iota((D, HD), 1)
        pick = (column_at == 40 * (head_at >> 4) + (head_at & 15)).astype(F32).astype(LOW)
        g.heads[...] = dot(spread.astype(LOW), pick)
        assemble(g.wkv, None, KV, 128)
        for rows in halves:
            block = tok[rows].astype(F32)
            keys_of(ROWS + rows.start, block * rms(block) * gain(0))
        part = g.kvb.at[core, pl.ds(ROWS, ROWS)]
        held["kv1"] = other.copy(part, part, mate)

    @job("c1")
    def _():
        held["tok"].wait_recv()
        for rows in halves:
            block = g.tokh[rows].astype(F32)
            keys_of(rows.start, block * rms(block) * gain(0))
        part = g.kvb.at[core, pl.ds(0, ROWS)]
        held["kv2"] = other.copy(part, part, mate)

    @job("c2")
    def _():
        assemble(g.wq, None, QUERY, 256)
        for i in range(2):
            at = slice(ROWS + 256 * i, ROWS + 256 * i + 256)
            raw = dot(g.n1[at], g.wq[...])
            for h in range(2):
                part = raw[:, HD * h : HD * h + HD]
                turned = turn(part * rms(part) * g.heads[0:1], g.cos[at], g.sin[at]).astype(LOW)
                for j in range(2):
                    g.qraw[2 * i + j, 128 * h : 128 * h + 128] = part[128 * j : 128 * j + 128]
                    g.q[2 * i + j, 128 * h : 128 * h + 128] = turned[128 * j : 128 * j + 128]

    def twice(block, axis):
        return jnp.concatenate([block, block], axis=axis)

    def attend(b):
        start = b * 128
        keys, values = g.kvb[0, pl.ds(start, D)], g.kvb[1, pl.ds(start, D)]
        scores = dot(g.q[b], keys, NT) * SCALE
        lowest = twice(g.lo_col[pl.ds(start, 128), 0:1], 0) - float(b * 128)
        place_k = iota((256, D), 1).astype(F32)
        highest = (iota((256, 1), 0) & 127).astype(F32) + float(WINDOW)
        scores = jnp.where((place_k >= lowest) & (place_k <= highest), scores, -1e30)
        expo = jnp.exp(scores - jnp.max(scores, axis=-1, keepdims=True))
        probs = (expo / jnp.sum(expo, axis=-1, keepdims=True)).astype(LOW)
        mixed = dot(probs, values).astype(LOW)
        g.o[pl.ds(start, 128), 0:HD] = mixed[:128]
        g.o[pl.ds(start, 128), HD : 2 * HD] = mixed[128:]

    @job("A0")
    def _():
        held["kv1"].wait_recv()
        held["kv2"].wait_recv()
        attend(0)

    for b in (1, 2, 3):
        jobs["A%d" % b] = lambda b=b: attend(b)

    @job("c3")
    def _():
        jobs["p1.finish"]()
        assemble(g.wo, None, OUT, 256)
        swap("a0", 0, halves[0], dot(g.o[halves[0]], g.wo[...], NT))

    @job("c4")
    def _():
        swap("a1", 0, halves[1], dot(g.o[halves[1]], g.wo[...], NT))

    def hidden_rows(i):
        rows = halves[i]
        branch = total("a%d" % i, 0, rows)
        g.a[rows] = branch
        hidden = tok[rows].astype(F32) + branch * rms(branch) * gain(1)
        g.h[rows] = hidden
        normed = hidden * rms(hidden) * gain(2)
        g.n2[rows] = normed.astype(LOW)
        g.n2t[:, rows] = jnp.transpose(normed).astype(LOW)

    c0, c1 = math.sqrt(2.0 / math.pi), 0.044715

    def forward_rows(k):
        rows = halves[k]

        def one(i):
            cols = pl.ds(i * 256, 256)
            gate = dot(g.n2[rows], g.wg[:, cols])
            up = dot(g.n2[rows], g.wu[:, cols])
            square = gate * gate
            t = jnp.tanh(c0 * gate * (1.0 + c1 * square))
            act = 0.5 * gate * (1.0 + t)
            slope = 0.5 * (1.0 + t) + 0.5 * gate * (1.0 - t * t) * (c0 * (1.0 + 3.0 * c1 * square))
            g.ga[rows, cols] = act
            g.gb[rows, cols] = up * slope
            g.u[rows, cols] = (act * up).astype(LOW)

        for i in range(4):
            one(i)

    @job("c6")
    def _():
        jobs["p2.finish"]()
        assemble(g.wg, g.wu, GATEUP, FFH)

    @job("c8")
    def _():
        jobs["p3.finish"]()
        gather_wires.drain()
        assemble(g.wd, None, DOWN, 512)
        swap("f0", 1, halves[0], dot(g.u[halves[0]], g.wd[...], NT))

    @job("c9")
    def _():
        swap("f1", 1, halves[1], dot(g.u[halves[1]], g.wd[...], NT))

    def output_rows(i):
        rows = halves[i]
        if i == 0:
            cot_read.wait()
        feed = total("f%d" % i, 1, rows)
        out[rows] = (g.h[rows] + feed * rms(feed) * gain(3)).astype(LOW)
        back, slope = norm_back(feed, gain(3), cot[rows].astype(F32))
        g.dgains[3:4] += slope
        g.gf[rows] = back.astype(LOW)
        g.gft[:, rows] = jnp.transpose(back).astype(LOW)
        write(out.at[rows], out_hbm.at[rows])

    def put(left, right, start, begin, end, gap, w=256):
        def one(i):
            at = i * w
            first = dot(left[...], right[:, pl.ds(at, w)]).reshape(16, 40, w)
            second = dot(left[...], right[:, pl.ds(at + gap, w)]).reshape(16, 40, w)
            block = jnp.concatenate([first, second], axis=1).astype(LOW)
            g.whole[:, :, :, pl.ds(start + at, w)] = block.reshape(4, 4, 80, w)

        for i in range(begin // w, end // w):
            one(i)

    jobs["P3"] = lambda: put(g.gft, g.u, DOWN, 0, 512, 512)
    jobs["PA"] = lambda: put(g.n2t, g.ggu, GATEUP, 0, 512, FFH)
    jobs["PB"] = lambda: put(g.n2t, g.ggu, GATEUP, 512, 1024, FFH)
    jobs["P1"] = lambda: put(g.gat, g.o, OUT, 0, 256, 256)
    jobs["PQ"] = lambda: put(g.n1t.at[:, ROWS:], g.gqr, QUERY, 0, 256, 256)

    def backward_rows(k):
        rows = halves[k]

        def one(i):
            at = i * 256
            cols = pl.ds(at, 256)
            inner = dot(g.gf[rows], g.wd[:, cols])
            g.ggu[rows, cols] = (inner * g.gb[rows, cols]).astype(LOW)
            g.ggu[rows, pl.ds(at + FFH, 256)] = (inner * g.ga[rows, cols]).astype(LOW)

        for i in range(4):
            one(i)

    def second_rows(i):
        rows = halves[i]
        part = dot(g.ggu[rows, 0:FFH], g.wg[...], NT) + dot(g.ggu[rows, FFH:], g.wu[...], NT)
        swap("g%d" % i, 0, rows, part)

    def norm_rows(i):
        rows = halves[i]
        back, slope = norm_back(g.h[rows], gain(2), total("g%d" % i, 0, rows))
        g.dgains[2:3] += slope
        hidden = cot[rows].astype(F32) + back
        g.gh[rows] = hidden
        back, slope = norm_back(g.a[rows], gain(1), hidden)
        g.dgains[1:2] += slope
        g.gat[:, rows] = jnp.transpose(back).astype(LOW)
        grad = dot(back.astype(LOW), g.wo[...]).astype(LOW)
        for j in range(2):
            for h in range(2):
                g.go[2 * i + j, 128 * h : 128 * h + 128] = grad[
                    128 * j : 128 * j + 128, HD * h : HD * h + HD
                ]

    for i in range(2):
        jobs["h%d" % i] = lambda i=i: hidden_rows(i)
        jobs["F%d" % i] = lambda i=i: forward_rows(i)
        jobs["o%d" % i] = lambda i=i: output_rows(i)
        jobs["FB%d" % i] = lambda i=i: backward_rows(i)
        jobs["G%d" % i] = lambda i=i: second_rows(i)
        jobs["N%d" % i] = lambda i=i: norm_rows(i)

    def attend_back(b):
        start = b * 128
        keys, values = g.kvb[0, pl.ds(start, D)], g.kvb[1, pl.ds(start, D)]
        queries, grad = g.q[b], g.go[b]
        scores = dot(keys, queries, NT) * SCALE
        lowest = twice(g.lo_row[0:1, pl.ds(start, 128)], 1) - float(b * 128)
        place_k = iota((D, 256), 0).astype(F32)
        highest = (iota((1, 256), 1) & 127).astype(F32) + float(WINDOW)
        scores = jnp.where((place_k >= lowest) & (place_k <= highest), scores, -1e30)
        expo = jnp.exp(scores - jnp.max(scores, axis=0, keepdims=True))
        probs = expo * (1.0 / jnp.sum(expo, axis=0, keepdims=True))
        grad_probs = dot(values, grad, NT)
        spread = jnp.sum(probs * grad_probs, axis=0, keepdims=True)
        grad_scores = (probs * (grad_probs - spread)).astype(LOW)
        g.gkv[0, pl.ds(start, D)] += dot(grad_scores, queries) * SCALE
        g.gkv[1, pl.ds(start, D)] += dot(probs.astype(LOW), grad)
        grad_q = dot(grad_scores, keys, TN) * SCALE
        at = pl.ds(ROWS + start, 128)
        grad_q = turn_back(grad_q, twice(g.cos[at], 0), twice(g.sin[at], 0))
        back, slope = norm_back(g.qraw[b], g.heads[0:1], grad_q)
        g.dheads[0:1] += slope
        g.gqr[pl.ds(start, 128), 0:HD] = back[:128].astype(LOW)
        g.gqr[pl.ds(start, 128), HD : 2 * HD] = back[128:].astype(LOW)

    def back_block(b):
        attend_back(b)
        if b in (1, 3):
            rows = pl.ds(0, 256) if b == 1 else pl.ds(256, 768)
            g.kvs[rows] = g.gkv[1 - core, rows].astype(LOW)
            held["kvx%d" % (b // 2)] = other.copy(g.kvs.at[rows], g.kvr.at[rows], mate)

    for b in range(4):
        jobs["B%d" % b] = lambda b=b: back_block(b)

    def summed_rows(i):
        rows = slice(0, 256) if i == 0 else slice(256, 1024)
        held["kvx%d" % i].wait_recv()
        g.gkv[core, rows] = added(g.gkv[core, rows], g.kvr[rows])
        g.hs[halves[i]] = g.gkv[core, halves[i]].astype(LOW)
        held["ha%d" % i] = other.copy(
            g.hs.at[halves[i]], g.hr.at[halves[i]], {"ctx": place(z - 1)}
        )

    def keys_back(start, grad):
        at = slice(start, start + 256)
        turned = turn_back(grad, g.cos[at], g.sin[at])
        back, slope = norm_back(g.kvraw[at], g.heads[1:2], turned)
        return jnp.where(core == 0, back, grad).astype(LOW), jnp.where(core == 0, slope, 0.0)

    @job("KB")
    def _():
        for start in range(0, 1024, 256):
            low, slope = keys_back(start, g.gkv[core, start : start + 256])
            g.dheads[1:2] += slope
            g.gkr[start : start + 256] = low
        put(g.n1t, g.gkr, KV, 0, 128, 128, w=128)

    @job("QS")
    def _():
        for rows in halves:
            g.a[rows] = dot(g.gqr[rows], g.wq[...], NT)

    def first_rows(i):
        rows = halves[i]
        held["ha%d" % i].wait_recv()
        start = ROWS + rows.start
        grad = added(g.gkv[core, start : start + 256], g.hr[rows])
        low, _ = keys_back(start, grad)
        swap("n%d" % i, 1, rows, g.a[rows] + dot(low, g.wkv[...], NT))

    def input_rows(i):
        rows = halves[i]
        back, slope = norm_back(tok[rows].astype(F32), gain(0), total("n%d" % i, 1, rows))
        g.dgains[0:1] += slope
        igrad[rows] = g.gh[rows] + back
        write(igrad.at[rows], igrad_hbm.at[rows])

    for i in range(2):
        jobs["V%d" % i] = lambda i=i: summed_rows(i)
        jobs["NN%d" % i] = lambda i=i: first_rows(i)
        jobs["I%d" % i] = lambda i=i: input_rows(i)

    @job("EX")
    def _():
        for d in range(16):
            g.ends[d, 0:8, 0:40] = g.dgains[:, 40 * d : 40 * d + 40]
            g.ends[d, 8:16, 0:16] = g.dheads[:, 16 * d : 16 * d + 16]
        g.end_snd[...] = g.ends[...].astype(LOW).reshape(4, 4, 16, 128)

    @job("se.one")
    def _():
        held["se"] = [
            other.copy(g.end_snd.at[place(y + k)], g.end_rcv.at[y], {"dp": place(y + k) * 4 + x})
            for k in (1, 3, 2)
        ]

    @job("se.two")
    def _():
        for made in held["se"]:
            made.wait_recv()
        g.end_rcv[y] = g.end_snd[y]
        g.end_mid[...] = added(*(g.end_rcv[i] for i in range(4))).astype(LOW)
        held["se"] = [
            other.copy(g.end_mid.at[place(x + k)], g.end_mrc.at[x], {"dp": y * 4 + place(x + k)})
            for k in (1, 3, 2)
        ]

    @job("se.five")
    def _():
        for made in held["se"]:
            made.wait_recv()
        g.end_mrc[x] = g.end_mid[x]
        g.end_z[z] = added(*(g.end_mrc[i] for i in range(4))).astype(LOW)
        held["se"] = [other.copy(g.end_z.at[z], g.end_z.at[z], target) for target in along_z] + [
            other.copy(g.end_z.at[z], g.end_far.at[z], target) for target in across
        ]

    @job("se.fin")
    def _():
        for made in held["se"]:
            made.wait_recv()
        own = added(*(g.end_z[i] for i in range(4)))
        far = added(*(g.end_far[i] for i in range(4)))
        ends[0:8] = own[0:8]
        ends[8:16] = own[8:16] + far[8:16]

    def put_final(name, source, start, at, width):
        def work():
            jobs[name + ".finish"]()
            cols = pl.ds(start, width)
            grads[:, at : at + width] = added(*(source[i, :, cols] for i in range(4)))
            write(grads.at[:, pl.ds(at, width)], grads_hbm.at[:, pl.ds(at, width)])

        jobs[name + ".fin"] = work

    put_final("s3", g.final, DOWN, DOWN, 512)
    put_final("sa", g.final, GATEUP, GATEUP, 512)
    put_final("sb", g.final, GATEUP + 512, GATEUP + 512, 512)
    put_final("s1", g.final, OUT, OUT, 256)

    @job("s0.fin")
    def _():
        jobs["s0.finish"]()
        own = added(*(g.final[i, :, KV:QUERY] for i in range(4)))
        far = added(*(g.far[i] for i in range(4)))
        grads[:, 0:128] = jnp.where(core == 0, own, far)
        grads[:, EXTRA:OUT] = jnp.where(core == 0, far, own)
        grads[:, QUERY:EXTRA] = added(*(g.final[i, :, QUERY:EXTRA] for i in range(4)))
        write(grads.at[:, pl.ds(0, OUT)], grads_hbm.at[:, pl.ds(0, OUT)])

    for name in ORDER:
        jobs[name]()
    scatter_wires.drain()
    waited = [held[n + str(i)] for n in "afgn" for i in (0, 1)]
    for made in other.started:
        if not any(made is one for one in waited):
            made.wait_send()
    for made in writes:
        made.wait()


def hand_out(output, input_grad, done_hbm, ends, *rest):
    targets, norms, heads = rest[:7], rest[7], rest[8]
    held, done, sems = rest[9:16], rest[16], rest[17]
    out, igrad, query, keyval, wide, gateup, down = held
    reads = [
        pltpu.make_async_copy(a, b, sems.at[i])
        for i, (a, b) in enumerate(((done_hbm, done), (input_grad, igrad), (output, out)))
    ]
    for made in reads:
        made.start()
    writes = [
        pltpu.make_async_copy(a, b, sems.at[3 + i]) for i, (a, b) in enumerate(zip(held, targets))
    ]
    norms[...] = ends[0:4, 0:40]
    heads[...] = ends[8:10, 0:16]
    reads[0].wait()
    gateup[0] = done[:40, GATEUP:DOWN]
    gateup[1] = done[40:, GATEUP:DOWN]
    writes[5].start()
    down[...] = unfold(done[:, DOWN:WIRE])
    writes[6].start()
    keyval[:, 0:256] = unfold(done[:, KV:QUERY])
    keyval[:, 256:512] = unfold(done[:, EXTRA:OUT])
    query[...] = unfold(done[:, QUERY:EXTRA])
    wide[...] = unfold(done[:, OUT:GATEUP])
    for i in (2, 3, 4):
        writes[i].start()
    reads[1].wait()
    writes[1].start()
    reads[2].wait()
    writes[0].start()
    for made in writes:
        made.wait()


def anywhere():
    return pl.BlockSpec(memory_space=pl.ANY)


def vmem():
    return pl.BlockSpec(memory_space=pltpu.VMEM)


def ring_buffers(cols):
    return [
        pltpu.VMEM((2, 2, 80, cols), LOW),
        pltpu.VMEM((2, 4, 80, cols), LOW),
        pltpu.VMEM((4, 80, cols), LOW),
        pltpu.VMEM((80, cols), LOW),
        pltpu.VMEM((2, 80, cols), LOW),
    ]


def shards(
    tokens, segments, cotangent, w_query, w_keyval, w_out, w_gateup, w_down, norm_gains, head_gains
):
    output, input_grad, done, ends = pl.pallas_call(
        layer_kernel,
        out_shape=(
            jax.ShapeDtypeStruct((ROWS, D), LOW),
            jax.ShapeDtypeStruct((ROWS, D), F32),
            jax.ShapeDtypeStruct((80, WIRE), F32),
            jax.ShapeDtypeStruct((16, 128), F32),
        ),
        in_specs=[anywhere(), vmem(), anywhere()] + [vmem()] * 7,
        out_specs=(anywhere(),) * 3 + (vmem(),),
        scratch_shapes=[
            *(pltpu.VMEM(*shape) for shape in SCRATCH.values()),
            *ring_buffers(SET_COLS[0]),
            *ring_buffers(SET_COLS[1]),
            pltpu.SemaphoreType.DMA((64,)),
            pltpu.SemaphoreType.DMA((64,)),
            pltpu.SemaphoreType.DMA((128,)),
            pltpu.SemaphoreType.DMA((128,)),
            pltpu.SemaphoreType.DMA((40,)),
            pltpu.SemaphoreType.DMA((40,)),
            pltpu.VMEM((ROWS, D), LOW),
            pltpu.VMEM((ROWS, D), LOW),
            pltpu.VMEM((ROWS, D), LOW),
            pltpu.VMEM((ROWS, D), F32),
            pltpu.VMEM((80, WIRE), F32),
            pltpu.SemaphoreType.DMA((16,)),
        ],
        compiler_params=pltpu.CompilerParams(
            collective_id=0, has_side_effects=True, vmem_limit_bytes=VMEM_BYTES
        ),
    )(
        tokens[0],
        segments,
        cotangent[0],
        w_query,
        w_keyval,
        w_out.T,
        w_gateup,
        w_down.T,
        norm_gains,
        head_gains,
    )
    results = pl.pallas_call(
        hand_out,
        out_shape=(
            jax.ShapeDtypeStruct((ROWS, D), LOW),
            jax.ShapeDtypeStruct((ROWS, D), F32),
            jax.ShapeDtypeStruct((40, 512), F32),
            jax.ShapeDtypeStruct((40, 512), F32),
            jax.ShapeDtypeStruct((40, 512), F32),
            jax.ShapeDtypeStruct((2, 40, FFH), F32),
            jax.ShapeDtypeStruct((40, FFH), F32),
            jax.ShapeDtypeStruct((4, 40), F32),
            jax.ShapeDtypeStruct((2, 16), F32),
        ),
        in_specs=[anywhere()] * 3 + [vmem()],
        out_specs=(anywhere(),) * 7 + (vmem(),) * 2,
        scratch_shapes=[
            pltpu.VMEM((ROWS, D), LOW),
            pltpu.VMEM((ROWS, D), F32),
            pltpu.VMEM((40, 512), F32),
            pltpu.VMEM((40, 512), F32),
            pltpu.VMEM((40, 512), F32),
            pltpu.VMEM((2, 40, FFH), F32),
            pltpu.VMEM((40, FFH), F32),
            pltpu.VMEM((80, WIRE), F32),
            pltpu.SemaphoreType.DMA((10,)),
        ],
        compiler_params=pltpu.CompilerParams(vmem_limit_bytes=VMEM_BYTES),
    )(output, input_grad, done, ends)
    return (
        results[0][None],
        results[1][None],
        results[2],
        results[3],
        results[4].T,
        results[5],
        results[6].T,
        results[7],
        results[8],
    )


def solution(mesh):
    placed = (
        P("dp", "ctx", None),
        P("dp", "ctx"),
        P("dp", "ctx", None),
        P("dp", "tensor"),
        P("dp", None),
        P("tensor", "dp"),
        P(None, "dp", "tensor"),
        P("tensor", "dp"),
        P(None, "dp"),
        P(None, "dp"),
    )
    return jax.shard_map(
        shards,
        mesh=mesh,
        in_specs=placed,
        out_specs=(
            P("dp", "ctx", None),
            P("dp", "ctx", None),
            P("dp", "tensor"),
            P("dp", None),
            P("tensor", "dp"),
            P(None, "dp", "tensor"),
            P("tensor", "dp"),
            P(None, "dp"),
            P(None, "dp"),
        ),
        check_vma=False,
    )
```

```python
import math
import types

import jax
import jax.numpy as jnp
from jax import lax
from jax.experimental import pallas as pl
from jax.experimental.pallas import tpu as pltpu
from jax.sharding import PartitionSpec as P

WINDOW = 512
EPSILON = 1e-06
MESH = pl.DeviceIdType.MESH
VMEM_BYTES = 60 * 1024 * 1024

KV, QUERY, OUT, GATEUP, DOWN, WIRE = 0, 128, 384, 640, 1664, 2176
GATHERS = (
    ((0, 128), (128, 128)),
    ((256, 128), (384, 256)),
    ((640, 512), (1152, 512)),
    ((1664, 256), (1920, 256)),
)
SCATTERS = (
    ("s3", (1664, 256), (1920, 256)),
    ("sa", (640, 256), (896, 256)),
    ("sb", (1152, 256), (1408, 256)),
    ("s1", (384, 128), (512, 128)),
    ("sq", (128, 128), (256, 128)),
    ("sk", (0, 128), None),
)
SET_COLS = (1152, 1024)
CUT = 48
ROWS, D, HD, FFH = 512, 640, 256, 1024
SCALE = 1.0 / math.sqrt(HD)
LOW = jnp.bfloat16
F32 = jnp.float32
NN, NT, TN = ((1,), (0,)), ((1,), (1,)), ((0,), (0,))


def place(u):
    return lax.rem(u + 8, 4)


class Wires:
    def __init__(self, send, recv):
        self.send, self.recv, self.used = send, recv, 0
        self.started = []

    def copy(self, src, dst, target):
        index = self.used
        self.used += 1
        made = pltpu.make_async_remote_copy(
            src_ref=src,
            dst_ref=dst,
            send_sem=self.send.at[index],
            recv_sem=self.recv.at[index],
            device_id=target,
            device_id_type=MESH,
        )
        made.start()
        self.started.append(made)
        return made

    def drain(self):
        for made in self.started:
            made.wait_send()
        self.started = []


class Ring:
    def __init__(self, first, x, y):
        self.first = first
        self.f, self.s = (x, y) if first == "x" else (y, x)

    def slot(self, ref, f, s, *rest):
        return ref.at[(s, f) + rest] if self.first == "x" else ref.at[(f, s) + rest]

    def index(self, f, s):
        return (s, f) if self.first == "x" else (f, s)

    def to_f(self, step):
        f = place(self.f + step)
        return {"dp": self.s * 4 + f} if self.first == "x" else {"dp": f * 4 + self.s}

    def to_s(self, step):
        s = place(self.s + step)
        return {"dp": s * 4 + self.f} if self.first == "x" else {"dp": self.f * 4 + s}


class Gather:
    def __init__(self, ring, wires, shard, whole, direct, start, width):
        self.ring, self.wires, self.shard, self.whole = ring, wires, shard, whole
        self.direct = direct
        self.cols = pl.ds(start, width)

    def one(self):
        r, c = self.ring, self.cols
        src = self.shard.at[:, c]
        dst = r.slot(self.whole, r.f, r.s, slice(None), c)
        self.a = self.wires.copy(src, dst, r.to_f(1))
        self.b = self.wires.copy(src, dst, r.to_f(-1))
        if self.direct:
            self.c = self.wires.copy(src, dst, r.to_f(2))

    def two(self):
        r, c = self.ring, self.cols
        self.a.wait_recv()
        part = r.slot(self.whole, place(r.f - 1), r.s, pl.ds(0, CUT), c)
        a = self.wires.copy(part, part, r.to_f(1))
        self.b.wait_recv()
        part = r.slot(self.whole, place(r.f + 1), r.s, pl.ds(CUT, 80 - CUT), c)
        b = self.wires.copy(part, part, r.to_f(-1))
        self.a, self.b = a, b

    def three(self):
        r, c = self.ring, self.cols
        self.a.wait_recv()
        self.b.wait_recv()
        if self.direct:
            self.c.wait_recv()
        part = r.slot(self.whole, slice(None), r.s, slice(None), c)
        self.a = self.wires.copy(part, part, r.to_s(1))
        self.b = self.wires.copy(part, part, r.to_s(-1))

    def four(self):
        r, c = self.ring, self.cols
        self.a.wait_recv()
        part = r.slot(self.whole, pl.ds(0, 2), place(r.s - 1), slice(None), c)
        a = self.wires.copy(part, part, r.to_s(1))
        self.b.wait_recv()
        part = r.slot(self.whole, pl.ds(2, 2), place(r.s + 1), slice(None), c)
        b = self.wires.copy(part, part, r.to_s(-1))
        self.a, self.b = a, b

    def finish(self):
        self.a.wait_recv()
        self.b.wait_recv()


def added(*terms):
    total = terms[0].astype(jnp.float32)
    for term in terms[1:]:
        total = total + term.astype(jnp.float32)
    return total


class Scatter:
    def __init__(self, ring, wires, grads, bufs, final, z, start, width, offset, far):
        self.ring, self.wires, self.grads, self.final, self.z = ring, wires, grads, final, z
        self.r1, self.r2, self.sums, self.r3, self.r4 = bufs
        self.cols = pl.ds(start, width)
        self.near = pl.ds(offset, width)
        self.far, self.start = far, start

    def one(self):
        r, c, n = self.ring, self.cols, self.near
        far = place(r.s + 2)
        self.a = self.wires.copy(
            r.slot(self.grads, pl.ds(0, 2), far, slice(None), c), self.r1.at[0, :, :, n], r.to_s(1)
        )
        self.b = self.wires.copy(
            r.slot(self.grads, pl.ds(2, 2), far, slice(None), c), self.r1.at[1, :, :, n], r.to_s(-1)
        )

    def two(self):
        r, c, n = self.ring, self.cols, self.near
        after, before = place(r.s + 1), place(r.s - 1)
        self.a.wait_recv()
        for i in range(2):
            at = r.index(i, after) + (slice(None), c)
            self.grads[at] = added(self.grads[at], self.r1[0, i, :, n]).astype(jnp.bfloat16)
        a = self.wires.copy(
            r.slot(self.grads, slice(None), after, slice(None), c), self.r2.at[0, :, :, n], r.to_s(1)
        )
        self.b.wait_recv()
        for i in range(2):
            at = r.index(2 + i, before) + (slice(None), c)
            self.grads[at] = added(self.grads[at], self.r1[1, i, :, n]).astype(jnp.bfloat16)
        b = self.wires.copy(
            r.slot(self.grads, slice(None), before, slice(None), c),
            self.r2.at[1, :, :, n],
            r.to_s(-1),
        )
        self.a, self.b = a, b

    def three(self):
        r, c, n = self.ring, self.cols, self.near
        self.a.wait_recv()
        self.b.wait_recv()
        for i in range(4):
            at = r.index(i, r.s) + (slice(None), c)
            self.sums[i, :, n] = added(
                self.grads[at], self.r2[0, i, :, n], self.r2[1, i, :, n]
            ).astype(jnp.bfloat16)
        far = place(r.f + 2)
        self.a = self.wires.copy(
            self.sums.at[far, pl.ds(0, CUT), n], self.r3.at[pl.ds(0, CUT), n], r.to_f(1)
        )
        self.b = self.wires.copy(
            self.sums.at[far, pl.ds(CUT, 80 - CUT), n],
            self.r3.at[pl.ds(CUT, 80 - CUT), n],
            r.to_f(-1),
        )

    def four(self):
        r, n = self.ring, self.near
        after, before = place(r.f + 1), place(r.f - 1)
        top, low = pl.ds(0, CUT), pl.ds(CUT, 80 - CUT)
        self.a.wait_recv()
        self.sums[after, top, n] = added(self.sums[after, top, n], self.r3[top, n]).astype(
            jnp.bfloat16
        )
        a = self.wires.copy(self.sums.at[after, :, n], self.r4.at[0, :, n], r.to_f(1))
        self.b.wait_recv()
        self.sums[before, low, n] = added(self.sums[before, low, n], self.r3[low, n]).astype(
            jnp.bfloat16
        )
        b = self.wires.copy(self.sums.at[before, :, n], self.r4.at[1, :, n], r.to_f(-1))
        self.a, self.b = a, b

    def five(self):
        r, c, n = self.ring, self.cols, self.near
        self.a.wait_recv()
        self.b.wait_recv()
        self.final[self.z, :, c] = added(
            self.sums[r.f, :, n], self.r4[0, :, n], self.r4[1, :, n]
        ).astype(jnp.bfloat16)
        part = self.final.at[self.z, :, c]
        self.zs = [self.wires.copy(part, part, {"ctx": place(self.z + k)}) for k in (1, 3, 2)]
        if self.far is not None:
            part = self.final.at[self.z, :, pl.ds(self.start, 128)]
            self.zs += [self.wires.copy(part, self.far[0], target) for target in self.far[1]]

    def finish(self):
        for made in self.zs:
            made.wait_recv()


def spot():
    d = lax.axis_index("dp")
    return lax.rem(d, 4), lax.div(d, 4), lax.axis_index("ctx")


def dot(a, b, dims=NN):
    return lax.dot_general(a, b, (dims, ((), ())), preferred_element_type=F32)


def rms(field):
    return lax.rsqrt(jnp.mean(field * field, axis=-1, keepdims=True) + EPSILON)


def norm_back(field, gain, grad):
    r = rms(field)
    hat = field * r
    scaled = grad * gain
    back = r * (scaled - hat * jnp.mean(scaled * hat, axis=-1, keepdims=True))
    return back, jnp.sum(grad * hat, axis=0, keepdims=True)


def turn(field, cos, sin):
    a, b = field[:, :128], field[:, 128:]
    return jnp.concatenate([a * cos - b * sin, b * cos + a * sin], axis=1)


def turn_back(field, cos, sin):
    a, b = field[:, :128], field[:, 128:]
    return jnp.concatenate([a * cos + b * sin, b * cos - a * sin], axis=1)


def fold(block):
    half = block.shape[-1] // 2
    return jnp.concatenate([block[..., :half], block[..., half:]], axis=-2)


def unfold(block):
    rows = block.shape[-2] // 2
    return jnp.concatenate([block[..., :rows, :], block[..., rows:, :]], axis=-1)


def iota(shape, axis):
    return lax.broadcasted_iota(jnp.int32, shape, axis)


SCRATCH = dict(
    wire=((80, WIRE), LOW),
    whole=((4, 4, 80, WIRE), LOW),
    tile=((16, 128), F32),
    tile_low=((16, 128), LOW),
    tiles=((4, 4, 16, 128), LOW),
    wq=((D, 512), LOW),
    wkv=((D, HD), LOW),
    wo=((D, 512), LOW),
    wg=((D, FFH), LOW),
    wu=((D, FFH), LOW),
    wd=((D, FFH), LOW),
    gains=((8, D), F32),
    heads=((8, HD), F32),
    dgains=((8, D), F32),
    ends=((16, 16, 128), F32),
    end_snd=((4, 4, 16, 128), LOW),
    end_rcv=((4, 4, 16, 128), LOW),
    end_mid=((4, 16, 128), LOW),
    end_mrc=((4, 16, 128), LOW),
    end_z=((4, 16, 128), LOW),
    end_far=((4, 16, 128), LOW),
    dheads=((8, HD), F32),
    tokh=((ROWS, D), LOW),
    segp=((1, ROWS), jnp.int32),
    lo_col=((ROWS, 128), F32),
    lo_row=((8, ROWS), F32),
    cos=((1024, 128), F32),
    sin=((1024, 128), F32),
    n1=((1024, D), LOW),
    n1t=((D, 1024), LOW),
    kvb=((2, 1024, HD), LOW),
    kvraw=((1024, HD), F32),
    qraw=((4, 256, HD), F32),
    q=((4, 256, HD), LOW),
    o=((ROWS, 512), LOW),
    go=((4, 256, HD), LOW),
    gqr=((ROWS, 512), LOW),
    a=((ROWS, D), F32),
    h=((ROWS, D), F32),
    n2=((ROWS, D), LOW),
    n2t=((D, ROWS), LOW),
    ga=((ROWS, FFH), F32),
    gb=((ROWS, FFH), F32),
    u=((ROWS, FFH), LOW),
    ggu=((ROWS, 2 * FFH), LOW),
    gf=((ROWS, D), LOW),
    gft=((D, ROWS), LOW),
    gal=((ROWS, D), LOW),
    gat=((D, ROWS), LOW),
    gh=((ROWS, D), F32),
    snd=((2, ROWS, D), LOW),
    rcv=((2, ROWS, D), LOW),
    gkv=((2, 1024, HD), F32),
    kvs=((1024, HD), LOW),
    kvr=((1024, HD), LOW),
    hs=((ROWS, HD), LOW),
    hr=((ROWS, HD), LOW),
    gkr=((1024, HD), LOW),
    gko=((ROWS, HD), LOW),
    final=((4, 80, WIRE), LOW),
    far=((4, 80, 128), LOW),
)


ORDER = (
    "w0", "w1", "p1.one", "w2", "p0.one", "p2.one", "w3", "p3.one", "ge.one", "tab", "p1.three",
    "p0.three", "ge.two", "p2.two", "p3.two", "p1.four", "p0.four", "p2.three", "p3.three",
    "c0", "c1", "c2", "mask", "A0", "A1", "c3", "p2.four", "h0", "A2", "A3", "c4", "p3.four",
    "h1", "c6", "F0", "c8", "F1", "c9", "o0", "FB0", "G0", "o1", "P3", "s3.one", "FB1", "PA",
    "sa.one", "PB", "sb.one", "N0", "B0", "s3.two", "G1", "sa.two", "B1", "N1", "sb.two", "B2",
    "B3", "s3.three", "P1", "s1.one", "QS", "V0", "V1", "sa.three", "PQ", "sq.one", "KB",
    "sk.one", "sb.three", "s3.four", "s1.two", "sa.four", "sq.two", "NN0", "sb.four", "s3.five",
    "NN1", "I0", "s1.three", "sk.two", "sa.five", "I1", "sq.three", "EX", "s1.four", "se.one",
    "sb.five", "sk.three", "sq.four", "s3.fin", "s1.five", "se.two", "sa.fin", "sk.four",
    "sq.five", "se.five", "sb.fin", "sk.five", "s1.fin", "sq.fin", "se.fin", "sk.fin",
)


def layer_kernel(
    tok_hbm, seg_row, cot_hbm, wq, wkv, wo, wgu, wd, ng, hg, out_hbm, igrad_hbm, grads_hbm, ends, *rest
):
    names = list(SCRATCH)
    g = types.SimpleNamespace(**dict(zip(names, rest[: len(names)])))
    rest = rest[len(names) :]
    bufs = (rest[0:5], rest[5:10])
    tok, cot, out, igrad, grads, local = rest[16:22]
    tok_read = pltpu.make_async_copy(tok_hbm, tok, local.at[0])
    cot_read = pltpu.make_async_copy(cot_hbm, cot, local.at[1])
    tok_read.start()
    cot_read.start()
    writes = []

    def write(source, target):
        made = pltpu.make_async_copy(source, target, local.at[2 + len(writes)])
        made.start()
        writes.append(made)

    x, y, z = spot()
    core = lax.axis_index("tensor")
    mate = {"tensor": 1 - core}
    rings = (Ring("x", x, y), Ring("y", x, y))
    gather_wires = Wires(rest[10], rest[11])
    scatter_wires = Wires(rest[12], rest[13])
    other = Wires(rest[14], rest[15])
    along_z = [{"ctx": place(z + k)} for k in (1, 3, 2)]
    across = [{"ctx": place(z + k), "tensor": 1 - core} for k in range(4)]
    targets = [r.to_f(k) for r in rings for k in (1, -1, 2)] + along_z + across
    barrier = pltpu.get_barrier_semaphore()
    for target in targets:
        pl.semaphore_signal(barrier, inc=1, device_id=target, device_id_type=MESH)

    jobs, held = {}, {}

    def job(name):
        def keep(work):
            jobs[name] = work
            return work

        return keep

    def steps(name, members, methods):
        for method in methods:
            jobs[name + "." + method] = lambda method=method: [getattr(m, method)() for m in members]

    for number, piece in enumerate(GATHERS):
        made = [
            Gather(ring, gather_wires, g.wire, g.whole, number < 2, *piece[i])
            for i, ring in enumerate(rings)
        ]
        steps("p%d" % number, made, ("one", "two", "three", "four", "finish"))
        if number == 1:
            p1 = made
    offsets = [0, 0]
    for name, *piece in SCATTERS:
        made = []
        for i, ring in enumerate(rings):
            if piece[i] is None:
                continue
            start, width = piece[i]
            far = (g.far.at[z], across) if start == KV else None
            made.append(
                Scatter(ring, scatter_wires, g.whole, bufs[i], g.final, z, start, width, offsets[i], far)
            )
            offsets[i] += width
        steps(name, made, ("one", "two", "three", "four", "five", "finish"))

    halves = [slice(0, 256), slice(256, 512)]

    def swap(name, number, rows, value):
        g.snd[number, rows] = value.astype(LOW)
        held[name] = other.copy(g.snd.at[number, rows], g.rcv.at[number, rows], mate)

    def total(name, number, rows):
        held[name].wait_recv()
        held[name].wait_send()
        return g.snd[number, rows].astype(F32) + g.rcv[number, rows].astype(F32)

    @job("w0")
    def _():
        mine = wkv[:, pl.ds(pl.multiple_of(core * HD, HD), HD)]
        g.wire[:, KV:QUERY] = fold(mine.astype(F32)).astype(LOW)
        g.wire[:, QUERY:OUT] = fold(wq[...].astype(F32)).astype(LOW)
        g.whole[y, x, :, KV:OUT] = g.wire[:, KV:OUT]
        g.tile[...] = jnp.zeros((16, 128), F32)
        g.tile[0:4, 0:40] = ng[...].astype(F32)
        g.tile[8:10, 0:16] = hg[...].astype(F32)
        g.tile_low[...] = g.tile[...].astype(LOW)
        pl.semaphore_wait(barrier, len(targets))

    @job("ge.one")
    def _():
        held["ge"] = [
            other.copy(g.tile_low, g.tiles.at[y, x], {"dp": y * 4 + place(x + k)}) for k in (1, 3, 2)
        ]

    @job("ge.two")
    def _():
        for made in held["ge"]:
            made.wait_recv()
        g.tiles[y, x] = g.tile_low[...]
        held["ge"] = [
            other.copy(g.tiles.at[y], g.tiles.at[y], {"dp": place(y + k) * 4 + x}) for k in (1, 3, 2)
        ]

    @job("w1")
    def _():
        held["seg"] = other.copy(seg_row, g.segp, {"ctx": place(z + 1)})
        tok_read.wait()
        held["tok"] = other.copy(tok, g.tokh, {"ctx": place(z + 1)})
        g.wire[:, OUT:GATEUP] = fold(wo[...].astype(F32)).astype(LOW)
        g.whole[y, x, :, OUT:GATEUP] = g.wire[:, OUT:GATEUP]

    @job("w2")
    def _():
        both = jnp.concatenate([wgu[0].astype(F32), wgu[1].astype(F32)], axis=0)
        g.wire[:, GATEUP:DOWN] = both.astype(LOW)
        g.whole[y, x, :, GATEUP:DOWN] = g.wire[:, GATEUP:DOWN]

    @job("w3")
    def _():
        g.wire[:, DOWN:WIRE] = fold(wd[...].astype(F32)).astype(LOW)
        g.whole[y, x, :, DOWN:WIRE] = g.wire[:, DOWN:WIRE]

    @job("tab")
    def _():
        rates = jnp.exp(iota((1, 128), 1).astype(F32) * (-2.0 * math.log(10000.0) / HD))
        fine = iota((128, 128), 0).astype(F32) * rates
        fine_cos, fine_sin = jnp.cos(fine), jnp.sin(fine)
        coarse = (iota((8, 128), 0) * 128 + (z * ROWS - ROWS)).astype(F32) * rates
        coarse_cos, coarse_sin = jnp.cos(coarse), jnp.sin(coarse)
        for i in range(8):
            cc, cs = coarse_cos[i : i + 1], coarse_sin[i : i + 1]
            g.cos[128 * i : 128 * i + 128] = fine_cos * cc - fine_sin * cs
            g.sin[128 * i : 128 * i + 128] = fine_sin * cc + fine_cos * cs
        g.dgains[...] = jnp.zeros((8, D), F32)
        g.dheads[...] = jnp.zeros((8, HD), F32)
        g.gkv[...] = jnp.zeros((2, 1024, HD), F32)
        g.ends[...] = jnp.zeros((16, 16, 128), F32)

    @job("mask")
    def _():
        held["seg"].wait_recv()
        own_ids, prior_ids = seg_row[...].astype(F32), g.segp[...].astype(F32)
        column = jnp.transpose(jnp.broadcast_to(own_ids, (128, ROWS)))[:, 0:1]
        below_prior = jnp.sum((prior_ids < column).astype(F32), axis=1, keepdims=True)
        below_prior = jnp.where(z == 0, float(ROWS), below_prior)
        below_own = jnp.sum((own_ids < column).astype(F32), axis=1, keepdims=True)
        lowest = jnp.maximum(below_prior + below_own, iota((ROWS, 1), 0).astype(F32) + 1.0)
        lowest = jnp.broadcast_to(lowest, (ROWS, 128))
        g.lo_col[...] = lowest
        g.lo_row[...] = jnp.transpose(lowest)[0:8]

    def assemble(first, second, start, width, w=128):
        def one(i):
            at = i * w
            block = g.whole[:, :, :, pl.ds(start + at, w)].astype(F32)
            first[:, pl.ds(at, w)] = block[:, :, :40].reshape(D, w).astype(LOW)
            if second is None:
                first[:, pl.ds(at + width, w)] = block[:, :, 40:].reshape(D, w).astype(LOW)
            else:
                second[:, pl.ds(at, w)] = block[:, :, 40:].reshape(D, w).astype(LOW)

        for i in range(width // w):
            one(i)

    def gain(i):
        return g.gains[i : i + 1]

    def keys_of(start, normed):
        at = slice(start, start + 256)
        low = normed.astype(LOW)
        g.n1[at] = low
        raw = dot(low, g.wkv[...])
        g.kvraw[at] = raw
        turned = turn(raw * rms(raw) * g.heads[1:2], g.cos[at], g.sin[at])
        g.kvb[core, at] = jnp.where(core == 0, turned, raw).astype(LOW)
        g.n1t[:, at] = jnp.transpose(normed).astype(LOW)

    @job("c0")
    def _():
        jobs["p0.finish"]()
        for made in held["ge"]:
            made.wait_recv()
        for d in range(16):
            block = g.tiles[d // 4, d % 4].astype(F32)
            g.gains[:, 40 * d : 40 * d + 40] = block[0:8, 0:40]
            g.heads[:, 16 * d : 16 * d + 16] = block[8:16, 0:16]
        assemble(g.wkv, None, KV, 128)
        for rows in halves:
            block = tok[rows].astype(F32)
            keys_of(ROWS + rows.start, block * rms(block) * gain(0))
        part = g.kvb.at[core, pl.ds(ROWS, ROWS)]
        held["kv1"] = other.copy(part, part, mate)

    @job("c1")
    def _():
        held["tok"].wait_recv()
        for rows in halves:
            block = g.tokh[rows].astype(F32)
            keys_of(rows.start, block * rms(block) * gain(0))
        part = g.kvb.at[core, pl.ds(0, ROWS)]
        held["kv2"] = other.copy(part, part, mate)

    @job("c2")
    def _():
        p1[0].finish()
        assemble(g.wq, None, QUERY, 256)
        for i in range(2):
            at = slice(ROWS + 256 * i, ROWS + 256 * i + 256)
            raw = dot(g.n1[at], g.wq[...])
            for h in range(2):
                part = raw[:, HD * h : HD * h + HD]
                turned = turn(part * rms(part) * g.heads[0:1], g.cos[at], g.sin[at]).astype(LOW)
                for j in range(2):
                    g.qraw[2 * i + j, 128 * h : 128 * h + 128] = part[128 * j : 128 * j + 128]
                    g.q[2 * i + j, 128 * h : 128 * h + 128] = turned[128 * j : 128 * j + 128]

    def twice(block, axis):
        return jnp.concatenate([block, block], axis=axis)

    def attend(b):
        start = b * 128
        keys, values = g.kvb[0, pl.ds(start, D)], g.kvb[1, pl.ds(start, D)]
        scores = dot(g.q[b], keys, NT) * SCALE
        lowest = twice(g.lo_col[pl.ds(start, 128), 0:1], 0) - float(b * 128)
        place_k = iota((256, D), 1).astype(F32)
        highest = (iota((256, 1), 0) & 127).astype(F32) + float(WINDOW)
        scores = jnp.where((place_k >= lowest) & (place_k <= highest), scores, -1e30)
        expo = jnp.exp(scores - jnp.max(scores, axis=-1, keepdims=True))
        probs = (expo / jnp.sum(expo, axis=-1, keepdims=True)).astype(LOW)
        mixed = dot(probs, values).astype(LOW)
        g.o[pl.ds(start, 128), 0:HD] = mixed[:128]
        g.o[pl.ds(start, 128), HD : 2 * HD] = mixed[128:]

    @job("A0")
    def _():
        held["kv1"].wait_recv()
        held["kv2"].wait_recv()
        attend(0)

    for b in (1, 2, 3):
        jobs["A%d" % b] = lambda b=b: attend(b)

    @job("c3")
    def _():
        p1[1].finish()
        assemble(g.wo, None, OUT, 256)
        swap("a0", 0, halves[0], dot(g.o[halves[0]], g.wo[...], NT))

    @job("c4")
    def _():
        swap("a1", 0, halves[1], dot(g.o[halves[1]], g.wo[...], NT))

    def hidden_rows(i):
        rows = halves[i]
        branch = total("a%d" % i, 0, rows)
        g.a[rows] = branch
        hidden = tok[rows].astype(F32) + branch * rms(branch) * gain(1)
        g.h[rows] = hidden
        normed = hidden * rms(hidden) * gain(2)
        g.n2[rows] = normed.astype(LOW)
        g.n2t[:, rows] = jnp.transpose(normed).astype(LOW)

    c0, c1 = math.sqrt(2.0 / math.pi), 0.044715

    def forward_rows(k):
        rows = halves[k]

        def one(i):
            cols = pl.ds(i * 256, 256)
            gate = dot(g.n2[rows], g.wg[:, cols])
            up = dot(g.n2[rows], g.wu[:, cols])
            square = gate * gate
            t = jnp.tanh(c0 * gate * (1.0 + c1 * square))
            act = 0.5 * gate * (1.0 + t)
            slope = 0.5 * (1.0 + t) + 0.5 * gate * (1.0 - t * t) * (c0 * (1.0 + 3.0 * c1 * square))
            g.ga[rows, cols] = act
            g.gb[rows, cols] = up * slope
            g.u[rows, cols] = (act * up).astype(LOW)

        for i in range(4):
            one(i)

    @job("c6")
    def _():
        jobs["p2.finish"]()
        assemble(g.wg, g.wu, GATEUP, FFH)

    @job("c8")
    def _():
        jobs["p3.finish"]()
        gather_wires.drain()
        assemble(g.wd, None, DOWN, 512)
        swap("f0", 1, halves[0], dot(g.u[halves[0]], g.wd[...], NT))

    @job("c9")
    def _():
        swap("f1", 1, halves[1], dot(g.u[halves[1]], g.wd[...], NT))

    def output_rows(i):
        rows = halves[i]
        if i == 0:
            cot_read.wait()
        feed = total("f%d" % i, 1, rows)
        out[rows] = (g.h[rows] + feed * rms(feed) * gain(3)).astype(LOW)
        back, slope = norm_back(feed, gain(3), cot[rows].astype(F32))
        g.dgains[3:4] += slope
        g.gf[rows] = back.astype(LOW)
        g.gft[:, rows] = jnp.transpose(back).astype(LOW)
        write(out.at[rows], out_hbm.at[rows])

    def put(left, right, start, begin, end, gap, w=256):
        def one(i):
            at = i * w
            first = dot(left[...], right[:, pl.ds(at, w)]).reshape(16, 40, w)
            second = dot(left[...], right[:, pl.ds(at + gap, w)]).reshape(16, 40, w)
            block = jnp.concatenate([first, second], axis=1).astype(LOW)
            g.whole[:, :, :, pl.ds(start + at, w)] = block.reshape(4, 4, 80, w)

        for i in range(begin // w, end // w):
            one(i)

    jobs["P3"] = lambda: put(g.gft, g.u, DOWN, 0, 512, 512)
    jobs["PA"] = lambda: put(g.n2t, g.ggu, GATEUP, 0, 512, FFH)
    jobs["PB"] = lambda: put(g.n2t, g.ggu, GATEUP, 512, 1024, FFH)
    jobs["P1"] = lambda: put(g.gat, g.o, OUT, 0, 256, 256)
    jobs["PQ"] = lambda: put(g.n1t.at[:, ROWS:], g.gqr, QUERY, 0, 256, 256)

    def backward_rows(k):
        rows = halves[k]

        def one(i):
            at = i * 256
            cols = pl.ds(at, 256)
            inner = dot(g.gf[rows], g.wd[:, cols])
            g.ggu[rows, cols] = (inner * g.gb[rows, cols]).astype(LOW)
            g.ggu[rows, pl.ds(at + FFH, 256)] = (inner * g.ga[rows, cols]).astype(LOW)

        for i in range(4):
            one(i)

    def second_rows(i):
        rows = halves[i]
        part = dot(g.ggu[rows, 0:FFH], g.wg[...], NT) + dot(g.ggu[rows, FFH:], g.wu[...], NT)
        swap("g%d" % i, 0, rows, part)

    def norm_rows(i):
        rows = halves[i]
        back, slope = norm_back(g.h[rows], gain(2), total("g%d" % i, 0, rows))
        g.dgains[2:3] += slope
        hidden = cot[rows].astype(F32) + back
        g.gh[rows] = hidden
        back, slope = norm_back(g.a[rows], gain(1), hidden)
        g.dgains[1:2] += slope
        g.gat[:, rows] = jnp.transpose(back).astype(LOW)
        grad = dot(back.astype(LOW), g.wo[...]).astype(LOW)
        for j in range(2):
            for h in range(2):
                g.go[2 * i + j, 128 * h : 128 * h + 128] = grad[
                    128 * j : 128 * j + 128, HD * h : HD * h + HD
                ]

    for i in range(2):
        jobs["h%d" % i] = lambda i=i: hidden_rows(i)
        jobs["F%d" % i] = lambda i=i: forward_rows(i)
        jobs["o%d" % i] = lambda i=i: output_rows(i)
        jobs["FB%d" % i] = lambda i=i: backward_rows(i)
        jobs["G%d" % i] = lambda i=i: second_rows(i)
        jobs["N%d" % i] = lambda i=i: norm_rows(i)

    def attend_back(b):
        start = b * 128
        keys, values = g.kvb[0, pl.ds(start, D)], g.kvb[1, pl.ds(start, D)]
        queries, grad = g.q[b], g.go[b]
        scores = dot(keys, queries, NT) * SCALE
        lowest = twice(g.lo_row[0:1, pl.ds(start, 128)], 1) - float(b * 128)
        place_k = iota((D, 256), 0).astype(F32)
        highest = (iota((1, 256), 1) & 127).astype(F32) + float(WINDOW)
        scores = jnp.where((place_k >= lowest) & (place_k <= highest), scores, -1e30)
        expo = jnp.exp(scores - jnp.max(scores, axis=0, keepdims=True))
        probs = expo * (1.0 / jnp.sum(expo, axis=0, keepdims=True))
        grad_probs = dot(values, grad, NT)
        spread = jnp.sum(probs * grad_probs, axis=0, keepdims=True)
        grad_scores = (probs * (grad_probs - spread)).astype(LOW)
        g.gkv[0, pl.ds(start, D)] += dot(grad_scores, queries) * SCALE
        g.gkv[1, pl.ds(start, D)] += dot(probs.astype(LOW), grad)
        grad_q = dot(grad_scores, keys, TN) * SCALE
        at = pl.ds(ROWS + start, 128)
        grad_q = turn_back(grad_q, twice(g.cos[at], 0), twice(g.sin[at], 0))
        back, slope = norm_back(g.qraw[b], g.heads[0:1], grad_q)
        g.dheads[0:1] += slope
        g.gqr[pl.ds(start, 128), 0:HD] = back[:128].astype(LOW)
        g.gqr[pl.ds(start, 128), HD : 2 * HD] = back[128:].astype(LOW)

    def back_block(b):
        attend_back(b)
        if b in (1, 3):
            rows = pl.ds(0, 256) if b == 1 else pl.ds(256, 768)
            g.kvs[rows] = g.gkv[1 - core, rows].astype(LOW)
            held["kvx%d" % (b // 2)] = other.copy(g.kvs.at[rows], g.kvr.at[rows], mate)

    for b in range(4):
        jobs["B%d" % b] = lambda b=b: back_block(b)

    def summed_rows(i):
        rows = slice(0, 256) if i == 0 else slice(256, 1024)
        held["kvx%d" % i].wait_recv()
        g.gkv[core, rows] = added(g.gkv[core, rows], g.kvr[rows])
        g.hs[halves[i]] = g.gkv[core, halves[i]].astype(LOW)
        held["ha%d" % i] = other.copy(
            g.hs.at[halves[i]], g.hr.at[halves[i]], {"ctx": place(z - 1)}
        )

    def keys_back(start, grad):
        at = slice(start, start + 256)
        turned = turn_back(grad, g.cos[at], g.sin[at])
        back, slope = norm_back(g.kvraw[at], g.heads[1:2], turned)
        return jnp.where(core == 0, back, grad).astype(LOW), jnp.where(core == 0, slope, 0.0)

    @job("KB")
    def _():
        for start in range(0, 1024, 256):
            low, slope = keys_back(start, g.gkv[core, start : start + 256])
            g.dheads[1:2] += slope
            g.gkr[start : start + 256] = low
        put(g.n1t, g.gkr, KV, 0, 128, 128, w=128)

    @job("QS")
    def _():
        for rows in halves:
            g.a[rows] = dot(g.gqr[rows], g.wq[...], NT)

    def first_rows(i):
        rows = halves[i]
        held["ha%d" % i].wait_recv()
        start = ROWS + rows.start
        grad = added(g.gkv[core, start : start + 256], g.hr[rows])
        low, _ = keys_back(start, grad)
        swap("n%d" % i, 1, rows, g.a[rows] + dot(low, g.wkv[...], NT))

    def input_rows(i):
        rows = halves[i]
        back, slope = norm_back(tok[rows].astype(F32), gain(0), total("n%d" % i, 1, rows))
        g.dgains[0:1] += slope
        igrad[rows] = g.gh[rows] + back
        write(igrad.at[rows], igrad_hbm.at[rows])

    for i in range(2):
        jobs["V%d" % i] = lambda i=i: summed_rows(i)
        jobs["NN%d" % i] = lambda i=i: first_rows(i)
        jobs["I%d" % i] = lambda i=i: input_rows(i)

    @job("EX")
    def _():
        for d in range(16):
            g.ends[d, 0:8, 0:40] = g.dgains[:, 40 * d : 40 * d + 40]
            g.ends[d, 8:16, 0:16] = g.dheads[:, 16 * d : 16 * d + 16]
        g.end_snd[...] = g.ends[...].astype(LOW).reshape(4, 4, 16, 128)

    @job("se.one")
    def _():
        held["se"] = [
            other.copy(g.end_snd.at[place(y + k)], g.end_rcv.at[y], {"dp": place(y + k) * 4 + x})
            for k in (1, 3, 2)
        ]

    @job("se.two")
    def _():
        for made in held["se"]:
            made.wait_recv()
        g.end_rcv[y] = g.end_snd[y]
        g.end_mid[...] = added(*(g.end_rcv[i] for i in range(4))).astype(LOW)
        held["se"] = [
            other.copy(g.end_mid.at[place(x + k)], g.end_mrc.at[x], {"dp": y * 4 + place(x + k)})
            for k in (1, 3, 2)
        ]

    @job("se.five")
    def _():
        for made in held["se"]:
            made.wait_recv()
        g.end_mrc[x] = g.end_mid[x]
        g.end_z[z] = added(*(g.end_mrc[i] for i in range(4))).astype(LOW)
        held["se"] = [other.copy(g.end_z.at[z], g.end_z.at[z], target) for target in along_z] + [
            other.copy(g.end_z.at[z], g.end_far.at[z], target) for target in across
        ]

    @job("se.fin")
    def _():
        for made in held["se"]:
            made.wait_recv()
        own = added(*(g.end_z[i] for i in range(4)))
        far = added(*(g.end_far[i] for i in range(4)))
        ends[0:8] = own[0:8]
        ends[8:16] = own[8:16] + far[8:16]

    def put_final(name, source, start, at, width):
        def work():
            jobs[name + ".finish"]()
            cols = pl.ds(start, width)
            grads[:, at : at + width] = added(*(source[i, :, cols] for i in range(4)))
            write(grads.at[:, pl.ds(at, width)], grads_hbm.at[:, pl.ds(at, width)])

        jobs[name + ".fin"] = work

    put_final("s3", g.final, DOWN, DOWN, 512)
    put_final("sa", g.final, GATEUP, GATEUP, 512)
    put_final("sb", g.final, GATEUP + 512, GATEUP + 512, 512)
    put_final("s1", g.final, OUT, OUT, 256)

    put_final("sq", g.final, QUERY, QUERY, 256)

    @job("sk.fin")
    def _():
        jobs["sk.finish"]()
        own = added(*(g.final[i, :, KV:QUERY] for i in range(4)))
        far = added(*(g.far[i] for i in range(4)))
        grads[:, 0:128] = jnp.where(core == 0, own, far)
        grads[:, WIRE : WIRE + 128] = jnp.where(core == 0, far, own)
        for cols in (pl.ds(0, 128), pl.ds(WIRE, 128)):
            write(grads.at[:, cols], grads_hbm.at[:, cols])

    for name in ORDER:
        jobs[name]()
    scatter_wires.drain()
    waited = [held[n + str(i)] for n in "afgn" for i in (0, 1)]
    for made in other.started:
        if not any(made is one for one in waited):
            made.wait_send()
    for made in writes:
        made.wait()


def hand_out(output, input_grad, done, ends, out, igrad, query, keyval, wide, gateup, down, norms, heads):
    out[...] = output[...]
    igrad[...] = input_grad[...]
    keyval[:, 0:256] = unfold(done[:, KV:QUERY])
    keyval[:, 256:512] = unfold(done[:, WIRE : WIRE + 128])
    query[...] = unfold(done[:, QUERY:OUT])
    wide[...] = unfold(done[:, OUT:GATEUP])
    gateup[0] = done[:40, GATEUP:DOWN]
    gateup[1] = done[40:, GATEUP:DOWN]
    down[...] = unfold(done[:, DOWN:WIRE])
    norms[...] = ends[0:4, 0:40]
    heads[...] = ends[8:10, 0:16]


def anywhere():
    return pl.BlockSpec(memory_space=pl.ANY)


def vmem():
    return pl.BlockSpec(memory_space=pltpu.VMEM)


def ring_buffers(cols):
    return [
        pltpu.VMEM((2, 2, 80, cols), LOW),
        pltpu.VMEM((2, 4, 80, cols), LOW),
        pltpu.VMEM((4, 80, cols), LOW),
        pltpu.VMEM((80, cols), LOW),
        pltpu.VMEM((2, 80, cols), LOW),
    ]


def shards(
    tokens, segments, cotangent, w_query, w_keyval, w_out, w_gateup, w_down, norm_gains, head_gains
):
    output, input_grad, done, ends = pl.pallas_call(
        layer_kernel,
        out_shape=(
            jax.ShapeDtypeStruct((ROWS, D), LOW),
            jax.ShapeDtypeStruct((ROWS, D), F32),
            jax.ShapeDtypeStruct((80, WIRE + 128), F32),
            jax.ShapeDtypeStruct((16, 128), F32),
        ),
        in_specs=[anywhere(), vmem(), anywhere()] + [vmem()] * 7,
        out_specs=(anywhere(),) * 3 + (vmem(),),
        scratch_shapes=[
            *(pltpu.VMEM(*shape) for shape in SCRATCH.values()),
            *ring_buffers(SET_COLS[0]),
            *ring_buffers(SET_COLS[1]),
            pltpu.SemaphoreType.DMA((64,)),
            pltpu.SemaphoreType.DMA((64,)),
            pltpu.SemaphoreType.DMA((128,)),
            pltpu.SemaphoreType.DMA((128,)),
            pltpu.SemaphoreType.DMA((40,)),
            pltpu.SemaphoreType.DMA((40,)),
            pltpu.VMEM((ROWS, D), LOW),
            pltpu.VMEM((ROWS, D), LOW),
            pltpu.VMEM((ROWS, D), LOW),
            pltpu.VMEM((ROWS, D), F32),
            pltpu.VMEM((80, WIRE + 128), F32),
            pltpu.SemaphoreType.DMA((16,)),
        ],
        compiler_params=pltpu.CompilerParams(
            collective_id=0, has_side_effects=True, vmem_limit_bytes=VMEM_BYTES
        ),
    )(
        tokens[0],
        segments,
        cotangent[0],
        w_query,
        w_keyval,
        w_out.T,
        w_gateup,
        w_down.T,
        norm_gains,
        head_gains,
    )
    results = pl.pallas_call(
        hand_out,
        out_shape=(
            jax.ShapeDtypeStruct((ROWS, D), LOW),
            jax.ShapeDtypeStruct((ROWS, D), F32),
            jax.ShapeDtypeStruct((40, 512), F32),
            jax.ShapeDtypeStruct((40, 512), F32),
            jax.ShapeDtypeStruct((40, 512), F32),
            jax.ShapeDtypeStruct((2, 40, FFH), F32),
            jax.ShapeDtypeStruct((40, FFH), F32),
            jax.ShapeDtypeStruct((4, 40), F32),
            jax.ShapeDtypeStruct((2, 16), F32),
        ),
        in_specs=[vmem()] * 4,
        out_specs=(vmem(),) * 9,
        compiler_params=pltpu.CompilerParams(vmem_limit_bytes=VMEM_BYTES),
    )(output, input_grad, done, ends)
    return (
        results[0][None],
        results[1][None],
        results[2],
        results[3],
        results[4].T,
        results[5],
        results[6].T,
        results[7],
        results[8],
    )


def solution(mesh):
    placed = (
        P("dp", "ctx", None),
        P("dp", "ctx"),
        P("dp", "ctx", None),
        P("dp", "tensor"),
        P("dp", None),
        P("tensor", "dp"),
        P(None, "dp", "tensor"),
        P("tensor", "dp"),
        P(None, "dp"),
        P(None, "dp"),
    )
    return jax.shard_map(
        shards,
        mesh=mesh,
        in_specs=placed,
        out_specs=(
            P("dp", "ctx", None),
            P("dp", "ctx", None),
            P("dp", "tensor"),
            P("dp", None),
            P("tensor", "dp"),
            P(None, "dp", "tensor"),
            P("tensor", "dp"),
            P(None, "dp"),
            P(None, "dp"),
        ),
        check_vma=False,
    )
```

```python
import math
import types

import jax
import jax.numpy as jnp
from jax import lax
from jax.experimental import pallas as pl
from jax.experimental.pallas import tpu as pltpu
from jax.sharding import PartitionSpec as P

WINDOW = 512
EPSILON = 1e-06
MESH = pl.DeviceIdType.MESH
VMEM_BYTES = 60 * 1024 * 1024

KV, QUERY, OUT, GATEUP, DOWN, WIRE = 0, 128, 384, 640, 1664, 2176
GATHERS = (
    ((0, 128), (128, 128)),
    ((256, 128), (384, 256)),
    ((640, 512), (1152, 512)),
    ((1664, 256), (1920, 256)),
)
SCATTERS = (
    ("s3", (1664, 256), (1920, 256)),
    ("sa", (640, 256), (896, 256)),
    ("sb", (1152, 256), (1408, 256)),
    ("s1", (384, 128), (512, 128)),
    ("sq", (128, 128), (256, 128)),
    ("sk", (0, 128), None),
)
SET_COLS = (1152, 1024)
CUT = 48
ROWS, D, HD, FFH = 512, 640, 256, 1024
SCALE = 1.0 / math.sqrt(HD)
LOW = jnp.bfloat16
F32 = jnp.float32
NN, NT, TN = ((1,), (0,)), ((1,), (1,)), ((0,), (0,))


def place(u):
    return lax.rem(u + 8, 4)


class Wires:
    def __init__(self, send, recv):
        self.send, self.recv, self.used = send, recv, 0
        self.started = []

    def copy(self, src, dst, target):
        index = self.used
        self.used += 1
        made = pltpu.make_async_remote_copy(
            src_ref=src,
            dst_ref=dst,
            send_sem=self.send.at[index],
            recv_sem=self.recv.at[index],
            device_id=target,
            device_id_type=MESH,
        )
        made.start()
        self.started.append(made)
        return made

    def drain(self):
        for made in self.started:
            made.wait_send()
        self.started = []


class Ring:
    def __init__(self, first, x, y):
        self.first = first
        self.f, self.s = (x, y) if first == "x" else (y, x)

    def slot(self, ref, f, s, *rest):
        return ref.at[(s, f) + rest] if self.first == "x" else ref.at[(f, s) + rest]

    def index(self, f, s):
        return (s, f) if self.first == "x" else (f, s)

    def to_f(self, step):
        f = place(self.f + step)
        return {"dp": self.s * 4 + f} if self.first == "x" else {"dp": f * 4 + self.s}

    def to_s(self, step):
        s = place(self.s + step)
        return {"dp": s * 4 + self.f} if self.first == "x" else {"dp": self.f * 4 + s}


class Gather:
    def __init__(self, ring, wires, shard, whole, direct, start, width):
        self.ring, self.wires, self.shard, self.whole = ring, wires, shard, whole
        self.direct = direct
        self.cols = pl.ds(start, width)

    def one(self):
        r, c = self.ring, self.cols
        src = self.shard.at[:, c]
        dst = r.slot(self.whole, r.f, r.s, slice(None), c)
        self.a = self.wires.copy(src, dst, r.to_f(1))
        self.b = self.wires.copy(src, dst, r.to_f(-1))
        if self.direct:
            self.c = self.wires.copy(src, dst, r.to_f(2))

    def two(self):
        r, c = self.ring, self.cols
        self.a.wait_recv()
        part = r.slot(self.whole, place(r.f - 1), r.s, pl.ds(0, CUT), c)
        a = self.wires.copy(part, part, r.to_f(1))
        self.b.wait_recv()
        part = r.slot(self.whole, place(r.f + 1), r.s, pl.ds(CUT, 80 - CUT), c)
        b = self.wires.copy(part, part, r.to_f(-1))
        self.a, self.b = a, b

    def three(self):
        r, c = self.ring, self.cols
        self.a.wait_recv()
        self.b.wait_recv()
        if self.direct:
            self.c.wait_recv()
        part = r.slot(self.whole, slice(None), r.s, slice(None), c)
        self.a = self.wires.copy(part, part, r.to_s(1))
        self.b = self.wires.copy(part, part, r.to_s(-1))

    def four(self):
        r, c = self.ring, self.cols
        self.a.wait_recv()
        part = r.slot(self.whole, pl.ds(0, 2), place(r.s - 1), slice(None), c)
        a = self.wires.copy(part, part, r.to_s(1))
        self.b.wait_recv()
        part = r.slot(self.whole, pl.ds(2, 2), place(r.s + 1), slice(None), c)
        b = self.wires.copy(part, part, r.to_s(-1))
        self.a, self.b = a, b

    def finish(self):
        self.a.wait_recv()
        self.b.wait_recv()


def added(*terms):
    total = terms[0].astype(jnp.float32)
    for term in terms[1:]:
        total = total + term.astype(jnp.float32)
    return total


class Scatter:
    def __init__(self, ring, wires, grads, bufs, final, z, start, width, offset, far):
        self.ring, self.wires, self.grads, self.final, self.z = ring, wires, grads, final, z
        self.r1, self.r2, self.sums, self.r3, self.r4 = bufs
        self.cols = pl.ds(start, width)
        self.near = pl.ds(offset, width)
        self.far, self.start = far, start

    def one(self):
        r, c, n = self.ring, self.cols, self.near
        far = place(r.s + 2)
        self.a = self.wires.copy(
            r.slot(self.grads, pl.ds(0, 2), far, slice(None), c), self.r1.at[0, :, :, n], r.to_s(1)
        )
        self.b = self.wires.copy(
            r.slot(self.grads, pl.ds(2, 2), far, slice(None), c), self.r1.at[1, :, :, n], r.to_s(-1)
        )

    def two(self):
        r, c, n = self.ring, self.cols, self.near
        after, before = place(r.s + 1), place(r.s - 1)
        self.a.wait_recv()
        for i in range(2):
            at = r.index(i, after) + (slice(None), c)
            self.grads[at] = added(self.grads[at], self.r1[0, i, :, n]).astype(jnp.bfloat16)
        a = self.wires.copy(
            r.slot(self.grads, slice(None), after, slice(None), c), self.r2.at[0, :, :, n], r.to_s(1)
        )
        self.b.wait_recv()
        for i in range(2):
            at = r.index(2 + i, before) + (slice(None), c)
            self.grads[at] = added(self.grads[at], self.r1[1, i, :, n]).astype(jnp.bfloat16)
        b = self.wires.copy(
            r.slot(self.grads, slice(None), before, slice(None), c),
            self.r2.at[1, :, :, n],
            r.to_s(-1),
        )
        self.a, self.b = a, b

    def three(self):
        r, c, n = self.ring, self.cols, self.near
        self.a.wait_recv()
        self.b.wait_recv()
        for i in range(4):
            at = r.index(i, r.s) + (slice(None), c)
            self.sums[i, :, n] = added(
                self.grads[at], self.r2[0, i, :, n], self.r2[1, i, :, n]
            ).astype(jnp.bfloat16)
        far = place(r.f + 2)
        self.a = self.wires.copy(
            self.sums.at[far, pl.ds(0, CUT), n], self.r3.at[pl.ds(0, CUT), n], r.to_f(1)
        )
        self.b = self.wires.copy(
            self.sums.at[far, pl.ds(CUT, 80 - CUT), n],
            self.r3.at[pl.ds(CUT, 80 - CUT), n],
            r.to_f(-1),
        )

    def four(self):
        r, n = self.ring, self.near
        after, before = place(r.f + 1), place(r.f - 1)
        top, low = pl.ds(0, CUT), pl.ds(CUT, 80 - CUT)
        self.a.wait_recv()
        self.sums[after, top, n] = added(self.sums[after, top, n], self.r3[top, n]).astype(
            jnp.bfloat16
        )
        a = self.wires.copy(self.sums.at[after, :, n], self.r4.at[0, :, n], r.to_f(1))
        self.b.wait_recv()
        self.sums[before, low, n] = added(self.sums[before, low, n], self.r3[low, n]).astype(
            jnp.bfloat16
        )
        b = self.wires.copy(self.sums.at[before, :, n], self.r4.at[1, :, n], r.to_f(-1))
        self.a, self.b = a, b

    def five(self):
        r, c, n = self.ring, self.cols, self.near
        self.a.wait_recv()
        self.b.wait_recv()
        self.final[self.z, :, c] = added(
            self.sums[r.f, :, n], self.r4[0, :, n], self.r4[1, :, n]
        ).astype(jnp.bfloat16)
        part = self.final.at[self.z, :, c]
        self.zs = [self.wires.copy(part, part, {"ctx": place(self.z + k)}) for k in (1, 3, 2)]
        if self.far is not None:
            part = self.final.at[self.z, :, pl.ds(self.start, 128)]
            self.zs += [self.wires.copy(part, self.far[0], target) for target in self.far[1]]

    def finish(self):
        for made in self.zs:
            made.wait_recv()


def spot():
    d = lax.axis_index("dp")
    return lax.rem(d, 4), lax.div(d, 4), lax.axis_index("ctx")


def dot(a, b, dims=NN):
    return lax.dot_general(a, b, (dims, ((), ())), preferred_element_type=F32)


def rms(field):
    return lax.rsqrt(jnp.mean(field * field, axis=-1, keepdims=True) + EPSILON)


def norm_back(field, gain, grad):
    r = rms(field)
    hat = field * r
    scaled = grad * gain
    back = r * (scaled - hat * jnp.mean(scaled * hat, axis=-1, keepdims=True))
    return back, jnp.sum(grad * hat, axis=0, keepdims=True)


def turn(field, cos, sin):
    a, b = field[:, :128], field[:, 128:]
    return jnp.concatenate([a * cos - b * sin, b * cos + a * sin], axis=1)


def turn_back(field, cos, sin):
    a, b = field[:, :128], field[:, 128:]
    return jnp.concatenate([a * cos + b * sin, b * cos - a * sin], axis=1)


def fold(block):
    half = block.shape[-1] // 2
    return jnp.concatenate([block[..., :half], block[..., half:]], axis=-2)


def unfold(block):
    rows = block.shape[-2] // 2
    return jnp.concatenate([block[..., :rows, :], block[..., rows:, :]], axis=-1)


def iota(shape, axis):
    return lax.broadcasted_iota(jnp.int32, shape, axis)


SCRATCH = dict(
    wire=((80, WIRE), LOW),
    whole=((4, 4, 80, WIRE), LOW),
    tile=((16, 128), F32),
    tile_low=((16, 128), LOW),
    tiles=((4, 4, 16, 128), LOW),
    wq=((D, 512), LOW),
    wkv=((D, HD), LOW),
    wo=((D, 512), LOW),
    wg=((D, FFH), LOW),
    wu=((D, FFH), LOW),
    wd=((D, FFH), LOW),
    gains=((8, D), F32),
    heads=((8, HD), F32),
    dgains=((8, D), F32),
    ends=((16, 16, 128), F32),
    end_snd=((4, 4, 16, 128), LOW),
    end_rcv=((4, 4, 16, 128), LOW),
    end_mid=((4, 16, 128), LOW),
    end_mrc=((4, 16, 128), LOW),
    end_z=((4, 16, 128), LOW),
    end_far=((4, 16, 128), LOW),
    dheads=((8, HD), F32),
    tokh=((ROWS, D), LOW),
    segp=((1, ROWS), jnp.int32),
    lo_col=((ROWS, 128), F32),
    lo_row=((8, ROWS), F32),
    cos=((1024, 128), F32),
    sin=((1024, 128), F32),
    n1=((1024, D), LOW),
    n1t=((D, 1024), LOW),
    kvb=((2, 1024, HD), LOW),
    kvraw=((1024, HD), F32),
    qraw=((4, 256, HD), F32),
    q=((4, 256, HD), LOW),
    o=((ROWS, 512), LOW),
    go=((4, 256, HD), LOW),
    gqr=((ROWS, 512), LOW),
    a=((ROWS, D), F32),
    h=((ROWS, D), F32),
    n2=((ROWS, D), LOW),
    n2t=((D, ROWS), LOW),
    ga=((ROWS, FFH), F32),
    gb=((ROWS, FFH), F32),
    u=((ROWS, FFH), LOW),
    ggu=((ROWS, 2 * FFH), LOW),
    gf=((ROWS, D), LOW),
    gft=((D, ROWS), LOW),
    gal=((ROWS, D), LOW),
    gat=((D, ROWS), LOW),
    gh=((ROWS, D), F32),
    snd=((2, ROWS, D), LOW),
    rcv=((2, ROWS, D), LOW),
    gkv=((2, 1024, HD), F32),
    kvs=((1024, HD), LOW),
    kvr=((1024, HD), LOW),
    hs=((ROWS, HD), LOW),
    hr=((ROWS, HD), LOW),
    gkr=((1024, HD), LOW),
    gko=((ROWS, HD), LOW),
    final=((4, 80, WIRE), LOW),
    far=((4, 80, 128), LOW),
)


ORDER = (
    "w0", "p0.one", "w1", "w2", "p2.one", "tab", "p1.one", "mask", "p0.three", "w3", "ge.one",
    "p3.one", "p2.two", "p1.three", "ge.two", "p0.four", "p3.two", "p2.three", "p1.four", "c0",
    "p3.three", "c1", "p2.four", "c2", "A0", "A1", "A2", "c3", "A3", "c4", "p3.four", "h0",
    "h1", "c6", "F0", "c8", "F1", "c9", "o0", "FB0", "G0", "o1", "P3", "s3.one", "FB1", "PA",
    "sa.one", "N0", "PB", "sb.one", "G1", "s3.two", "B0", "sa.two", "B1", "sb.two", "N1", "B2",
    "B3", "s3.three", "PQ", "sq.one", "V0", "P1", "s1.one", "sa.three", "V1", "QS", "KB",
    "sk.one", "sb.three", "s3.four", "sq.two", "s1.two", "sa.four", "sb.four", "NN0", "s3.five",
    "NN1", "sq.three", "I0", "sk.two", "s1.three", "sa.five", "I1", "sq.four", "EX", "se.one",
    "sb.five", "sk.three", "s1.four", "s3.fin", "sq.five", "se.two", "sa.fin", "sk.four",
    "s1.five", "se.five", "sb.fin", "sk.five", "sq.fin", "s1.fin", "se.fin", "sk.fin",
)


def layer_kernel(
    tok_hbm, seg_row, cot_hbm, wq, wkv, wo, wgu, wd, ng, hg, out_hbm, igrad_hbm, grads_hbm, ends, *rest
):
    names = list(SCRATCH)
    g = types.SimpleNamespace(**dict(zip(names, rest[: len(names)])))
    rest = rest[len(names) :]
    bufs = (rest[0:5], rest[5:10])
    tok, cot, out, igrad, grads, local = rest[16:22]
    tok_read = pltpu.make_async_copy(tok_hbm, tok, local.at[0])
    cot_read = pltpu.make_async_copy(cot_hbm, cot, local.at[1])
    tok_read.start()
    cot_read.start()
    writes = []

    def write(source, target):
        made = pltpu.make_async_copy(source, target, local.at[2 + len(writes)])
        made.start()
        writes.append(made)

    x, y, z = spot()
    core = lax.axis_index("tensor")
    mate = {"tensor": 1 - core}
    rings = (Ring("x", x, y), Ring("y", x, y))
    gather_wires = Wires(rest[10], rest[11])
    scatter_wires = Wires(rest[12], rest[13])
    other = Wires(rest[14], rest[15])
    along_z = [{"ctx": place(z + k)} for k in (1, 3, 2)]
    across = [{"ctx": place(z + k), "tensor": 1 - core} for k in range(4)]
    targets = [r.to_f(k) for r in rings for k in (1, -1, 2)] + along_z + across
    barrier = pltpu.get_barrier_semaphore()
    for target in targets:
        pl.semaphore_signal(barrier, inc=1, device_id=target, device_id_type=MESH)

    jobs, held = {}, {}

    def job(name):
        def keep(work):
            jobs[name] = work
            return work

        return keep

    def steps(name, members, methods):
        for method in methods:
            jobs[name + "." + method] = lambda method=method: [getattr(m, method)() for m in members]

    for number, piece in enumerate(GATHERS):
        made = [
            Gather(ring, gather_wires, g.wire, g.whole, number < 2, *piece[i])
            for i, ring in enumerate(rings)
        ]
        steps("p%d" % number, made, ("one", "two", "three", "four", "finish"))
        if number == 1:
            p1 = made
    offsets = [0, 0]
    for name, *piece in SCATTERS:
        made = []
        for i, ring in enumerate(rings):
            if piece[i] is None:
                continue
            start, width = piece[i]
            far = (g.far.at[z], across) if start == KV else None
            made.append(
                Scatter(ring, scatter_wires, g.whole, bufs[i], g.final, z, start, width, offsets[i], far)
            )
            offsets[i] += width
        steps(name, made, ("one", "two", "three", "four", "five", "finish"))

    halves = [slice(0, 256), slice(256, 512)]

    def swap(name, number, rows, value):
        g.snd[number, rows] = value.astype(LOW)
        held[name] = other.copy(g.snd.at[number, rows], g.rcv.at[number, rows], mate)

    def total(name, number, rows):
        held[name].wait_recv()
        held[name].wait_send()
        return g.snd[number, rows].astype(F32) + g.rcv[number, rows].astype(F32)

    @job("w0")
    def _():
        mine = wkv[:, pl.ds(pl.multiple_of(core * HD, HD), HD)]
        g.wire[:, KV:QUERY] = fold(mine.astype(F32)).astype(LOW)
        g.wire[:, QUERY:OUT] = fold(wq[...].astype(F32)).astype(LOW)
        g.whole[y, x, :, KV:OUT] = g.wire[:, KV:OUT]
        g.tile[...] = jnp.zeros((16, 128), F32)
        g.tile[0:4, 0:40] = ng[...].astype(F32)
        g.tile[8:10, 0:16] = hg[...].astype(F32)
        g.tile_low[...] = g.tile[...].astype(LOW)
        pl.semaphore_wait(barrier, len(targets))

    @job("ge.one")
    def _():
        held["ge"] = [
            other.copy(g.tile_low, g.tiles.at[y, x], {"dp": y * 4 + place(x + k)}) for k in (1, 3, 2)
        ]

    @job("ge.two")
    def _():
        for made in held["ge"]:
            made.wait_recv()
        g.tiles[y, x] = g.tile_low[...]
        held["ge"] = [
            other.copy(g.tiles.at[y], g.tiles.at[y], {"dp": place(y + k) * 4 + x}) for k in (1, 3, 2)
        ]

    @job("w1")
    def _():
        held["seg"] = other.copy(seg_row, g.segp, {"ctx": place(z + 1)})
        tok_read.wait()
        held["tok"] = other.copy(tok, g.tokh, {"ctx": place(z + 1)})
        g.wire[:, OUT:GATEUP] = fold(wo[...].astype(F32)).astype(LOW)
        g.whole[y, x, :, OUT:GATEUP] = g.wire[:, OUT:GATEUP]

    @job("w2")
    def _():
        both = jnp.concatenate([wgu[0].astype(F32), wgu[1].astype(F32)], axis=0)
        g.wire[:, GATEUP:DOWN] = both.astype(LOW)
        g.whole[y, x, :, GATEUP:DOWN] = g.wire[:, GATEUP:DOWN]

    @job("w3")
    def _():
        g.wire[:, DOWN:WIRE] = fold(wd[...].astype(F32)).astype(LOW)
        g.whole[y, x, :, DOWN:WIRE] = g.wire[:, DOWN:WIRE]

    @job("tab")
    def _():
        rates = jnp.exp(iota((1, 128), 1).astype(F32) * (-2.0 * math.log(10000.0) / HD))
        fine = iota((128, 128), 0).astype(F32) * rates
        fine_cos, fine_sin = jnp.cos(fine), jnp.sin(fine)
        coarse = (iota((8, 128), 0) * 128 + (z * ROWS - ROWS)).astype(F32) * rates
        coarse_cos, coarse_sin = jnp.cos(coarse), jnp.sin(coarse)
        for i in range(8):
            cc, cs = coarse_cos[i : i + 1], coarse_sin[i : i + 1]
            g.cos[128 * i : 128 * i + 128] = fine_cos * cc - fine_sin * cs
            g.sin[128 * i : 128 * i + 128] = fine_sin * cc + fine_cos * cs
        g.dgains[...] = jnp.zeros((8, D), F32)
        g.dheads[...] = jnp.zeros((8, HD), F32)
        g.gkv[...] = jnp.zeros((2, 1024, HD), F32)
        g.ends[...] = jnp.zeros((16, 16, 128), F32)

    @job("mask")
    def _():
        held["seg"].wait_recv()
        own_ids, prior_ids = seg_row[...].astype(F32), g.segp[...].astype(F32)
        column = jnp.transpose(jnp.broadcast_to(own_ids, (128, ROWS)))[:, 0:1]
        below_prior = jnp.sum((prior_ids < column).astype(F32), axis=1, keepdims=True)
        below_prior = jnp.where(z == 0, float(ROWS), below_prior)
        below_own = jnp.sum((own_ids < column).astype(F32), axis=1, keepdims=True)
        lowest = jnp.maximum(below_prior + below_own, iota((ROWS, 1), 0).astype(F32) + 1.0)
        lowest = jnp.broadcast_to(lowest, (ROWS, 128))
        g.lo_col[...] = lowest
        g.lo_row[...] = jnp.transpose(lowest)[0:8]

    def assemble(first, second, start, width, w=128):
        def one(i):
            at = i * w
            block = g.whole[:, :, :, pl.ds(start + at, w)].astype(F32)
            first[:, pl.ds(at, w)] = block[:, :, :40].reshape(D, w).astype(LOW)
            if second is None:
                first[:, pl.ds(at + width, w)] = block[:, :, 40:].reshape(D, w).astype(LOW)
            else:
                second[:, pl.ds(at, w)] = block[:, :, 40:].reshape(D, w).astype(LOW)

        for i in range(width // w):
            one(i)

    def gain(i):
        return g.gains[i : i + 1]

    def keys_of(start, normed):
        at = slice(start, start + 256)
        low = normed.astype(LOW)
        g.n1[at] = low
        raw = dot(low, g.wkv[...])
        g.kvraw[at] = raw
        turned = turn(raw * rms(raw) * g.heads[1:2], g.cos[at], g.sin[at])
        g.kvb[core, at] = jnp.where(core == 0, turned, raw).astype(LOW)
        g.n1t[:, at] = jnp.transpose(normed).astype(LOW)

    @job("c0")
    def _():
        jobs["p0.finish"]()
        for made in held["ge"]:
            made.wait_recv()
        for d in range(16):
            block = g.tiles[d // 4, d % 4].astype(F32)
            g.gains[:, 40 * d : 40 * d + 40] = block[0:8, 0:40]
            g.heads[:, 16 * d : 16 * d + 16] = block[8:16, 0:16]
        assemble(g.wkv, None, KV, 128)
        for rows in halves:
            block = tok[rows].astype(F32)
            keys_of(ROWS + rows.start, block * rms(block) * gain(0))
        part = g.kvb.at[core, pl.ds(ROWS, ROWS)]
        held["kv1"] = other.copy(part, part, mate)

    @job("c1")
    def _():
        held["tok"].wait_recv()
        for rows in halves:
            block = g.tokh[rows].astype(F32)
            keys_of(rows.start, block * rms(block) * gain(0))
        part = g.kvb.at[core, pl.ds(0, ROWS)]
        held["kv2"] = other.copy(part, part, mate)

    @job("c2")
    def _():
        p1[0].finish()
        assemble(g.wq, None, QUERY, 256)
        for i in range(2):
            at = slice(ROWS + 256 * i, ROWS + 256 * i + 256)
            raw = dot(g.n1[at], g.wq[...])
            for h in range(2):
                part = raw[:, HD * h : HD * h + HD]
                turned = turn(part * rms(part) * g.heads[0:1], g.cos[at], g.sin[at]).astype(LOW)
                for j in range(2):
                    g.qraw[2 * i + j, 128 * h : 128 * h + 128] = part[128 * j : 128 * j + 128]
                    g.q[2 * i + j, 128 * h : 128 * h + 128] = turned[128 * j : 128 * j + 128]

    def twice(block, axis):
        return jnp.concatenate([block, block], axis=axis)

    def attend(b):
        start = b * 128
        keys, values = g.kvb[0, pl.ds(start, D)], g.kvb[1, pl.ds(start, D)]
        scores = dot(g.q[b], keys, NT) * SCALE
        lowest = twice(g.lo_col[pl.ds(start, 128), 0:1], 0) - float(b * 128)
        place_k = iota((256, D), 1).astype(F32)
        highest = (iota((256, 1), 0) & 127).astype(F32) + float(WINDOW)
        scores = jnp.where((place_k >= lowest) & (place_k <= highest), scores, -1e30)
        expo = jnp.exp(scores - jnp.max(scores, axis=-1, keepdims=True))
        probs = (expo / jnp.sum(expo, axis=-1, keepdims=True)).astype(LOW)
        mixed = dot(probs, values).astype(LOW)
        g.o[pl.ds(start, 128), 0:HD] = mixed[:128]
        g.o[pl.ds(start, 128), HD : 2 * HD] = mixed[128:]

    @job("A0")
    def _():
        held["kv1"].wait_recv()
        held["kv2"].wait_recv()
        attend(0)

    for b in (1, 2, 3):
        jobs["A%d" % b] = lambda b=b: attend(b)

    @job("c3")
    def _():
        p1[1].finish()
        assemble(g.wo, None, OUT, 256)
        swap("a0", 0, halves[0], dot(g.o[halves[0]], g.wo[...], NT))

    @job("c4")
    def _():
        swap("a1", 0, halves[1], dot(g.o[halves[1]], g.wo[...], NT))

    def hidden_rows(i):
        rows = halves[i]
        branch = total("a%d" % i, 0, rows)
        g.a[rows] = branch
        hidden = tok[rows].astype(F32) + branch * rms(branch) * gain(1)
        g.h[rows] = hidden
        normed = hidden * rms(hidden) * gain(2)
        g.n2[rows] = normed.astype(LOW)
        g.n2t[:, rows] = jnp.transpose(normed).astype(LOW)

    c0, c1 = math.sqrt(2.0 / math.pi), 0.044715

    def forward_rows(k):
        rows = halves[k]

        def one(i):
            cols = pl.ds(i * 256, 256)
            gate = dot(g.n2[rows], g.wg[:, cols])
            up = dot(g.n2[rows], g.wu[:, cols])
            square = gate * gate
            t = jnp.tanh(c0 * gate * (1.0 + c1 * square))
            act = 0.5 * gate * (1.0 + t)
            slope = 0.5 * (1.0 + t) + 0.5 * gate * (1.0 - t * t) * (c0 * (1.0 + 3.0 * c1 * square))
            g.ga[rows, cols] = act
            g.gb[rows, cols] = up * slope
            g.u[rows, cols] = (act * up).astype(LOW)

        for i in range(4):
            one(i)

    @job("c6")
    def _():
        jobs["p2.finish"]()
        assemble(g.wg, g.wu, GATEUP, FFH)

    @job("c8")
    def _():
        jobs["p3.finish"]()
        gather_wires.drain()
        assemble(g.wd, None, DOWN, 512)
        swap("f0", 1, halves[0], dot(g.u[halves[0]], g.wd[...], NT))

    @job("c9")
    def _():
        swap("f1", 1, halves[1], dot(g.u[halves[1]], g.wd[...], NT))

    def output_rows(i):
        rows = halves[i]
        if i == 0:
            cot_read.wait()
        feed = total("f%d" % i, 1, rows)
        out[rows] = (g.h[rows] + feed * rms(feed) * gain(3)).astype(LOW)
        back, slope = norm_back(feed, gain(3), cot[rows].astype(F32))
        g.dgains[3:4] += slope
        g.gf[rows] = back.astype(LOW)
        g.gft[:, rows] = jnp.transpose(back).astype(LOW)
        write(out.at[rows], out_hbm.at[rows])

    def put(left, right, start, begin, end, gap, w=256):
        def one(i):
            at = i * w
            first = dot(left[...], right[:, pl.ds(at, w)]).reshape(16, 40, w)
            second = dot(left[...], right[:, pl.ds(at + gap, w)]).reshape(16, 40, w)
            block = jnp.concatenate([first, second], axis=1).astype(LOW)
            g.whole[:, :, :, pl.ds(start + at, w)] = block.reshape(4, 4, 80, w)

        for i in range(begin // w, end // w):
            one(i)

    jobs["P3"] = lambda: put(g.gft, g.u, DOWN, 0, 512, 512)
    jobs["PA"] = lambda: put(g.n2t, g.ggu, GATEUP, 0, 512, FFH)
    jobs["PB"] = lambda: put(g.n2t, g.ggu, GATEUP, 512, 1024, FFH)
    jobs["P1"] = lambda: put(g.gat, g.o, OUT, 0, 256, 256)
    jobs["PQ"] = lambda: put(g.n1t.at[:, ROWS:], g.gqr, QUERY, 0, 256, 256)

    def backward_rows(k):
        rows = halves[k]

        def one(i):
            at = i * 256
            cols = pl.ds(at, 256)
            inner = dot(g.gf[rows], g.wd[:, cols])
            g.ggu[rows, cols] = (inner * g.gb[rows, cols]).astype(LOW)
            g.ggu[rows, pl.ds(at + FFH, 256)] = (inner * g.ga[rows, cols]).astype(LOW)

        for i in range(4):
            one(i)

    def second_rows(i):
        rows = halves[i]
        part = dot(g.ggu[rows, 0:FFH], g.wg[...], NT) + dot(g.ggu[rows, FFH:], g.wu[...], NT)
        swap("g%d" % i, 0, rows, part)

    def norm_rows(i):
        rows = halves[i]
        back, slope = norm_back(g.h[rows], gain(2), total("g%d" % i, 0, rows))
        g.dgains[2:3] += slope
        hidden = cot[rows].astype(F32) + back
        g.gh[rows] = hidden
        back, slope = norm_back(g.a[rows], gain(1), hidden)
        g.dgains[1:2] += slope
        g.gat[:, rows] = jnp.transpose(back).astype(LOW)
        grad = dot(back.astype(LOW), g.wo[...]).astype(LOW)
        for j in range(2):
            for h in range(2):
                g.go[2 * i + j, 128 * h : 128 * h + 128] = grad[
                    128 * j : 128 * j + 128, HD * h : HD * h + HD
                ]

    for i in range(2):
        jobs["h%d" % i] = lambda i=i: hidden_rows(i)
        jobs["F%d" % i] = lambda i=i: forward_rows(i)
        jobs["o%d" % i] = lambda i=i: output_rows(i)
        jobs["FB%d" % i] = lambda i=i: backward_rows(i)
        jobs["G%d" % i] = lambda i=i: second_rows(i)
        jobs["N%d" % i] = lambda i=i: norm_rows(i)

    def attend_back(b):
        start = b * 128
        keys, values = g.kvb[0, pl.ds(start, D)], g.kvb[1, pl.ds(start, D)]
        queries, grad = g.q[b], g.go[b]
        scores = dot(keys, queries, NT) * SCALE
        lowest = twice(g.lo_row[0:1, pl.ds(start, 128)], 1) - float(b * 128)
        place_k = iota((D, 256), 0).astype(F32)
        highest = (iota((1, 256), 1) & 127).astype(F32) + float(WINDOW)
        scores = jnp.where((place_k >= lowest) & (place_k <= highest), scores, -1e30)
        expo = jnp.exp(scores - jnp.max(scores, axis=0, keepdims=True))
        probs = expo * (1.0 / jnp.sum(expo, axis=0, keepdims=True))
        grad_probs = dot(values, grad, NT)
        spread = jnp.sum(probs * grad_probs, axis=0, keepdims=True)
        grad_scores = (probs * (grad_probs - spread)).astype(LOW)
        g.gkv[0, pl.ds(start, D)] += dot(grad_scores, queries) * SCALE
        g.gkv[1, pl.ds(start, D)] += dot(probs.astype(LOW), grad)
        grad_q = dot(grad_scores, keys, TN) * SCALE
        at = pl.ds(ROWS + start, 128)
        grad_q = turn_back(grad_q, twice(g.cos[at], 0), twice(g.sin[at], 0))
        back, slope = norm_back(g.qraw[b], g.heads[0:1], grad_q)
        g.dheads[0:1] += slope
        g.gqr[pl.ds(start, 128), 0:HD] = back[:128].astype(LOW)
        g.gqr[pl.ds(start, 128), HD : 2 * HD] = back[128:].astype(LOW)

    def back_block(b):
        attend_back(b)
        if b in (1, 3):
            rows = pl.ds(0, 256) if b == 1 else pl.ds(256, 768)
            g.kvs[rows] = g.gkv[1 - core, rows].astype(LOW)
            held["kvx%d" % (b // 2)] = other.copy(g.kvs.at[rows], g.kvr.at[rows], mate)

    for b in range(4):
        jobs["B%d" % b] = lambda b=b: back_block(b)

    def summed_rows(i):
        rows = slice(0, 256) if i == 0 else slice(256, 1024)
        held["kvx%d" % i].wait_recv()
        g.gkv[core, rows] = added(g.gkv[core, rows], g.kvr[rows])
        g.hs[halves[i]] = g.gkv[core, halves[i]].astype(LOW)
        held["ha%d" % i] = other.copy(
            g.hs.at[halves[i]], g.hr.at[halves[i]], {"ctx": place(z - 1)}
        )

    def keys_back(start, grad):
        at = slice(start, start + 256)
        turned = turn_back(grad, g.cos[at], g.sin[at])
        back, slope = norm_back(g.kvraw[at], g.heads[1:2], turned)
        return jnp.where(core == 0, back, grad).astype(LOW), jnp.where(core == 0, slope, 0.0)

    @job("KB")
    def _():
        for start in range(0, 1024, 256):
            low, slope = keys_back(start, g.gkv[core, start : start + 256])
            g.dheads[1:2] += slope
            g.gkr[start : start + 256] = low
        put(g.n1t, g.gkr, KV, 0, 128, 128, w=128)

    @job("QS")
    def _():
        for rows in halves:
            g.a[rows] = dot(g.gqr[rows], g.wq[...], NT)

    def first_rows(i):
        rows = halves[i]
        held["ha%d" % i].wait_recv()
        start = ROWS + rows.start
        grad = added(g.gkv[core, start : start + 256], g.hr[rows])
        low, _ = keys_back(start, grad)
        swap("n%d" % i, 1, rows, g.a[rows] + dot(low, g.wkv[...], NT))

    def input_rows(i):
        rows = halves[i]
        back, slope = norm_back(tok[rows].astype(F32), gain(0), total("n%d" % i, 1, rows))
        g.dgains[0:1] += slope
        igrad[rows] = g.gh[rows] + back
        write(igrad.at[rows], igrad_hbm.at[rows])

    for i in range(2):
        jobs["V%d" % i] = lambda i=i: summed_rows(i)
        jobs["NN%d" % i] = lambda i=i: first_rows(i)
        jobs["I%d" % i] = lambda i=i: input_rows(i)

    @job("EX")
    def _():
        for d in range(16):
            g.ends[d, 0:8, 0:40] = g.dgains[:, 40 * d : 40 * d + 40]
            g.ends[d, 8:16, 0:16] = g.dheads[:, 16 * d : 16 * d + 16]
        g.end_snd[...] = g.ends[...].astype(LOW).reshape(4, 4, 16, 128)

    @job("se.one")
    def _():
        held["se"] = [
            other.copy(g.end_snd.at[place(y + k)], g.end_rcv.at[y], {"dp": place(y + k) * 4 + x})
            for k in (1, 3, 2)
        ]

    @job("se.two")
    def _():
        for made in held["se"]:
            made.wait_recv()
        g.end_rcv[y] = g.end_snd[y]
        g.end_mid[...] = added(*(g.end_rcv[i] for i in range(4))).astype(LOW)
        held["se"] = [
            other.copy(g.end_mid.at[place(x + k)], g.end_mrc.at[x], {"dp": y * 4 + place(x + k)})
            for k in (1, 3, 2)
        ]

    @job("se.five")
    def _():
        for made in held["se"]:
            made.wait_recv()
        g.end_mrc[x] = g.end_mid[x]
        g.end_z[z] = added(*(g.end_mrc[i] for i in range(4))).astype(LOW)
        held["se"] = [other.copy(g.end_z.at[z], g.end_z.at[z], target) for target in along_z] + [
            other.copy(g.end_z.at[z], g.end_far.at[z], target) for target in across
        ]

    @job("se.fin")
    def _():
        for made in held["se"]:
            made.wait_recv()
        own = added(*(g.end_z[i] for i in range(4)))
        far = added(*(g.end_far[i] for i in range(4)))
        ends[0:8] = own[0:8]
        ends[8:16] = own[8:16] + far[8:16]

    def put_final(name, source, start, at, width):
        def work():
            jobs[name + ".finish"]()
            cols = pl.ds(start, width)
            grads[:, at : at + width] = added(*(source[i, :, cols] for i in range(4)))
            write(grads.at[:, pl.ds(at, width)], grads_hbm.at[:, pl.ds(at, width)])

        jobs[name + ".fin"] = work

    put_final("s3", g.final, DOWN, DOWN, 512)
    put_final("sa", g.final, GATEUP, GATEUP, 512)
    put_final("sb", g.final, GATEUP + 512, GATEUP + 512, 512)
    put_final("s1", g.final, OUT, OUT, 256)

    put_final("sq", g.final, QUERY, QUERY, 256)

    @job("sk.fin")
    def _():
        jobs["sk.finish"]()
        own = added(*(g.final[i, :, KV:QUERY] for i in range(4)))
        far = added(*(g.far[i] for i in range(4)))
        grads[:, 0:128] = jnp.where(core == 0, own, far)
        grads[:, WIRE : WIRE + 128] = jnp.where(core == 0, far, own)
        for cols in (pl.ds(0, 128), pl.ds(WIRE, 128)):
            write(grads.at[:, cols], grads_hbm.at[:, cols])

    for name in ORDER:
        jobs[name]()
    scatter_wires.drain()
    waited = [held[n + str(i)] for n in "afgn" for i in (0, 1)]
    for made in other.started:
        if not any(made is one for one in waited):
            made.wait_send()
    for made in writes:
        made.wait()


def hand_out(output, input_grad, done, ends, out, igrad, query, keyval, wide, gateup, down, norms, heads):
    out[...] = output[...]
    igrad[...] = input_grad[...]
    keyval[:, 0:256] = unfold(done[:, KV:QUERY])
    keyval[:, 256:512] = unfold(done[:, WIRE : WIRE + 128])
    query[...] = unfold(done[:, QUERY:OUT])
    wide[...] = unfold(done[:, OUT:GATEUP])
    gateup[0] = done[:40, GATEUP:DOWN]
    gateup[1] = done[40:, GATEUP:DOWN]
    down[...] = unfold(done[:, DOWN:WIRE])
    norms[...] = ends[0:4, 0:40]
    heads[...] = ends[8:10, 0:16]


def anywhere():
    return pl.BlockSpec(memory_space=pl.ANY)


def vmem():
    return pl.BlockSpec(memory_space=pltpu.VMEM)


def ring_buffers(cols):
    return [
        pltpu.VMEM((2, 2, 80, cols), LOW),
        pltpu.VMEM((2, 4, 80, cols), LOW),
        pltpu.VMEM((4, 80, cols), LOW),
        pltpu.VMEM((80, cols), LOW),
        pltpu.VMEM((2, 80, cols), LOW),
    ]


def shards(
    tokens, segments, cotangent, w_query, w_keyval, w_out, w_gateup, w_down, norm_gains, head_gains
):
    output, input_grad, done, ends = pl.pallas_call(
        layer_kernel,
        out_shape=(
            jax.ShapeDtypeStruct((ROWS, D), LOW),
            jax.ShapeDtypeStruct((ROWS, D), F32),
            jax.ShapeDtypeStruct((80, WIRE + 128), F32),
            jax.ShapeDtypeStruct((16, 128), F32),
        ),
        in_specs=[anywhere(), vmem(), anywhere()] + [vmem()] * 7,
        out_specs=(anywhere(),) * 3 + (vmem(),),
        scratch_shapes=[
            *(pltpu.VMEM(*shape) for shape in SCRATCH.values()),
            *ring_buffers(SET_COLS[0]),
            *ring_buffers(SET_COLS[1]),
            pltpu.SemaphoreType.DMA((64,)),
            pltpu.SemaphoreType.DMA((64,)),
            pltpu.SemaphoreType.DMA((128,)),
            pltpu.SemaphoreType.DMA((128,)),
            pltpu.SemaphoreType.DMA((40,)),
            pltpu.SemaphoreType.DMA((40,)),
            pltpu.VMEM((ROWS, D), LOW),
            pltpu.VMEM((ROWS, D), LOW),
            pltpu.VMEM((ROWS, D), LOW),
            pltpu.VMEM((ROWS, D), F32),
            pltpu.VMEM((80, WIRE + 128), F32),
            pltpu.SemaphoreType.DMA((16,)),
        ],
        compiler_params=pltpu.CompilerParams(
            collective_id=0, has_side_effects=True, vmem_limit_bytes=VMEM_BYTES
        ),
    )(
        tokens[0],
        segments,
        cotangent[0],
        w_query,
        w_keyval,
        w_out.T,
        w_gateup,
        w_down.T,
        norm_gains,
        head_gains,
    )
    results = pl.pallas_call(
        hand_out,
        out_shape=(
            jax.ShapeDtypeStruct((ROWS, D), LOW),
            jax.ShapeDtypeStruct((ROWS, D), F32),
            jax.ShapeDtypeStruct((40, 512), F32),
            jax.ShapeDtypeStruct((40, 512), F32),
            jax.ShapeDtypeStruct((40, 512), F32),
            jax.ShapeDtypeStruct((2, 40, FFH), F32),
            jax.ShapeDtypeStruct((40, FFH), F32),
            jax.ShapeDtypeStruct((4, 40), F32),
            jax.ShapeDtypeStruct((2, 16), F32),
        ),
        in_specs=[vmem()] * 4,
        out_specs=(vmem(),) * 9,
        compiler_params=pltpu.CompilerParams(vmem_limit_bytes=VMEM_BYTES),
    )(output, input_grad, done, ends)
    return (
        results[0][None],
        results[1][None],
        results[2],
        results[3],
        results[4].T,
        results[5],
        results[6].T,
        results[7],
        results[8],
    )


def solution(mesh):
    placed = (
        P("dp", "ctx", None),
        P("dp", "ctx"),
        P("dp", "ctx", None),
        P("dp", "tensor"),
        P("dp", None),
        P("tensor", "dp"),
        P(None, "dp", "tensor"),
        P("tensor", "dp"),
        P(None, "dp"),
        P(None, "dp"),
    )
    return jax.shard_map(
        shards,
        mesh=mesh,
        in_specs=placed,
        out_specs=(
            P("dp", "ctx", None),
            P("dp", "ctx", None),
            P("dp", "tensor"),
            P("dp", None),
            P("tensor", "dp"),
            P(None, "dp", "tensor"),
            P("tensor", "dp"),
            P(None, "dp"),
            P(None, "dp"),
        ),
        check_vma=False,
    )
```
